128 devices in a mesh: row: 8 (over y, core), col: 16 (over x, z).
Axes of the slice: x: 4, y: 4, z: 4, core: 2. Of those that a mesh axis runs over, the one named last changes fastest.
Arguments:
- features: bfloat16 [131072, 128], P(('row', 'col')), may hold values from -6 to 6
- weight: bfloat16 [128, 128], replicated, may hold values from -0.5 to 0.5
- adj_tiles: bfloat16 [12288, 128, 128], P(('row', 'col')), may hold values from -0.21875 to 0.21875
- tile_rows: int32 [12288], P(('row', 'col')), may hold values from 0 to 127
- tile_cols: int32 [12288], P(('row', 'col')), may hold values from 0 to 63
- tile_count: int32 [128], P(('row', 'col')), may hold values from 24 to 96, as said below
- cotangent: bfloat16 [131072, 128], P(('row', 'col')), may hold values from -6 to 6
Outputs:
- out_features: bfloat16 [131072, 128], P(('row', 'col'))
- weight_grad: float32 [128, 128], replicated
- feature_grad: bfloat16 [131072, 128], P(('row', 'col'))
The draws below stay inside these ranges and needn't reach their ends.
Inputs may be any that keep to these rules, and one draw needn't show every extreme that they name: Each device has 96 slots, of which the first tile_count are in use; in every draw all devices of at least one row panel use all 96 slots.
All inputs are finite; a program needn't handle non-finite values.
Results may differ from the reference program's by a relative error of at most 0.019.
Values may be sent and summed in bfloat16 or wider, within the bound.
A program may use at most 128 MiB of HBM per device.

```python
import jax
import jax.numpy as jnp
from jax import lax

F = 128
TILE = 128
NODE_DEV = 1024
TILES_DEV = 96
NODES = 131072
PANEL_TILES = 128
GROUP_TILES = 64
ALL_TILES = 12288
N_ROW = 8
N_COL = 16
DEVICES = 128


def draw_tile_count(key, part):
    first_key, second_key = jax.random.split(jax.random.fold_in(key, 71))
    hub_panels = max(1, N_ROW // 8)
    ranking = jax.random.permutation(first_key, N_ROW)
    hub_flags = (ranking < hub_panels).astype(jnp.int32)
    device_flags = jnp.repeat(hub_flags, N_COL)
    light_counts = jax.random.randint(second_key, (DEVICES,), TILES_DEV // 4, TILES_DEV // 2 + 1)
    return jnp.where(device_flags == 1, TILES_DEV, light_counts).astype(jnp.int32)


def set_ends(drawn, key, low, top_value):
    longest = drawn.shape.index(max(drawn.shape))
    spots = []
    for shift in (0, 1):
        where = [jax.random.randint(jax.random.fold_in(key, axis), (), 0, length) for axis, length in enumerate(drawn.shape)]
        where[longest] = (where[longest] + shift) % drawn.shape[longest]
        spots.append(tuple(where))
    return drawn.at[spots[0]].set(low).at[spots[1]].set(top_value)


def steps_of(rng, dims, cuts, smallest, high):
    loudness, own = 1.0, jax.random.fold_in(rng, 6)
    for axis_at, parts in cuts:
        draws = jnp.exp(jax.random.uniform(jax.random.fold_in(own, axis_at), (parts,), jnp.float32, smallest / len(cuts), high / len(cuts)))
        loudness = loudness * jnp.repeat(draws, dims[axis_at] // parts).reshape([-1 if axis == axis_at else 1 for axis in range(len(dims))])
    return loudness


def scatter_about(rng, dims, scale, bound, pieces=(), held_as=jnp.bfloat16):
    factor_of = steps_of(rng, dims, pieces, -0.22, 0.18) if pieces else 1.0
    drawn = jax.random.normal(rng, dims, jnp.float32) * scale * factor_of
    return jnp.minimum(jnp.maximum(drawn, -bound), bound).astype(held_as)


def setup_inputs(seed: int = 0) -> dict:
    splits = jax.random.split(jax.random.key(seed), 8)
    features = scatter_about(splits[0], (NODES, F), 1.0, 6.0, ((0, 128),))
    weight = scatter_about(splits[1], (F, F), F ** -0.5, 0.5)
    adj_tiles = scatter_about(splits[2], (ALL_TILES, TILE, TILE), (TILES_DEV * TILE * TILE * 9 // (20 * NODE_DEV)) ** -0.5, 0.21875, ((0, 128),))
    tile_rows = set_ends(jax.random.randint(splits[3], (ALL_TILES,), 0, PANEL_TILES), jax.random.fold_in(splits[3], 1), 0, PANEL_TILES - 1).astype(jnp.int32)
    tile_cols = set_ends(jax.random.randint(splits[4], (ALL_TILES,), 0, GROUP_TILES), jax.random.fold_in(splits[4], 1), 0, GROUP_TILES - 1).astype(jnp.int32)
    tile_count = draw_tile_count(jax.random.fold_in(splits[7], 71), 0)
    cotangent = scatter_about(splits[6], (NODES, F), 1.0, 6.0, ((0, 128),))
    return dict(features=features, weight=weight, adj_tiles=adj_tiles, tile_rows=tile_rows, tile_cols=tile_cols, tile_count=tile_count, cotangent=cotangent)


def activate(value):
    return jax.nn.gelu(value, approximate=True)

def activate_grad(pre_act, upstream):
    _, pullback = jax.vjp(activate, pre_act)
    return pullback(upstream)[0]

def reference(features, weight, adj_tiles, tile_rows, tile_cols, tile_count, cotangent):
    node_blocks = features.reshape(N_ROW, N_COL, NODE_DEV, F)
    tile_values = adj_tiles.reshape(DEVICES, TILES_DEV, TILE, TILE)
    row_table = tile_rows.reshape(DEVICES, TILES_DEV)
    col_table = tile_cols.reshape(DEVICES, TILES_DEV)
    positions = jnp.arange(TILES_DEV, dtype=jnp.int32)

    def masked(device):
        usable = (positions < tile_count[device]).astype(jnp.float32)
        return tile_values[device].astype(jnp.float32) * usable[:, None, None]

    def forward_step(summed, device):
        panel_index = device // N_COL
        group_index = device % N_COL
        group_rows = lax.dynamic_index_in_dim(node_blocks, group_index, 1, keepdims=False)
        group_rows = group_rows.reshape(GROUP_TILES, TILE, F).astype(jnp.float32)
        product = jnp.einsum('bij,bjf->bif', masked(device), group_rows[col_table[device]])
        partial_sum = jnp.zeros((PANEL_TILES, TILE, F), jnp.float32).at[row_table[device]].add(product)
        return (summed.at[panel_index].add(partial_sum), None)
    devices_list = jnp.arange(DEVICES, dtype=jnp.int32)
    summed, _ = lax.scan(forward_step, jnp.zeros((N_ROW, PANEL_TILES, TILE, F), jnp.float32), devices_list)
    hidden = summed.reshape(NODES, F).astype(jnp.bfloat16)
    pre_act = jnp.dot(hidden, weight, preferred_element_type=jnp.float32)
    out_features = activate(pre_act).astype(jnp.bfloat16)
    pre_grad = activate_grad(pre_act, cotangent.astype(jnp.float32)).astype(jnp.bfloat16)
    weight_grad = jnp.dot(hidden.T, pre_grad, preferred_element_type=jnp.float32)
    hidden_grad = jnp.dot(pre_grad, weight.T, preferred_element_type=jnp.float32).astype(jnp.bfloat16)
    grad_panels = hidden_grad.reshape(N_ROW, PANEL_TILES, TILE, F).astype(jnp.float32)

    def backward_step(summed, device):
        panel_index = device // N_COL
        group_index = device % N_COL
        panel_grad = lax.dynamic_index_in_dim(grad_panels, panel_index, 0, keepdims=False)
        product = jnp.einsum('bij,bif->bjf', masked(device), panel_grad[row_table[device]])
        partial_sum = jnp.zeros((GROUP_TILES, TILE, F), jnp.float32).at[col_table[device]].add(product)
        return (summed.at[group_index].add(partial_sum), None)
    group_grads, _ = lax.scan(backward_step, jnp.zeros((N_COL, GROUP_TILES, TILE, F), jnp.float32), devices_list)
    feature_grad = group_grads.reshape(N_COL, N_ROW, NODE_DEV, F).transpose(1, 0, 2, 3).reshape(NODES, F)
    return (out_features, weight_grad, feature_grad.astype(jnp.bfloat16))
```

```python
import jax
import jax.numpy as jnp
from jax import lax
from jax.experimental import pallas as pl
from jax.experimental.pallas import tpu as pltpu
from jax.sharding import PartitionSpec as P

MESH = pl.DeviceIdType.MESH
BF16, F32 = jnp.bfloat16, jnp.float32
VMEM_BYTES = 48 * 2**20
RING = 4
UNROLL = 8


class Links:
    def __init__(self, send_sem, recv_sem):
        self.send_sem, self.recv_sem, self.copies = send_sem, recv_sem, []

    def start(self, src, dst, device):
        at = len(self.copies)
        copy = pltpu.make_async_remote_copy(
            src_ref=src,
            dst_ref=dst,
            send_sem=self.send_sem.at[at],
            recv_sem=self.recv_sem.at[at],
            device_id=device,
            device_id_type=MESH,
        )
        copy.start()
        self.copies.append(copy)
        return copy

    def drain(self):
        for copy in self.copies:
            copy.wait_send()


class Axis:
    def __init__(self, position, device_at):
        self.position = position
        self.up = device_at(lax.rem(position + 1, RING))
        self.down = device_at(lax.rem(position + 3, RING))

    def at(self, offset):
        return lax.rem(self.position + offset, RING) if offset else self.position


class Place:
    def __init__(self):
        row, col = lax.axis_index("row"), lax.axis_index("col")
        self.row, self.col = row, col
        y, self.core = lax.div(row, 2), lax.rem(row, 2)
        x, z = lax.div(col, RING), lax.rem(col, RING)
        core = self.core
        self.y = Axis(y, lambda k: (k * 2 + core, col))
        self.x = Axis(x, lambda k: (row, k * RING + z))
        self.z = Axis(z, lambda k: (row, x * RING + k))
        self.sibling_row = row + 1 - 2 * core
        self.sibling = (self.sibling_row, col)

    def greet(self, axes, sibling):
        others = [d for axis in axes for d in (axis.up, axis.down)]
        if sibling:
            others.append(self.sibling)
        barrier = pltpu.get_barrier_semaphore()
        for other in others:
            pl.semaphore_signal(barrier, inc=1, device_id=other, device_id_type=MESH)
        pl.semaphore_wait(barrier, len(others))


class Sum4:
    def __init__(self, links, axis, part, buffers):
        self.links, self.axis, self.part = links, axis, part
        self.relay_up, self.relay_down, self.from_down, self.from_up = buffers
        half = self.relay_up.shape[0]
        self.low, self.high = pl.ds(0, half), pl.ds(half, half)

    def push_far(self):
        far = self.part(2)
        self.c_up = self.links.start(far.at[self.low], self.relay_up, self.axis.up)
        self.c_down = self.links.start(far.at[self.high], self.relay_down, self.axis.down)

    def push_up(self):
        self.n_up = self.links.start(
            self.part(1).at[self.high], self.from_down.at[self.high], self.axis.up
        )

    def push_down(self):
        self.n_down = self.links.start(
            self.part(3).at[self.low], self.from_up.at[self.low], self.axis.down
        )

    def push(self):
        self.push_far()
        self.push_up()
        self.push_down()

    def relay(self):
        self.c_up.wait_recv()
        mine = self.part(1)[self.low]
        self.relay_up[...] = (self.relay_up[...].astype(F32) + mine.astype(F32)).astype(BF16)
        self.r_up = self.links.start(self.relay_up, self.from_down.at[self.low], self.axis.up)
        self.c_down.wait_recv()
        mine = self.part(3)[self.high]
        self.relay_down[...] = (self.relay_down[...].astype(F32) + mine.astype(F32)).astype(BF16)
        self.r_down = self.links.start(
            self.relay_down, self.from_up.at[self.high], self.axis.down
        )

    def finish(self):
        for copy in (self.n_up, self.n_down, self.r_up, self.r_down):
            copy.wait_recv()
        return (
            self.part(0)[...].astype(F32)
            + self.from_down[...].astype(F32)
            + self.from_up[...].astype(F32)
        )


class Share4:
    def __init__(self, links, axis, slot, half):
        self.links, self.axis, self.slot = links, axis, slot
        self.low, self.high = pl.ds(0, half), pl.ds(half, half)

    def send(self, k, rows, device):
        ref = self.slot(k).at[rows]
        return self.links.start(ref, ref, device)

    def push(self):
        self.up_low = self.send(0, self.low, self.axis.up)
        self.down_high = self.send(0, self.high, self.axis.down)
        self.up_high = self.send(0, self.high, self.axis.up)
        self.down_low = self.send(0, self.low, self.axis.down)

    def relay(self):
        self.up_low.wait_recv()
        self.far_low = self.send(3, self.low, self.axis.up)
        self.down_high.wait_recv()
        self.far_high = self.send(1, self.high, self.axis.down)

    def near(self):
        self.up_high.wait_recv()
        self.down_low.wait_recv()

    def far(self):
        self.far_low.wait_recv()
        self.far_high.wait_recv()


def gather_row_kernel(own_ref, all_ref, send_sem, recv_sem):
    here = Place()
    here.greet([here.y], True)
    links = Links(send_sem, recv_sem)
    half = own_ref.shape[0] // 2
    all_ref[here.row] = own_ref[...]

    def slot(k):
        return all_ref.at[here.y.at(k) * 2 + here.core]

    share = Share4(links, here.y, slot, half)

    def across(k, rows):
        ref = slot(k).at[rows]
        return links.start(ref, ref, here.sibling)

    low, high = share.low, share.high
    share.push()
    twins = [across(0, low), across(0, high)]
    share.relay()
    twins += [across(3, low), across(1, high)]
    share.near()
    twins += [across(3, high), across(1, low)]
    share.far()
    twins += [across(2, low), across(2, high)]
    for copy in twins:
        copy.wait_recv()
    links.drain()


def tile_kernel(backward, count_ref, to_ref, from_ref, tiles_ref, source_ref, out_ref, total):
    total[...] = jnp.zeros_like(total)
    count = count_ref[0]
    contract = ((0,), (0,)) if backward else ((1,), (0,))

    def step(block, _):
        first = block * UNROLL
        products = []
        for k in range(UNROLL):
            product = lax.dot_general(
                tiles_ref[first + k],
                source_ref[from_ref[first + k]],
                (contract, ((), ())),
                preferred_element_type=F32,
            )
            products.append(jnp.where(first + k < count, product, 0.0))
        for k in range(UNROLL):
            total[to_ref[first + k]] += products[k]
        return 0

    lax.fori_loop(0, lax.div(count + UNROLL - 1, UNROLL), step, 0)
    out_ref[...] = total[...].astype(BF16)


def activation(value):
    root = 0.7978845608028654
    square = value * value
    t = jnp.tanh(root * (value + 0.044715 * (value * square)))
    half = 0.5 * (1.0 + t)
    slope = half + (0.5 * value) * (1.0 - t * t) * (root * (1.0 + 3.0 * 0.044715 * square))
    return value * half, slope


def middle_kernel(
    part_ref, weight_ref, cot_ref, out_ref, term_ref, grads_ref,
    relay_buf, from_buf, part2_buf, relay2_buf, from2_buf, hidden_buf, grad_buf, send_sem, recv_sem,
):
    here = Place()
    here.greet([here.x, here.z], False)
    links = Links(send_sem, recv_sem)
    rows = part_ref.shape[1] // 2
    quarter = rows // 2
    halves = (0, 1)
    slices = [pl.ds(h * rows, rows) for h in halves]
    firsts, seconds = (here.z, here.x), (here.x, here.z)

    def col_of(h, first, second):
        return second * RING + first if h == 0 else first * RING + second

    def sum_first(h, delta):
        first, second = firsts[h], seconds[h]

        def part(k):
            return part_ref.at[col_of(h, first.at(k), second.at(delta)), slices[h]]

        r, f = relay_buf.at[h, delta], from_buf.at[h, delta]
        return Sum4(links, first, part, (r.at[0], r.at[1], f.at[0], f.at[1]))

    def sum_second(h):
        r, f = relay2_buf.at[h], from2_buf.at[h]
        return Sum4(
            links, seconds[h], lambda k: part2_buf.at[h, k], (r.at[0], r.at[1], f.at[0], f.at[1])
        )

    sums = [[sum_first(h, d) for d in range(RING)] for h in halves]
    lasts = [sum_second(h) for h in halves]

    def done_first(h, d):
        part2_buf[h, d] = sums[h][d].finish().astype(part2_buf.dtype)

    for d in (2, 1):
        for h in halves:
            sums[h][d].push()
    for d, then in ((2, 3), (1, 0)):
        for h in halves:
            sums[h][d].relay()
        for h in halves:
            sums[h][then].push()
    for h in halves:
        done_first(h, 2)
        lasts[h].push_far()
    for d in (3, 0):
        for h in halves:
            sums[h][d].relay()
    for h in halves:
        done_first(h, 1)
        lasts[h].push_up()
        done_first(h, 3)
        lasts[h].push_down()
    for h in halves:
        lasts[h].relay()
    for h in halves:
        done_first(h, 0)

    weight = weight_ref[...]

    def dense(h):
        hidden = lasts[h].finish().astype(BF16)
        pre_act = jnp.dot(hidden, weight, preferred_element_type=F32)
        value, slope = activation(pre_act)
        pre_grad = (cot_ref[slices[h]].astype(F32) * slope).astype(BF16)
        own = lax.dot_general(
            pre_grad, weight, (((1,), (1,)), ((), ())), preferred_element_type=F32
        )
        grads_ref[here.col, slices[h]] = own.astype(BF16)
        out_ref[slices[h]] = value.astype(BF16)
        hidden_buf[slices[h]] = hidden
        grad_buf[slices[h]] = pre_grad

    def share_first(h):
        first, second = seconds[h], firsts[h]
        return Share4(
            links,
            first,
            lambda k: grads_ref.at[col_of(1 - h, first.at(k), second.position), slices[h]],
            quarter,
        )

    def share_second(h, delta):
        first, second = seconds[h], firsts[h]
        return Share4(
            links,
            second,
            lambda k: grads_ref.at[col_of(1 - h, first.at(delta), second.at(k)), slices[h]],
            quarter,
        )

    ones = [share_first(h) for h in halves]
    twos = [[share_second(h, d) for d in range(RING)] for h in halves]
    for h in halves:
        dense(h)
        ones[h].push()
        twos[h][0].push()
    term_ref[...] = lax.dot_general(
        hidden_buf[...], grad_buf[...], (((0,), (0,)), ((), ())), preferred_element_type=F32
    )
    for h in halves:
        ones[h].relay()
    for h in halves:
        ones[h].near()
        twos[h][0].relay()
        twos[h][1].push()
        twos[h][3].push()
    for h in halves:
        ones[h].far()
        twos[h][2].push()
    for d in (1, 3, 2):
        for h in halves:
            twos[h][d].relay()
    for d in (0, 1, 3, 2):
        for h in halves:
            twos[h][d].near()
            twos[h][d].far()
    links.drain()


def sum_row_kernel(part_ref, out_ref, own_buf, twin_buf, relay_buf, from_buf, send_sem, recv_sem):
    here = Place()
    here.greet([here.y], True)
    links = Links(send_sem, recv_sem)

    def block(k, core):
        return part_ref.at[here.y.at(k) * 2 + core]

    order = (2, 1, 3, 0)
    twins = {k: links.start(block(k, 1 - here.core), twin_buf.at[k], here.sibling) for k in order}
    total = Sum4(
        links,
        here.y,
        lambda k: own_buf.at[k],
        (relay_buf.at[0], relay_buf.at[1], from_buf.at[0], from_buf.at[1]),
    )
    pushes = {2: total.push_far, 1: total.push_up, 3: total.push_down}
    for k in order:
        twins[k].wait_recv()
        own_buf[k] = (block(k, here.core)[...].astype(F32) + twin_buf[k].astype(F32)).astype(
            own_buf.dtype
        )
        if k in pushes:
            pushes[k]()
    total.relay()
    out_ref[...] = total.finish().astype(BF16)
    links.drain()


def whole():
    return pl.BlockSpec(memory_space=pltpu.VMEM)


def small():
    return pl.BlockSpec(memory_space=pltpu.SMEM)


def semaphores(count):
    return [pltpu.SemaphoreType.DMA((count,))] * 2


def params(collective_id=None):
    if collective_id is None:
        return pltpu.CompilerParams(vmem_limit_bytes=VMEM_BYTES)
    return pltpu.CompilerParams(
        vmem_limit_bytes=VMEM_BYTES, collective_id=collective_id, has_side_effects=True
    )


def tile_pass(backward, count, to, source_ids, tiles, source, out_tiles):
    tile, width = source.shape[1:]
    return pl.pallas_call(
        lambda *refs: tile_kernel(backward, *refs),
        out_shape=jax.ShapeDtypeStruct((out_tiles, tile, width), BF16),
        in_specs=[small()] * 3 + [whole()] * 2,
        out_specs=whole(),
        scratch_shapes=[pltpu.VMEM((out_tiles, tile, width), F32)],
        compiler_params=params(),
        name="backward_tiles" if backward else "forward_tiles",
    )(count, to, source_ids, tiles, source)


def shards(features, weight, adj_tiles, tile_rows, tile_cols, tile_count, cotangent):
    nodes, width = features.shape
    tile = adj_tiles.shape[1]
    n_row, n_col = lax.axis_size("row"), lax.axis_size("col")
    panel_tiles, group_tiles = n_col * nodes // tile, n_row * nodes // tile
    half, quarter = nodes // 2, nodes // 4

    group = pl.pallas_call(
        gather_row_kernel,
        out_shape=jax.ShapeDtypeStruct((n_row, nodes, width), BF16),
        in_specs=[whole()],
        out_specs=whole(),
        scratch_shapes=semaphores(14),
        compiler_params=params(0),
        name="gather_row",
    )(features)
    partial = tile_pass(
        False, tile_count, tile_rows, tile_cols, adj_tiles,
        group.reshape(group_tiles, tile, width), panel_tiles,
    )
    out_features, term, grads = pl.pallas_call(
        middle_kernel,
        out_shape=(
            jax.ShapeDtypeStruct((nodes, width), BF16),
            jax.ShapeDtypeStruct((width, width), F32),
            jax.ShapeDtypeStruct((n_col, nodes, width), BF16),
        ),
        in_specs=[whole()] * 3,
        out_specs=(whole(),) * 3,
        scratch_shapes=[
            pltpu.VMEM((2, RING, 2, quarter, width), BF16),
            pltpu.VMEM((2, RING, 2, half, width), BF16),
            pltpu.VMEM((2, RING, half, width), BF16),
            pltpu.VMEM((2, 2, quarter, width), BF16),
            pltpu.VMEM((2, 2, half, width), BF16),
            pltpu.VMEM((nodes, width), BF16),
            pltpu.VMEM((nodes, width), BF16),
            *semaphores(120),
        ],
        compiler_params=params(1),
        name="middle",
    )(partial.reshape(n_col, nodes, width), weight, cotangent)
    weight_grad = lax.psum(term, ("row", "col"))
    sums = tile_pass(
        True, tile_count, tile_cols, tile_rows, adj_tiles,
        grads.reshape(panel_tiles, tile, width), group_tiles,
    )
    feature_grad = pl.pallas_call(
        sum_row_kernel,
        out_shape=jax.ShapeDtypeStruct((nodes, width), BF16),
        in_specs=[whole()],
        out_specs=whole(),
        scratch_shapes=[
            pltpu.VMEM((RING, nodes, width), BF16),
            pltpu.VMEM((RING, nodes, width), BF16),
            pltpu.VMEM((2, half, width), BF16),
            pltpu.VMEM((2, nodes, width), BF16),
            *semaphores(10),
        ],
        compiler_params=params(2),
        name="sum_row",
    )(sums.reshape(n_row, nodes, width))
    return (out_features, weight_grad, feature_grad)


def solution(mesh):
    in_specs = (
        P(("row", "col"), None),
        P(),
        P(("row", "col"), None, None),
        P(("row", "col")),
        P(("row", "col")),
        P(("row", "col")),
        P(("row", "col"), None),
    )
    out_specs = (P(("row", "col"), None), P(), P(("row", "col"), None))
    return jax.shard_map(shards, mesh=mesh, in_specs=in_specs, out_specs=out_specs, check_vma=False)
```

```python
import jax
import jax.numpy as jnp
from jax import lax
from jax.experimental import pallas as pl
from jax.experimental.pallas import tpu as pltpu
from jax.sharding import PartitionSpec as P

MESH = pl.DeviceIdType.MESH
BF16, F32 = jnp.bfloat16, jnp.float32
VMEM_BYTES = 48 * 2**20
RING = 4
UNROLL = 8


class Links:
    def __init__(self, send_sem, recv_sem):
        self.send_sem, self.recv_sem, self.copies = send_sem, recv_sem, []

    def start(self, src, dst, device):
        at = len(self.copies)
        copy = pltpu.make_async_remote_copy(
            src_ref=src,
            dst_ref=dst,
            send_sem=self.send_sem.at[at],
            recv_sem=self.recv_sem.at[at],
            device_id=device,
            device_id_type=MESH,
        )
        copy.start()
        self.copies.append(copy)
        return copy

    def drain(self):
        for copy in self.copies:
            copy.wait_send()


class Axis:
    def __init__(self, position, device_at):
        self.position = position
        self.up = device_at(lax.rem(position + 1, RING))
        self.down = device_at(lax.rem(position + 3, RING))
        odd = lax.rem(position, 2)
        self.pair = device_at(position + 1 - 2 * odd)
        self.other_pair = device_at(lax.rem(position + 3 + 2 * odd, RING))

    def at(self, offset):
        return lax.rem(self.position + offset, RING) if offset else self.position


class Place:
    def __init__(self):
        row, col = lax.axis_index("row"), lax.axis_index("col")
        self.row, self.col = row, col
        y, self.core = lax.div(row, 2), lax.rem(row, 2)
        x, z = lax.div(col, RING), lax.rem(col, RING)
        core = self.core
        self.y = Axis(y, lambda k: (k * 2 + core, col))
        self.x = Axis(x, lambda k: (row, k * RING + z))
        self.z = Axis(z, lambda k: (row, x * RING + k))
        self.sibling_row = row + 1 - 2 * core
        self.sibling = (self.sibling_row, col)

    def greet(self, axes, sibling):
        others = [d for axis in axes for d in (axis.up, axis.down)]
        if sibling:
            others.append(self.sibling)
        barrier = pltpu.get_barrier_semaphore()
        for other in others:
            pl.semaphore_signal(barrier, inc=1, device_id=other, device_id_type=MESH)
        pl.semaphore_wait(barrier, len(others))


def add_to(ref, value):
    ref[...] = (ref[...].astype(F32) + value.astype(F32)).astype(ref.dtype)


class Sum4:
    def __init__(self, links, axis, part, buffers):
        self.links, self.axis, self.part = links, axis, part
        self.relay_up, self.relay_down, self.from_down, self.from_up = buffers
        half = self.relay_up.shape[0]
        self.low, self.high = pl.ds(0, half), pl.ds(half, half)

    def push_far(self):
        far = self.part(2)
        self.c_up = self.links.start(far.at[self.low], self.relay_up, self.axis.up)
        self.c_down = self.links.start(far.at[self.high], self.relay_down, self.axis.down)

    def push_up(self):
        self.n_up = self.links.start(
            self.part(1).at[self.high], self.from_down.at[self.high], self.axis.up
        )

    def push_down(self):
        self.n_down = self.links.start(
            self.part(3).at[self.low], self.from_up.at[self.low], self.axis.down
        )

    def push(self):
        self.push_far()
        self.push_up()
        self.push_down()

    def relay(self):
        self.c_up.wait_recv()
        mine = self.part(1)[self.low]
        add_to(self.relay_up, mine)
        self.r_up = self.links.start(self.relay_up, self.from_down.at[self.low], self.axis.up)
        self.c_down.wait_recv()
        mine = self.part(3)[self.high]
        add_to(self.relay_down, mine)
        self.r_down = self.links.start(
            self.relay_down, self.from_up.at[self.high], self.axis.down
        )

    def finish(self):
        for copy in (self.n_up, self.n_down, self.r_up, self.r_down):
            copy.wait_recv()
        return (
            self.part(0)[...].astype(F32)
            + self.from_down[...].astype(F32)
            + self.from_up[...].astype(F32)
        )


class Share4:
    def __init__(self, links, axis, slot, half):
        self.links, self.axis, self.slot = links, axis, slot
        self.low, self.high = pl.ds(0, half), pl.ds(half, half)

    def send(self, k, rows, device):
        ref = self.slot(k).at[rows]
        return self.links.start(ref, ref, device)

    def push(self):
        self.up_low = self.send(0, self.low, self.axis.up)
        self.down_high = self.send(0, self.high, self.axis.down)
        self.up_high = self.send(0, self.high, self.axis.up)
        self.down_low = self.send(0, self.low, self.axis.down)

    def relay(self):
        self.up_low.wait_recv()
        self.far_low = self.send(3, self.low, self.axis.up)
        self.down_high.wait_recv()
        self.far_high = self.send(1, self.high, self.axis.down)

    def near(self):
        self.up_high.wait_recv()
        self.down_low.wait_recv()

    def far(self):
        self.far_low.wait_recv()
        self.far_high.wait_recv()


class SumAll:
    def __init__(self, links, here, term, result, relay, came, own, got):
        x = here.x
        self.links, self.own, self.got = links, own, got
        self.ring = Sum4(
            links, x, lambda k: term.at[x.at(k)], (relay.at[0], relay.at[1], came.at[0], came.at[1])
        )
        self.share = Share4(links, x, lambda k: result.at[x.at(k)], result.shape[1] // 2)
        self.slot = result.at[x.position]
        pairs = (here.z.pair, here.z.other_pair, here.y.pair, here.y.other_pair, here.sibling)
        self.steps = self.run(pairs)

    def run(self, pairs):
        self.ring.push()
        yield
        self.ring.relay()
        yield
        total = self.ring.finish()
        for at, pair in enumerate(pairs):
            self.own[at] = total
            copy = self.links.start(self.own.at[at], self.got.at[at], pair)
            yield
            copy.wait_recv()
            total = self.own[at] + self.got[at]
        self.slot[...] = total
        self.share.push()
        yield
        self.share.relay()
        yield
        self.share.near()
        self.share.far()

    def next(self):
        next(self.steps, None)


def gather_row_kernel(own_ref, all_ref, send_sem, recv_sem):
    here = Place()
    here.greet([here.y], True)
    links = Links(send_sem, recv_sem)
    half = own_ref.shape[0] // 2
    all_ref[here.row] = own_ref[...]

    def slot(k):
        return all_ref.at[here.y.at(k) * 2 + here.core]

    share = Share4(links, here.y, slot, half)

    def across(k, rows):
        ref = slot(k).at[rows]
        return links.start(ref, ref, here.sibling)

    low, high = share.low, share.high
    share.push()
    twins = [across(0, low), across(0, high)]
    share.relay()
    twins += [across(3, low), across(1, high)]
    share.near()
    twins += [across(3, high), across(1, low)]
    share.far()
    twins += [across(2, low), across(2, high)]
    for copy in twins:
        copy.wait_recv()
    links.drain()


def tile_kernel(backward, count_ref, to_ref, from_ref, tiles_ref, source_ref, out_ref, total):
    total[...] = jnp.zeros_like(total)
    count = count_ref[0]
    contract = ((0,), (0,)) if backward else ((1,), (0,))

    def step(block, _):
        first = block * UNROLL
        products = []
        for k in range(UNROLL):
            product = lax.dot_general(
                tiles_ref[first + k],
                source_ref[from_ref[first + k]],
                (contract, ((), ())),
                preferred_element_type=F32,
            )
            products.append(jnp.where(first + k < count, product, 0.0))
        for k in range(UNROLL):
            total[to_ref[first + k]] += products[k]
        return 0

    lax.fori_loop(0, lax.div(count + UNROLL - 1, UNROLL), step, 0)
    out_ref[...] = total[...].astype(BF16)


def activation(value):
    root = 0.7978845608028654
    square = value * value
    t = jnp.tanh(root * (value + 0.044715 * (value * square)))
    half = 0.5 * (1.0 + t)
    slope = half + (0.5 * value) * (1.0 - t * t) * (root * (1.0 + 3.0 * 0.044715 * square))
    return value * half, slope


def middle_kernel(
    part_ref, weight_ref, cot_ref, out_ref, weight_grad_ref, grads_ref,
    relay_buf, from_buf, part2_buf, relay2_buf, from2_buf, hidden_buf, grad_buf,
    term_buf, term_relay, term_from, term_own, term_got, send_sem, recv_sem,
):
    here = Place()
    here.greet([here.x, here.y, here.z], True)
    links = Links(send_sem, recv_sem)
    rows = part_ref.shape[1] // 2
    quarter = rows // 2
    halves = (0, 1)
    slices = [pl.ds(h * rows, rows) for h in halves]
    firsts, seconds = (here.z, here.x), (here.x, here.z)

    def col_of(h, first, second):
        return second * RING + first if h == 0 else first * RING + second

    def sum_first(h, delta):
        first, second = firsts[h], seconds[h]

        def part(k):
            return part_ref.at[col_of(h, first.at(k), second.at(delta)), slices[h]]

        r, f = relay_buf.at[h, delta], from_buf.at[h, delta]
        return Sum4(links, first, part, (r.at[0], r.at[1], f.at[0], f.at[1]))

    def sum_second(h):
        r, f = relay2_buf.at[h], from2_buf.at[h]
        return Sum4(
            links, seconds[h], lambda k: part2_buf.at[h, k], (r.at[0], r.at[1], f.at[0], f.at[1])
        )

    sums = [[sum_first(h, d) for d in range(RING)] for h in halves]
    lasts = [sum_second(h) for h in halves]

    def done_first(h, d):
        part2_buf[h, d] = sums[h][d].finish().astype(part2_buf.dtype)

    for d in (2, 1):
        for h in halves:
            sums[h][d].push()
    for d, then in ((2, 3), (1, 0)):
        for h in halves:
            sums[h][d].relay()
        for h in halves:
            sums[h][then].push()
    for h in halves:
        done_first(h, 2)
        lasts[h].push_far()
    for d in (3, 0):
        for h in halves:
            sums[h][d].relay()
    for h in halves:
        done_first(h, 1)
        lasts[h].push_up()
        done_first(h, 3)
        lasts[h].push_down()
    for h in halves:
        lasts[h].relay()
    for h in halves:
        done_first(h, 0)

    weight = weight_ref[...]

    def dense(h):
        hidden = lasts[h].finish().astype(BF16)
        pre_act = jnp.dot(hidden, weight, preferred_element_type=F32)
        value, slope = activation(pre_act)
        pre_grad = (cot_ref[slices[h]].astype(F32) * slope).astype(BF16)
        own = lax.dot_general(
            pre_grad, weight, (((1,), (1,)), ((), ())), preferred_element_type=F32
        )
        grads_ref[here.col, slices[h]] = own.astype(BF16)
        out_ref[slices[h]] = value.astype(BF16)
        hidden_buf[slices[h]] = hidden
        grad_buf[slices[h]] = pre_grad

    def share_first(h):
        first, second = seconds[h], firsts[h]
        return Share4(
            links,
            first,
            lambda k: grads_ref.at[col_of(1 - h, first.at(k), second.position), slices[h]],
            quarter,
        )

    def share_second(h, delta):
        first, second = seconds[h], firsts[h]
        return Share4(
            links,
            second,
            lambda k: grads_ref.at[col_of(1 - h, first.at(delta), second.at(k)), slices[h]],
            quarter,
        )

    ones = [share_first(h) for h in halves]
    twos = [[share_second(h, d) for d in range(RING)] for h in halves]
    for h in halves:
        dense(h)
        ones[h].push()
        twos[h][0].push()
    term = lax.dot_general(
        hidden_buf[...], grad_buf[...], (((0,), (0,)), ((), ())), preferred_element_type=F32
    )
    term_buf[...] = term.reshape(term_buf.shape)
    total = SumAll(
        links, here, term_buf, weight_grad_ref, term_relay, term_from, term_own, term_got
    )
    total.next()
    for h in halves:
        ones[h].relay()
    total.next()
    for h in halves:
        ones[h].near()
        twos[h][0].relay()
        twos[h][1].push()
        twos[h][3].push()
    total.next()
    for h in halves:
        ones[h].far()
        twos[h][2].push()
    total.next()
    for d in (1, 3, 2):
        for h in halves:
            twos[h][d].relay()
        total.next()
    for d in (0, 1, 3, 2):
        for h in halves:
            twos[h][d].near()
            twos[h][d].far()
        total.next()
    links.drain()


def sum_row_kernel(part_ref, out_ref, own_buf, twin_buf, relay_buf, from_buf, send_sem, recv_sem):
    here = Place()
    here.greet([here.y], True)
    links = Links(send_sem, recv_sem)

    def block(k, core):
        return part_ref.at[here.y.at(k) * 2 + core]

    order = (2, 1, 3, 0)
    twins = {k: links.start(block(k, 1 - here.core), twin_buf.at[k], here.sibling) for k in order}
    total = Sum4(
        links,
        here.y,
        lambda k: own_buf.at[k],
        (relay_buf.at[0], relay_buf.at[1], from_buf.at[0], from_buf.at[1]),
    )
    pushes = {2: total.push_far, 1: total.push_up, 3: total.push_down}
    for k in order:
        twins[k].wait_recv()
        own_buf[k] = (block(k, here.core)[...].astype(F32) + twin_buf[k].astype(F32)).astype(
            own_buf.dtype
        )
        if k in pushes:
            pushes[k]()
    total.relay()
    out_ref[...] = total.finish().astype(BF16)
    links.drain()


def whole():
    return pl.BlockSpec(memory_space=pltpu.VMEM)


def small():
    return pl.BlockSpec(memory_space=pltpu.SMEM)


def semaphores(count):
    return [pltpu.SemaphoreType.DMA((count,))] * 2


def params(collective_id=None):
    if collective_id is None:
        return pltpu.CompilerParams(vmem_limit_bytes=VMEM_BYTES)
    return pltpu.CompilerParams(
        vmem_limit_bytes=VMEM_BYTES, collective_id=collective_id, has_side_effects=True
    )


def tile_pass(backward, count, to, source_ids, tiles, source, out_tiles):
    tile, width = source.shape[1:]
    return pl.pallas_call(
        lambda *refs: tile_kernel(backward, *refs),
        out_shape=jax.ShapeDtypeStruct((out_tiles, tile, width), BF16),
        in_specs=[small()] * 3 + [whole()] * 2,
        out_specs=whole(),
        scratch_shapes=[pltpu.VMEM((out_tiles, tile, width), F32)],
        compiler_params=params(),
        name="backward_tiles" if backward else "forward_tiles",
    )(count, to, source_ids, tiles, source)


def shards(features, weight, adj_tiles, tile_rows, tile_cols, tile_count, cotangent):
    nodes, width = features.shape
    tile = adj_tiles.shape[1]
    n_row, n_col = lax.axis_size("row"), lax.axis_size("col")
    panel_tiles, group_tiles = n_col * nodes // tile, n_row * nodes // tile
    half, quarter = nodes // 2, nodes // 4

    group = pl.pallas_call(
        gather_row_kernel,
        out_shape=jax.ShapeDtypeStruct((n_row, nodes, width), BF16),
        in_specs=[whole()],
        out_specs=whole(),
        scratch_shapes=semaphores(14),
        compiler_params=params(0),
        name="gather_row",
    )(features)
    partial = tile_pass(
        False, tile_count, tile_rows, tile_cols, adj_tiles,
        group.reshape(group_tiles, tile, width), panel_tiles,
    )
    out_features, weight_grad, grads = pl.pallas_call(
        middle_kernel,
        out_shape=(
            jax.ShapeDtypeStruct((nodes, width), BF16),
            jax.ShapeDtypeStruct((RING, width // RING, width), F32),
            jax.ShapeDtypeStruct((n_col, nodes, width), BF16),
        ),
        in_specs=[whole()] * 3,
        out_specs=(whole(),) * 3,
        scratch_shapes=[
            pltpu.VMEM((2, RING, 2, quarter, width), BF16),
            pltpu.VMEM((2, RING, 2, half, width), BF16),
            pltpu.VMEM((2, RING, half, width), BF16),
            pltpu.VMEM((2, 2, quarter, width), BF16),
            pltpu.VMEM((2, 2, half, width), BF16),
            pltpu.VMEM((nodes, width), BF16),
            pltpu.VMEM((nodes, width), BF16),
            pltpu.VMEM((RING, width // RING, width), F32),
            pltpu.VMEM((2, width // RING // 2, width), F32),
            pltpu.VMEM((2, width // RING, width), F32),
            pltpu.VMEM((5, width // RING, width), F32),
            pltpu.VMEM((5, width // RING, width), F32),
            *semaphores(137),
        ],
        compiler_params=params(1),
        name="middle",
    )(partial.reshape(n_col, nodes, width), weight, cotangent)
    sums = tile_pass(
        True, tile_count, tile_cols, tile_rows, adj_tiles,
        grads.reshape(panel_tiles, tile, width), group_tiles,
    )
    feature_grad = pl.pallas_call(
        sum_row_kernel,
        out_shape=jax.ShapeDtypeStruct((nodes, width), BF16),
        in_specs=[whole()],
        out_specs=whole(),
        scratch_shapes=[
            pltpu.VMEM((RING, nodes, width), BF16),
            pltpu.VMEM((RING, nodes, width), BF16),
            pltpu.VMEM((2, half, width), BF16),
            pltpu.VMEM((2, nodes, width), BF16),
            *semaphores(10),
        ],
        compiler_params=params(2),
        name="sum_row",
    )(sums.reshape(n_row, nodes, width))
    return (out_features, weight_grad.reshape(width, width), feature_grad)


def solution(mesh):
    in_specs = (
        P(("row", "col"), None),
        P(),
        P(("row", "col"), None, None),
        P(("row", "col")),
        P(("row", "col")),
        P(("row", "col")),
        P(("row", "col"), None),
    )
    out_specs = (P(("row", "col"), None), P(), P(("row", "col"), None))
    return jax.shard_map(shards, mesh=mesh, in_specs=in_specs, out_specs=out_specs, check_vma=False)
```

```python
import jax
import jax.numpy as jnp
from jax import lax
from jax.experimental import pallas as pl
from jax.experimental.pallas import tpu as pltpu
from jax.sharding import PartitionSpec as P

MESH = pl.DeviceIdType.MESH
BF16, F32 = jnp.bfloat16, jnp.float32
VMEM_BYTES = 63 * 2**20
RING = 4
UNROLL = 8


class Links:
    def __init__(self, send_sem, recv_sem):
        self.send_sem, self.recv_sem, self.copies = send_sem, recv_sem, []

    def start(self, src, dst, device):
        at = len(self.copies)
        copy = pltpu.make_async_remote_copy(
            src_ref=src,
            dst_ref=dst,
            send_sem=self.send_sem.at[at],
            recv_sem=self.recv_sem.at[at],
            device_id=device,
            device_id_type=MESH,
        )
        copy.start()
        self.copies.append(copy)
        return copy

    def drain(self):
        for copy in self.copies:
            copy.wait_send()


class Axis:
    def __init__(self, position, device_at):
        self.position = position
        self.up = device_at(lax.rem(position + 1, RING))
        self.down = device_at(lax.rem(position + 3, RING))
        odd = lax.rem(position, 2)
        self.pair = device_at(position + 1 - 2 * odd)
        self.other_pair = device_at(lax.rem(position + 3 + 2 * odd, RING))

    def at(self, offset):
        return lax.rem(self.position + offset, RING) if offset else self.position


class Place:
    def __init__(self):
        row, col = lax.axis_index("row"), lax.axis_index("col")
        self.row, self.col = row, col
        y, self.core = lax.div(row, 2), lax.rem(row, 2)
        x, z = lax.div(col, RING), lax.rem(col, RING)
        core = self.core
        self.y = Axis(y, lambda k: (k * 2 + core, col))
        self.x = Axis(x, lambda k: (row, k * RING + z))
        self.z = Axis(z, lambda k: (row, x * RING + k))
        self.sibling_row = row + 1 - 2 * core
        self.sibling = (self.sibling_row, col)

    def greet(self):
        barrier = pltpu.get_barrier_semaphore()
        others = [d for axis in (self.x, self.y, self.z) for d in (axis.up, axis.down)]
        others.append(self.sibling)
        for other in others:
            pl.semaphore_signal(barrier, inc=1, device_id=other, device_id_type=MESH)
        return lambda: pl.semaphore_wait(barrier, len(others))


def add_to(ref, value):
    ref[...] = (ref[...].astype(F32) + value.astype(F32)).astype(ref.dtype)


class Sum4:
    def __init__(self, links, axis, part, buffers):
        self.links, self.axis, self.part = links, axis, part
        self.relay_up, self.relay_down, self.from_down, self.from_up = buffers
        half = self.relay_up.shape[0]
        self.low, self.high = pl.ds(0, half), pl.ds(half, half)

    def push_far(self):
        far = self.part(2)
        self.c_up = self.links.start(far.at[self.low], self.relay_up, self.axis.up)
        self.c_down = self.links.start(far.at[self.high], self.relay_down, self.axis.down)

    def push_up(self):
        self.n_up = self.links.start(
            self.part(1).at[self.high], self.from_down.at[self.high], self.axis.up
        )

    def push_down(self):
        self.n_down = self.links.start(
            self.part(3).at[self.low], self.from_up.at[self.low], self.axis.down
        )

    def push(self):
        self.push_far()
        self.push_up()
        self.push_down()

    def relay(self):
        self.c_up.wait_recv()
        mine = self.part(1)[self.low]
        add_to(self.relay_up, mine)
        self.r_up = self.links.start(self.relay_up, self.from_down.at[self.low], self.axis.up)
        self.c_down.wait_recv()
        mine = self.part(3)[self.high]
        add_to(self.relay_down, mine)
        self.r_down = self.links.start(
            self.relay_down, self.from_up.at[self.high], self.axis.down
        )

    def finish(self):
        for copy in (self.n_up, self.n_down, self.r_up, self.r_down):
            copy.wait_recv()
        return (
            self.part(0)[...].astype(F32)
            + self.from_down[...].astype(F32)
            + self.from_up[...].astype(F32)
        )


class Share4:
    def __init__(self, links, axis, slot, half):
        self.links, self.axis, self.slot = links, axis, slot
        self.low, self.high = pl.ds(0, half), pl.ds(half, half)

    def send(self, k, rows, device):
        ref = self.slot(k).at[rows]
        return self.links.start(ref, ref, device)

    def push(self):
        self.up_low = self.send(0, self.low, self.axis.up)
        self.down_high = self.send(0, self.high, self.axis.down)
        self.up_high = self.send(0, self.high, self.axis.up)
        self.down_low = self.send(0, self.low, self.axis.down)

    def relay(self):
        self.up_low.wait_recv()
        self.far_low = self.send(3, self.low, self.axis.up)
        self.down_high.wait_recv()
        self.far_high = self.send(1, self.high, self.axis.down)

    def near(self):
        self.up_high.wait_recv()
        self.down_low.wait_recv()

    def far(self):
        self.far_low.wait_recv()
        self.far_high.wait_recv()


class SumAll:
    def __init__(self, links, here, term, result, relay, came, own, got):
        x = here.x
        self.links, self.own, self.got = links, own, got
        self.ring = Sum4(
            links, x, lambda k: term.at[x.at(k)], (relay.at[0], relay.at[1], came.at[0], came.at[1])
        )
        self.share = Share4(links, x, lambda k: result.at[x.at(k)], result.shape[1] // 2)
        self.slot = result.at[x.position]
        pairs = (here.z.pair, here.z.other_pair, here.y.pair, here.y.other_pair, here.sibling)
        self.steps = self.run(pairs)

    def run(self, pairs):
        self.ring.push()
        yield
        self.ring.relay()
        yield
        total = self.ring.finish()
        for at, pair in enumerate(pairs):
            self.own[at] = total
            copy = self.links.start(self.own.at[at], self.got.at[at], pair)
            yield
            copy.wait_recv()
            total = self.own[at] + self.got[at]
        self.slot[...] = total
        self.share.push()
        yield
        self.share.relay()
        yield
        self.share.near()
        self.share.far()

    def next(self):
        next(self.steps, None)


def activation(value):
    root = 0.7978845608028654
    square = value * value
    t = jnp.tanh(root * (value + 0.044715 * (value * square)))
    half = 0.5 * (1.0 + t)
    slope = half + (0.5 * value) * (1.0 - t * t) * (root * (1.0 + 3.0 * 0.044715 * square))
    return value * half, slope


def spread(row):
    wide = jnp.broadcast_to(row, (row.shape[1], row.shape[1]))
    return wide, wide.T


def slot_order(key, source, count, empty):
    lanes = key.shape[1]
    lane = lax.broadcasted_iota(jnp.int32, (lanes, lanes), 1)
    sub = lax.broadcasted_iota(jnp.int32, (lanes, lanes), 0)
    at = lax.broadcasted_iota(jnp.int32, (1, lanes), 1)
    key = jnp.where(at < count, key, 2 * lanes)

    def over(mask, value):
        return jnp.sum(jnp.where(mask, value, 0), axis=0, keepdims=True)

    unique_row, unique_col = spread(key * lanes + at)
    _, rank = spread(over(unique_col < unique_row, 1))
    _, key_col = spread(key)
    _, source_col = spread(source)
    hit = rank == lane
    slot, source, sorted_key = over(hit, sub), over(hit, source_col), over(hit, key_col)
    same = over((rank == lane - 1) & (key_col == sorted_key), 1)
    last = jnp.where(over(key_col == lane, 1) > 0, over(key_col <= lane, 1) - 1, empty)
    return slot, source, same, last


def layer_kernel(
    count_ref, features_ref, weight_ref, adj_ref, rows_ref, cols_ref, cot_ref,
    out_ref, weight_grad_ref, feature_grad_ref,
    x_buf, weight_buf, adj, ids_buf, cot_buf, table_buf, table,
    group_0, group_1, running, parts, relay_buf, from_buf, part2_buf, relay2_buf, from2_buf,
    cot_t, hidden_buf, grad_buf, value_buf, grads_0, grads_1,
    term_buf, term_relay, term_from, term_own, term_got,
    sums, own_buf, twin_buf, relay3_buf, from3_buf, local_sem, send_sem, recv_sem,
):
    here = Place()
    group, grads = (group_0, group_1), (grads_0, grads_1)
    tiles, width, tile = parts.shape[2], parts.shape[3], parts.shape[4]
    slots = adj.shape[0]
    links = Links(send_sem, recv_sem)
    loads = [
        pltpu.make_async_copy(src, dst, local_sem.at[i])
        for i, (src, dst) in enumerate(
            (
                (features_ref, x_buf),
                (rows_ref, ids_buf.at[0]),
                (cols_ref, ids_buf.at[1]),
                (adj_ref, adj),
                (weight_ref, weight_buf),
                (cot_ref, cot_buf),
            )
        )
    ]
    for load in loads:
        load.start()
    met = here.greet()
    feature_halves = node_halves = (0, 1)

    def tile_rows(t):
        return pl.ds(t * tile, tile)

    shares = []
    twins = [[], []]

    def row_slot(h, k):
        return group[h].at[here.y.at(k) * 2 + here.core]

    def across(h, k, rows):
        ref = row_slot(h, k).at[rows]
        twins[h].append(links.start(ref, ref, here.sibling))

    loads[0].wait()
    for h in feature_halves:
        for t in range(tiles):
            block = x_buf[tile_rows(t), pl.ds(h * width, width)]
            group[h][here.row, t] = block.astype(F32).T.astype(BF16)
        if h == 0:
            met()
        share = Share4(links, here.y, lambda k, h=h: row_slot(h, k), tiles // 2)
        share.push()
        low, high = share.low, share.high
        across(h, 0, low)
        across(h, 0, high)
        shares.append(share)

    loads[1].wait()
    loads[2].wait()
    table_buf[...] = jnp.zeros_like(table_buf)
    for i in (0, 1):
        table_buf[i : i + 1, 0:slots] = ids_buf[i]
    by_row, by_col = table_buf[0:1, :], table_buf[1:2, :]
    count = count_ref[0]
    order = slot_order(by_row, by_col, count, slots) + slot_order(by_col, by_row, count, slots)
    for i, line in enumerate(order):
        table_buf[i : i + 1, :] = line
    to_scalars = pltpu.make_async_copy(table_buf, table, local_sem.at[6])
    to_scalars.start()
    running[slots] = jnp.zeros(running.shape[1:], BF16)

    def gather_near(h):
        shares[h].relay()
        across(h, 3, low)
        across(h, 1, high)
        shares[h].near()
        across(h, 3, high)
        across(h, 1, low)

    def gather_far(h):
        shares[h].far()
        across(h, 2, low)
        across(h, 2, high)

    def gather_done(h):
        for copy in twins[h]:
            copy.wait_recv()

    def tile_pass(source, backward):
        base = 4 if backward else 0
        contract = ((1,), (0,)) if backward else ((1,), (1,))

        def step(block, acc):
            products = []
            for k in range(UNROLL):
                at = block * UNROLL + k
                node = table[base + 1, at]
                products.append(
                    lax.dot_general(
                        source[lax.div(node, tiles), lax.rem(node, tiles)],
                        adj[table[base, at]],
                        (contract, ((), ())),
                        preferred_element_type=F32,
                    )
                )
            for k in range(UNROLL):
                at = block * UNROLL + k
                acc = acc * table[base + 2, at].astype(F32) + products[k]
                running[at] = acc.astype(BF16)
            return acc

        lax.fori_loop(0, slots // UNROLL, step, jnp.zeros((width, tile), F32))

    def pick(target, base, block):
        for t in range(tiles):
            target[block, t] = running[table[base + 3, block * tiles + t]]

    firsts, seconds = (here.z, here.x), (here.x, here.z)
    node_slices = [pl.ds(a * (tiles // 2), tiles // 2) for a in node_halves]

    def col_of(a, first, second):
        return second * RING + first if a == 0 else first * RING + second

    def sum_first(h, a, delta):
        first, second = firsts[a], seconds[a]

        def part(k):
            return parts.at[h, col_of(a, first.at(k), second.at(delta)), node_slices[a]]

        r, f = relay_buf.at[h, a, delta], from_buf.at[h, a, delta]
        return Sum4(links, first, part, (r.at[0], r.at[1], f.at[0], f.at[1]))

    def sum_second(h, a):
        r, f = relay2_buf.at[h, a], from2_buf.at[h, a]
        return Sum4(
            links, seconds[a], lambda k: part2_buf.at[h, a, k], (r.at[0], r.at[1], f.at[0], f.at[1])
        )

    first_sums = [
        [[sum_first(h, a, d) for d in range(RING)] for a in node_halves] for h in feature_halves
    ]
    last_sums = [[sum_second(h, a) for a in node_halves] for h in feature_halves]

    def push_first(h, d):
        for a in node_halves:
            first_sums[h][a][d].push()

    def relay_first(h, d):
        for a in node_halves:
            first_sums[h][a][d].relay()

    def done_first(h, a, d):
        part2_buf[h, a, d] = first_sums[h][a][d].finish().astype(BF16)

    def scatter_start(h):
        lax.fori_loop(0, RING * RING, lambda b, _: (pick(parts.at[h], 0, b), 0)[1], 0)
        for d in (2, 1, 3):
            push_first(h, d)

    def scatter_relay(h):
        relay_first(h, 2)
        push_first(h, 0)
        relay_first(h, 1)

    def scatter_far(h):
        for a in node_halves:
            done_first(h, a, 2)
            last_sums[h][a].push_far()
        relay_first(h, 3)
        relay_first(h, 0)

    def scatter_last(h):
        for a in node_halves:
            done_first(h, a, 1)
            last_sums[h][a].push_up()
            done_first(h, a, 3)
            last_sums[h][a].push_down()

    def scatter_end(h):
        for a in node_halves:
            last_sums[h][a].relay()
        for a in node_halves:
            done_first(h, a, 0)

    gather_near(0)
    gather_far(0)
    gather_near(1)
    gather_done(0)
    to_scalars.wait()
    loads[3].wait()
    tile_pass(group[0], False)
    scatter_start(0)
    gather_far(1)
    gather_done(1)
    tile_pass(group[1], False)
    scatter_start(1)
    scatter_relay(0)
    loads[4].wait()
    loads[5].wait()
    for t in range(tiles):
        cot_t[t] = cot_buf[tile_rows(t), :].astype(F32).T
    scatter_relay(1)
    scatter_far(0)
    scatter_far(1)
    scatter_last(0)
    scatter_last(1)
    scatter_end(0)
    scatter_end(1)

    weight = weight_buf[...]

    def dense(a):
        whole = [last_sums[h][a].finish().astype(BF16) for h in feature_halves]
        for i in range(tiles // 2):
            t = a * (tiles // 2) + i
            hidden = jnp.concatenate([whole[0][i], whole[1][i]], axis=0)
            pre_act = lax.dot_general(
                weight, hidden, (((0,), (0,)), ((), ())), preferred_element_type=F32
            )
            value, slope = activation(pre_act)
            pre_grad = (cot_t[t] * slope).astype(BF16)
            own = jnp.dot(weight, pre_grad, preferred_element_type=F32).astype(BF16)
            for h in feature_halves:
                grads[h][here.col, t] = own[h * width : (h + 1) * width]
            value_buf[t] = value
            hidden_buf[t] = hidden
            grad_buf[t] = pre_grad

    def share_first(h, a):
        first, second = seconds[a], firsts[a]
        return Share4(
            links,
            first,
            lambda k: grads[h].at[col_of(1 - a, first.at(k), second.position), node_slices[a]],
            tiles // 4,
        )

    def share_second(h, a, delta):
        first, second = seconds[a], firsts[a]
        return Share4(
            links,
            second,
            lambda k: grads[h].at[col_of(1 - a, first.at(delta), second.at(k)), node_slices[a]],
            tiles // 4,
        )

    ones = [[share_first(h, a) for a in node_halves] for h in feature_halves]
    twos = [
        [[share_second(h, a, d) for a in node_halves] for d in range(RING)] for h in feature_halves
    ]

    def each(things, *verbs):
        for verb in verbs:
            for thing in things:
                getattr(thing, verb)()

    totals = [
        Sum4(
            links,
            here.y,
            lambda k, h=h: own_buf.at[h, k],
            (relay3_buf.at[h, 0], relay3_buf.at[h, 1], from3_buf.at[h, 0], from3_buf.at[h, 1]),
        )
        for h in feature_halves
    ]
    near_order = (2, 1, 3, 0)
    exchanged = [{}, {}]

    def block(h, k, core):
        return sums.at[h, here.y.at(k) * 2 + core]

    def back_start(h):
        tile_pass(grads[h], True)
        lax.fori_loop(0, RING * 2, lambda b, _: (pick(sums.at[h], 4, b), 0)[1], 0)
        for k in near_order:
            exchanged[h][k] = links.start(
                block(h, k, 1 - here.core), twin_buf.at[h, k], here.sibling
            )

    def back_push(h):
        pushes = {2: totals[h].push_far, 1: totals[h].push_up, 3: totals[h].push_down}
        for k in near_order:
            exchanged[h][k].wait_recv()
            own = block(h, k, here.core)[...].astype(F32) + twin_buf[h, k].astype(F32)
            own_buf[h, k] = own.astype(BF16)
            if k in pushes:
                pushes[k]()

    def back_end(h):
        whole = totals[h].finish()
        for t in range(tiles):
            feature_grad_ref[tile_rows(t), pl.ds(h * width, width)] = whole[t].T.astype(BF16)

    for a in node_halves:
        dense(a)
        ones[0][a].push()
        twos[0][0][a].push()
    for t in range(tiles):
        term = lax.dot_general(
            hidden_buf[t], grad_buf[t], (((1,), (1,)), ((), ())), preferred_element_type=F32
        ).reshape(term_buf.shape)
        if t == 0:
            term_buf[...] = term
        else:
            term_buf[...] += term
    weights = SumAll(
        links, here, term_buf, weight_grad_ref, term_relay, term_from, term_own, term_got
    )
    each(ones[0], "relay")
    weights.next()
    each(ones[1], "push")
    each(ones[0], "near")
    each(twos[0][1] + twos[0][3], "push")
    each(twos[0][0], "relay")
    weights.next()
    each(ones[0], "far")
    each(twos[0][2], "push")
    each(twos[1][0], "push")
    weights.next()
    each(ones[1], "relay")
    each(twos[0][1] + twos[0][3], "relay")
    weights.next()
    each(ones[1], "near")
    each(twos[1][1] + twos[1][3], "push")
    each(twos[0][2], "relay")
    weights.next()
    each(twos[1][0], "relay")
    for d in (0, 1, 3, 2):
        each(twos[0][d], "near", "far")
    each(ones[1], "far")
    each(twos[1][2], "push")
    weights.next()
    back_start(0)
    each(twos[1][1] + twos[1][3], "relay")
    weights.next()
    back_push(0)
    each(twos[1][2], "relay")
    weights.next()
    totals[0].relay()
    for t in range(tiles):
        out_ref[tile_rows(t), :] = value_buf[t].T.astype(BF16)
    weights.next()
    for d in (0, 1, 3, 2):
        each(twos[1][d], "near", "far")
    back_start(1)
    weights.next()
    back_push(1)
    back_end(0)
    weights.next()
    totals[1].relay()
    back_end(1)
    links.drain()


def shards(features, weight, adj_tiles, tile_rows, tile_cols, tile_count, cotangent):
    nodes, width = features.shape
    slots, tile = adj_tiles.shape[:2]
    n_row, n_col = lax.axis_size("row"), lax.axis_size("col")
    tiles, half, member = nodes // tile, width // 2, width // RING
    one = (half, tile)

    def vmem(*shape, dtype=BF16):
        return pltpu.VMEM(shape, dtype)

    anywhere = pl.BlockSpec(memory_space=pl.ANY)
    in_vmem = pl.BlockSpec(memory_space=pltpu.VMEM)
    out_features, weight_grad, feature_grad = pl.pallas_call(
        layer_kernel,
        out_shape=(
            jax.ShapeDtypeStruct((nodes, width), BF16),
            jax.ShapeDtypeStruct((RING, member, width), F32),
            jax.ShapeDtypeStruct((nodes, width), BF16),
        ),
        in_specs=[pl.BlockSpec(memory_space=pltpu.SMEM)] + [anywhere] * 6,
        out_specs=(in_vmem,) * 3,
        scratch_shapes=[
            vmem(nodes, width),
            vmem(width, width),
            vmem(slots, tile, tile),
            vmem(2, 1, slots, dtype=jnp.int32),
            vmem(nodes, width),
            vmem(8, 128, dtype=jnp.int32),
            pltpu.SMEM((8, 128), jnp.int32),
            vmem(n_row, tiles, *one),
            vmem(n_row, tiles, *one),
            vmem(slots + 1, *one),
            vmem(2, n_col, tiles, *one),
            vmem(2, 2, RING, 2, tiles // 4, *one),
            vmem(2, 2, RING, 2, tiles // 2, *one),
            vmem(2, 2, RING, tiles // 2, *one),
            vmem(2, 2, 2, tiles // 4, *one),
            vmem(2, 2, 2, tiles // 2, *one),
            vmem(tiles, width, tile, dtype=F32),
            vmem(tiles, width, tile),
            vmem(tiles, width, tile),
            vmem(tiles, width, tile, dtype=F32),
            vmem(n_col, tiles, *one),
            vmem(n_col, tiles, *one),
            vmem(RING, member, width, dtype=F32),
            vmem(2, member // 2, width, dtype=F32),
            vmem(2, member, width, dtype=F32),
            vmem(5, member, width, dtype=F32),
            vmem(5, member, width, dtype=F32),
            vmem(2, n_row, tiles, *one),
            vmem(2, RING, tiles, *one),
            vmem(2, RING, tiles, *one),
            vmem(2, 2, tiles // 2, *one),
            vmem(2, 2, tiles, *one),
            pltpu.SemaphoreType.DMA((7,)),
            pltpu.SemaphoreType.DMA((305,)),
            pltpu.SemaphoreType.DMA((305,)),
        ],
        compiler_params=pltpu.CompilerParams(
            vmem_limit_bytes=VMEM_BYTES, collective_id=0, has_side_effects=True
        ),
        name="layer",
    )(
        tile_count, features, weight, adj_tiles,
        tile_rows.reshape(1, slots), tile_cols.reshape(1, slots), cotangent,
    )
    return (out_features, weight_grad.reshape(width, width), feature_grad)


def solution(mesh):
    in_specs = (
        P(("row", "col"), None),
        P(),
        P(("row", "col"), None, None),
        P(("row", "col")),
        P(("row", "col")),
        P(("row", "col")),
        P(("row", "col"), None),
    )
    out_specs = (P(("row", "col"), None), P(), P(("row", "col"), None))
    return jax.shard_map(shards, mesh=mesh, in_specs=in_specs, out_specs=out_specs, check_vma=False)
```

```python
import jax
import jax.numpy as jnp
from jax import lax
from jax.experimental import pallas as pl
from jax.experimental.pallas import tpu as pltpu
from jax.sharding import PartitionSpec as P

MESH = pl.DeviceIdType.MESH
BF16, F32 = jnp.bfloat16, jnp.float32
VMEM_BYTES = 63 * 2**20
RING = 4
UNROLL = 8


class Links:
    def __init__(self, send_sem, recv_sem):
        self.send_sem, self.recv_sem = send_sem, recv_sem
        self.used, self.phases = 0, []

    def semaphore(self):
        self.used += 1
        return self.recv_sem.at[self.used - 1]

    def phase(self, ref):
        self.phases.append(ref)
        return len(self.phases) - 1

    def start(self, src, dst, device, arrived, phase):
        pltpu.make_async_remote_copy(
            src_ref=src,
            dst_ref=dst,
            send_sem=self.send_sem.at[phase],
            recv_sem=arrived,
            device_id=device,
            device_id_type=MESH,
        ).start()

    def wait(self, arrived, ref):
        pltpu.make_async_copy(ref, ref, arrived).wait()

    def drain(self):
        for at, ref in enumerate(self.phases):
            self.wait(self.send_sem.at[at], ref)


class Axis:
    def __init__(self, position, device_at):
        self.position = position
        self.up = device_at(lax.rem(position + 1, RING))
        self.down = device_at(lax.rem(position + 3, RING))
        odd = lax.rem(position, 2)
        self.pair = device_at(position + 1 - 2 * odd)
        self.other_pair = device_at(lax.rem(position + 3 + 2 * odd, RING))

    def at(self, offset):
        return lax.rem(self.position + offset, RING) if offset else self.position


class Place:
    def __init__(self):
        row, col = lax.axis_index("row"), lax.axis_index("col")
        self.row, self.col = row, col
        y, self.core = lax.div(row, 2), lax.rem(row, 2)
        x, z = lax.div(col, RING), lax.rem(col, RING)
        core = self.core
        self.y = Axis(y, lambda k: (k * 2 + core, col))
        self.x = Axis(x, lambda k: (row, k * RING + z))
        self.z = Axis(z, lambda k: (row, x * RING + k))
        self.sibling_row = row + 1 - 2 * core
        self.sibling = (self.sibling_row, col)

    def greet(self):
        barrier = pltpu.get_barrier_semaphore()
        others = [d for axis in (self.x, self.y, self.z) for d in (axis.up, axis.down)]
        others.append(self.sibling)
        for other in others:
            pl.semaphore_signal(barrier, inc=1, device_id=other, device_id_type=MESH)
        return lambda: pl.semaphore_wait(barrier, len(others))


def add_to(ref, value):
    ref[...] = (ref[...].astype(F32) + value.astype(F32)).astype(ref.dtype)


class Sum4:
    def __init__(self, links, axis, part, relays, blocks, passing, arrived, phase):
        self.links, self.axis, self.part = links, axis, part
        self.relay_up, self.relay_down = relays.at[0], relays.at[1]
        self.from_down, self.from_up = blocks.at[0], blocks.at[1]
        self.passing, self.arrived, self.phase = passing, arrived, phase
        half = relays.shape[1]
        self.low, self.high = pl.ds(0, half), pl.ds(half, half)

    def send(self, src, dst, device, arrived):
        self.links.start(src, dst, device, arrived, self.phase)

    def push_far(self):
        far = self.part(2)
        self.send(far.at[self.low], self.relay_up, self.axis.up, self.passing)
        self.send(far.at[self.high], self.relay_down, self.axis.down, self.passing)

    def push_up(self):
        near = self.part(1).at[self.high]
        self.send(near, self.from_down.at[self.high], self.axis.up, self.arrived)

    def push_down(self):
        near = self.part(3).at[self.low]
        self.send(near, self.from_up.at[self.low], self.axis.down, self.arrived)

    def push(self):
        self.push_far()
        self.push_up()
        self.push_down()

    def relay(self):
        add_to(self.relay_up, self.part(1)[self.low])
        self.send(self.relay_up, self.from_down.at[self.low], self.axis.up, self.arrived)
        add_to(self.relay_down, self.part(3)[self.high])
        self.send(self.relay_down, self.from_up.at[self.high], self.axis.down, self.arrived)

    def total(self):
        return (
            self.part(0)[...].astype(F32)
            + self.from_down[...].astype(F32)
            + self.from_up[...].astype(F32)
        )


class Share4:
    def __init__(self, links, axis, slot, half, first, near, far, phase):
        self.links, self.axis, self.slot = links, axis, slot
        self.first, self.near, self.far, self.phase = first, near, far, phase
        self.low, self.high = pl.ds(0, half), pl.ds(half, half)

    def send(self, k, rows, device, arrived):
        ref = self.slot(k).at[rows]
        self.links.start(ref, ref, device, arrived, self.phase)

    def push(self):
        self.send(0, self.low, self.axis.up, self.first)
        self.send(0, self.high, self.axis.down, self.first)
        self.send(0, self.high, self.axis.up, self.near)
        self.send(0, self.low, self.axis.down, self.near)

    def relay(self):
        self.send(3, self.low, self.axis.up, self.far)
        self.send(1, self.high, self.axis.down, self.far)


class SumAll:
    def __init__(self, links, here, term, result, relay, came, own, got):
        x = here.x
        self.links, self.own, self.got, self.relays, self.came = links, own, got, relay, came
        self.result = result
        phase = links.phase(own)
        passing, arrived, self.first, self.rest = (links.semaphore() for _ in range(4))
        self.ring = Sum4(links, x, lambda k: term.at[x.at(k)], relay, came, passing, arrived, phase)
        self.share = Share4(
            links, x, lambda k: result.at[x.at(k)], result.shape[1] // 2,
            self.first, self.rest, self.rest, phase,
        )
        self.slot = result.at[x.position]
        pairs = (here.z.pair, here.z.other_pair, here.y.pair, here.y.other_pair, here.sibling)
        self.steps = self.run(pairs)

    def run(self, pairs):
        links, ring, share = self.links, self.ring, self.share
        ring.push()
        yield
        links.wait(ring.passing, self.relays)
        ring.relay()
        yield
        links.wait(ring.arrived, self.came)
        total = ring.total()
        for at, pair in enumerate(pairs):
            self.own[at] = total
            arrived = links.semaphore()
            links.start(self.own.at[at], self.got.at[at], pair, arrived, ring.phase)
            yield
            links.wait(arrived, self.got.at[at])
            total = self.own[at] + self.got[at]
        self.slot[...] = total
        share.push()
        yield
        links.wait(self.first, self.result.at[0])
        share.relay()
        yield
        links.wait(self.rest, self.result.at[pl.ds(0, 2)])

    def next(self):
        next(self.steps, None)


def activation(value):
    root = 0.7978845608028654
    square = value * value
    t = jnp.tanh(root * (value + 0.044715 * (value * square)))
    half = 0.5 * (1.0 + t)
    slope = half + (0.5 * value) * (1.0 - t * t) * (root * (1.0 + 3.0 * 0.044715 * square))
    return value * half, slope


def spread(row):
    wide = jnp.broadcast_to(row, (row.shape[1], row.shape[1]))
    return wide, wide.T


def slot_order(key, source, count, empty):
    lanes = key.shape[1]
    lane = lax.broadcasted_iota(jnp.int32, (lanes, lanes), 1)
    sub = lax.broadcasted_iota(jnp.int32, (lanes, lanes), 0)
    at = lax.broadcasted_iota(jnp.int32, (1, lanes), 1)
    key = jnp.where(at < count, key, 2 * lanes)

    def over(mask, value):
        return jnp.sum(jnp.where(mask, value, 0), axis=0, keepdims=True)

    unique_row, unique_col = spread(key * lanes + at)
    _, rank = spread(over(unique_col < unique_row, 1))
    _, key_col = spread(key)
    _, source_col = spread(source)
    hit = rank == lane
    slot, source, sorted_key = over(hit, sub), over(hit, source_col), over(hit, key_col)
    same = over((rank == lane - 1) & (key_col == sorted_key), 1)
    last = jnp.where(over(key_col == lane, 1) > 0, over(key_col <= lane, 1) - 1, empty)
    return slot, source, same, last


def layer_kernel(
    count_ref, features_ref, weight_ref, adj_ref, rows_ref, cols_ref, cot_ref,
    out_ref, weight_grad_ref, feature_grad_ref,
    x_buf, weight_buf, adj, ids_buf, cot_buf, table_buf, table,
    group_0, group_1, running, parts, relay_buf, from_buf, part2_buf, relay2_buf, from2_buf,
    cot_t, hidden_buf, grad_buf, value_buf, grads_0, grads_1,
    term_buf, term_relay, term_from, term_own, term_got,
    sums, own_buf, twin_buf, relay3_buf, from3_buf, local_sem, send_sem, recv_sem,
):
    here = Place()
    group, grads = (group_0, group_1), (grads_0, grads_1)
    tiles, width, tile = parts.shape[2], parts.shape[3], parts.shape[4]
    slots = adj.shape[0]
    links = Links(send_sem, recv_sem)
    loads = [
        pltpu.make_async_copy(src, dst, local_sem.at[i])
        for i, (src, dst) in enumerate(
            (
                (features_ref, x_buf),
                (rows_ref, ids_buf.at[0]),
                (cols_ref, ids_buf.at[1]),
                (adj_ref, adj),
                (weight_ref, weight_buf),
                (cot_ref, cot_buf),
            )
        )
    ]
    for load in loads:
        load.start()
    met = here.greet()
    feature_halves = node_halves = (0, 1)

    def tile_rows(t):
        return pl.ds(t * tile, tile)

    def row_slot(h, k):
        return group[h].at[here.y.at(k) * 2 + here.core]

    def share_row(h):
        first, near, far = (links.semaphore() for _ in range(3))
        phase = links.phase(parts.at[h, pl.ds(0, 7)])
        return Share4(
            links, here.y, lambda k: row_slot(h, k), tiles // 2, first, near, far, phase
        )

    shares = [share_row(h) for h in feature_halves]
    twins = [links.semaphore() for _ in feature_halves]
    low, high = shares[0].low, shares[0].high

    def across(h, k, rows):
        ref = row_slot(h, k).at[rows]
        links.start(ref, ref, here.sibling, twins[h], shares[h].phase)

    def gather_load(h):
        for t in range(tiles):
            block = x_buf[tile_rows(t), pl.ds(h * width, width)]
            group[h][here.row, t] = block.astype(F32).T.astype(BF16)

    def gather_push(h):
        shares[h].push()
        across(h, 0, low)
        across(h, 0, high)

    def gather_relay(h):
        links.wait(shares[h].first, group[h].at[0])
        shares[h].relay()
        across(h, 3, low)
        across(h, 1, high)

    def gather_near(h):
        links.wait(shares[h].near, group[h].at[0])
        across(h, 3, high)
        across(h, 1, low)

    def gather_far(h):
        links.wait(shares[h].far, group[h].at[0])
        across(h, 2, low)
        across(h, 2, high)

    def gather_done(h):
        links.wait(twins[h], group[h].at[pl.ds(0, 4)])

    loads[0].wait()
    gather_load(0)
    met()
    gather_push(0)
    gather_load(1)

    loads[1].wait()
    loads[2].wait()
    table_buf[...] = jnp.zeros_like(table_buf)
    for i in (0, 1):
        table_buf[i : i + 1, 0:slots] = ids_buf[i]
    by_row, by_col = table_buf[0:1, :], table_buf[1:2, :]
    count = count_ref[0]
    order = slot_order(by_row, by_col, count, slots) + slot_order(by_col, by_row, count, slots)
    for i, line in enumerate(order):
        table_buf[i : i + 1, :] = line
    to_scalars = pltpu.make_async_copy(table_buf, table, local_sem.at[6])
    to_scalars.start()
    running[slots] = jnp.zeros(running.shape[1:], BF16)

    def tile_pass(source, backward):
        base = 4 if backward else 0
        contract = ((1,), (0,)) if backward else ((1,), (1,))

        def step(block, acc):
            products = []
            for k in range(UNROLL):
                at = block * UNROLL + k
                node = table[base + 1, at]
                products.append(
                    lax.dot_general(
                        source[lax.div(node, tiles), lax.rem(node, tiles)],
                        adj[table[base, at]],
                        (contract, ((), ())),
                        preferred_element_type=F32,
                    )
                )
            for k in range(UNROLL):
                at = block * UNROLL + k
                acc = acc * table[base + 2, at].astype(F32) + products[k]
                running[at] = acc.astype(BF16)
            return acc

        lax.fori_loop(0, slots // UNROLL, step, jnp.zeros((width, tile), F32))

    def pick(target, base, block):
        for t in range(tiles):
            target[block, t] = running[table[base + 3, block * tiles + t]]

    firsts, seconds = (here.z, here.x), (here.x, here.z)
    node_slices = [pl.ds(a * (tiles // 2), tiles // 2) for a in node_halves]

    def col_of(a, first, second):
        return second * RING + first if a == 0 else first * RING + second

    passing, arrived = (
        [[links.semaphore() for _ in range(RING)] for _ in feature_halves] for _ in range(2)
    )
    passing_2, arrived_2 = ([links.semaphore() for _ in feature_halves] for _ in range(2))
    phases = [links.phase(parts.at[h, pl.ds(0, 15)]) for h in feature_halves]

    def sum_first(h, a, delta):
        first, second = firsts[a], seconds[a]

        def part(k):
            return parts.at[h, col_of(a, first.at(k), second.at(delta)), node_slices[a]]

        return Sum4(
            links, first, part, relay_buf.at[h, delta, a], from_buf.at[h, delta, a],
            passing[h][delta], arrived[h][delta], phases[h],
        )

    def sum_second(h, a):
        return Sum4(
            links, seconds[a], lambda k: part2_buf.at[h, a, k], relay2_buf.at[h, a],
            from2_buf.at[h, a], passing_2[h], arrived_2[h], phases[h],
        )

    first_sums = [
        [[sum_first(h, a, d) for d in range(RING)] for a in node_halves] for h in feature_halves
    ]
    last_sums = [[sum_second(h, a) for a in node_halves] for h in feature_halves]

    def push_first(h, d):
        for a in node_halves:
            first_sums[h][a][d].push()

    def relay_first(h, d):
        links.wait(passing[h][d], relay_buf.at[h, d])
        for a in node_halves:
            first_sums[h][a][d].relay()

    def wait_first(h, d):
        links.wait(arrived[h][d], from_buf.at[h, d])

    def done_first(h, a, d):
        part2_buf[h, a, d] = first_sums[h][a][d].total().astype(BF16)

    def scatter_start(h):
        lax.fori_loop(0, RING * RING, lambda b, _: (pick(parts.at[h], 0, b), 0)[1], 0)
        for d in (2, 1, 3, 0):
            push_first(h, d)

    def scatter_relay(h):
        for d in (2, 1, 3, 0):
            relay_first(h, d)

    def scatter_far(h):
        wait_first(h, 2)
        for a in node_halves:
            done_first(h, a, 2)
            last_sums[h][a].push_far()

    def scatter_near(h):
        wait_first(h, 1)
        for a in node_halves:
            done_first(h, a, 1)
            last_sums[h][a].push_up()
        wait_first(h, 3)
        for a in node_halves:
            done_first(h, a, 3)
            last_sums[h][a].push_down()

    def scatter_end(h):
        links.wait(passing_2[h], relay2_buf.at[h])
        for a in node_halves:
            last_sums[h][a].relay()
        wait_first(h, 0)
        for a in node_halves:
            done_first(h, a, 0)

    gather_relay(0)
    gather_push(1)
    gather_near(0)
    gather_far(0)
    gather_relay(1)
    gather_done(0)
    to_scalars.wait()
    loads[3].wait()
    tile_pass(group[0], False)
    scatter_start(0)
    gather_near(1)
    gather_far(1)
    gather_done(1)
    tile_pass(group[1], False)
    scatter_start(1)
    scatter_relay(0)
    loads[4].wait()
    loads[5].wait()
    for t in range(tiles):
        cot_t[t] = cot_buf[tile_rows(t), :].astype(F32).T
    scatter_relay(1)
    scatter_far(0)
    scatter_far(1)
    scatter_near(0)
    scatter_near(1)
    scatter_end(0)
    scatter_end(1)

    weight = weight_buf[...]

    def dense(a):
        whole = [last_sums[h][a].total().astype(BF16) for h in feature_halves]
        for i in range(tiles // 2):
            t = a * (tiles // 2) + i
            hidden = jnp.concatenate([whole[0][i], whole[1][i]], axis=0)
            pre_act = lax.dot_general(
                weight, hidden, (((0,), (0,)), ((), ())), preferred_element_type=F32
            )
            value, slope = activation(pre_act)
            pre_grad = (cot_t[t] * slope).astype(BF16)
            own = jnp.dot(weight, pre_grad, preferred_element_type=F32).astype(BF16)
            for h in feature_halves:
                grads[h][here.col, t] = own[h * width : (h + 1) * width]
            value_buf[t] = value
            hidden_buf[t] = hidden
            grad_buf[t] = pre_grad

    share_phases = [links.phase(parts.at[h, pl.ds(0, 15)]) for h in feature_halves]
    one_sems = [[links.semaphore() for _ in range(3)] for _ in feature_halves]
    two_sems = [[links.semaphore() for _ in range(RING)] for _ in feature_halves]
    rest_sems = [links.semaphore() for _ in feature_halves]

    def share_first(h, a):
        first, second = seconds[a], firsts[a]
        return Share4(
            links,
            first,
            lambda k: grads[h].at[col_of(1 - a, first.at(k), second.position), node_slices[a]],
            tiles // 4,
            *one_sems[h],
            share_phases[h],
        )

    def share_second(h, a, delta):
        first, second = seconds[a], firsts[a]
        return Share4(
            links,
            second,
            lambda k: grads[h].at[col_of(1 - a, first.at(delta), second.at(k)), node_slices[a]],
            tiles // 4,
            two_sems[h][delta],
            rest_sems[h],
            rest_sems[h],
            share_phases[h],
        )

    ones = [[share_first(h, a) for a in node_halves] for h in feature_halves]
    twos = [
        [[share_second(h, a, d) for a in node_halves] for d in range(RING)] for h in feature_halves
    ]

    def one_push(h):
        for share in ones[h]:
            share.push()

    def one_wait(h, which):
        links.wait(one_sems[h][which], grads[h].at[0])

    def one_relay(h):
        one_wait(h, 0)
        for share in ones[h]:
            share.relay()

    def two_push(h, *offsets):
        for d in offsets:
            for share in twos[h][d]:
                share.push()

    def two_relay(h, *offsets):
        for d in offsets:
            links.wait(two_sems[h][d], grads[h].at[0])
            for share in twos[h][d]:
                share.relay()

    def shared(h):
        links.wait(rest_sems[h], grads[h].at[pl.ds(0, 8)])

    back_phases = [links.phase(parts.at[h, pl.ds(0, 7)]) for h in feature_halves]
    passing_3, arrived_3 = ([links.semaphore() for _ in feature_halves] for _ in range(2))
    swapped = [[links.semaphore() for _ in range(RING)] for _ in feature_halves]
    totals = [
        Sum4(
            links, here.y, lambda k, h=h: own_buf.at[h, k], relay3_buf.at[h], from3_buf.at[h],
            passing_3[h], arrived_3[h], back_phases[h],
        )
        for h in feature_halves
    ]
    near_order = (2, 1, 3, 0)

    def block(h, k, core):
        return sums.at[h, here.y.at(k) * 2 + core]

    def back_swap(h):
        lax.fori_loop(0, RING * 2, lambda b, _: (pick(sums.at[h], 4, b), 0)[1], 0)
        for k in near_order:
            links.start(
                block(h, k, 1 - here.core), twin_buf.at[h, k], here.sibling, swapped[h][k],
                back_phases[h],
            )

    def back_push(h):
        pushes = {2: totals[h].push_far, 1: totals[h].push_up, 3: totals[h].push_down}
        for k in near_order:
            links.wait(swapped[h][k], twin_buf.at[h, k])
            own = block(h, k, here.core)[...].astype(F32) + twin_buf[h, k].astype(F32)
            own_buf[h, k] = own.astype(BF16)
            if k in pushes:
                pushes[k]()

    def back_relay(h):
        links.wait(passing_3[h], relay3_buf.at[h])
        totals[h].relay()

    def back_end(h):
        links.wait(arrived_3[h], from3_buf.at[h])
        whole = totals[h].total()
        for t in range(tiles):
            feature_grad_ref[tile_rows(t), pl.ds(h * width, width)] = whole[t].T.astype(BF16)

    for h in feature_halves:
        links.wait(arrived_2[h], from2_buf.at[h])
    for a in node_halves:
        dense(a)
        ones[0][a].push()
        twos[0][0][a].push()
    for t in range(tiles):
        term = lax.dot_general(
            hidden_buf[t], grad_buf[t], (((1,), (1,)), ((), ())), preferred_element_type=F32
        ).reshape(term_buf.shape)
        if t == 0:
            term_buf[...] = term
        else:
            term_buf[...] += term
    weights = SumAll(
        links, here, term_buf, weight_grad_ref, term_relay, term_from, term_own, term_got
    )
    one_relay(0)
    one_wait(0, 1)
    two_push(0, 1, 3)
    weights.next()
    two_relay(0, 0)
    one_wait(0, 2)
    two_push(0, 2)
    two_relay(0, 1)
    weights.next()
    two_relay(0, 3)
    two_relay(0, 2)
    one_push(1)
    two_push(1, 0)
    weights.next()
    shared(0)
    tile_pass(grads[0], True)
    one_relay(1)
    one_wait(1, 1)
    two_push(1, 1, 3)
    weights.next()
    two_relay(1, 0)
    back_swap(0)
    one_wait(1, 2)
    two_push(1, 2)
    weights.next()
    back_push(0)
    two_relay(1, 1)
    two_relay(1, 3)
    weights.next()
    back_relay(0)
    two_relay(1, 2)
    weights.next()
    for t in range(tiles):
        out_ref[tile_rows(t), :] = value_buf[t].T.astype(BF16)
    weights.next()
    back_end(0)
    shared(1)
    tile_pass(grads[1], True)
    back_swap(1)
    weights.next()
    back_push(1)
    weights.next()
    back_relay(1)
    back_end(1)
    links.drain()


def copy_kernel(*refs):
    half = len(refs) // 2
    copies = [
        pltpu.make_async_copy(refs[i], refs[half + i], refs[-1].at[i]) for i in range(half)
    ]
    for copy in copies:
        copy.start()
    for copy in copies:
        copy.wait()


def shards(features, weight, adj_tiles, tile_rows, tile_cols, tile_count, cotangent):
    nodes, width = features.shape
    slots, tile = adj_tiles.shape[:2]
    n_row, n_col = lax.axis_size("row"), lax.axis_size("col")
    tiles, half, member = nodes // tile, width // 2, width // RING
    one = (half, tile)

    def vmem(*shape, dtype=BF16):
        return pltpu.VMEM(shape, dtype)

    anywhere = pl.BlockSpec(memory_space=pl.ANY)
    in_vmem = pl.BlockSpec(memory_space=pltpu.VMEM)
    results = pl.pallas_call(
        layer_kernel,
        out_shape=(
            jax.ShapeDtypeStruct((nodes, width), BF16),
            jax.ShapeDtypeStruct((RING, member, width), F32),
            jax.ShapeDtypeStruct((nodes, width), BF16),
        ),
        in_specs=[pl.BlockSpec(memory_space=pltpu.SMEM)] + [anywhere] * 6,
        out_specs=(in_vmem,) * 3,
        scratch_shapes=[
            vmem(nodes, width),
            vmem(width, width),
            vmem(slots, tile, tile),
            vmem(2, 1, slots, dtype=jnp.int32),
            vmem(nodes, width),
            vmem(8, 128, dtype=jnp.int32),
            pltpu.SMEM((8, 128), jnp.int32),
            vmem(n_row, tiles, *one),
            vmem(n_row, tiles, *one),
            vmem(slots + 1, *one),
            vmem(2, n_col, tiles, *one),
            vmem(2, RING, 2, 2, tiles // 4, *one),
            vmem(2, RING, 2, 2, tiles // 2, *one),
            vmem(2, 2, RING, tiles // 2, *one),
            vmem(2, 2, 2, tiles // 4, *one),
            vmem(2, 2, 2, tiles // 2, *one),
            vmem(tiles, width, tile, dtype=F32),
            vmem(tiles, width, tile),
            vmem(tiles, width, tile),
            vmem(tiles, width, tile, dtype=F32),
            vmem(n_col, tiles, *one),
            vmem(n_col, tiles, *one),
            vmem(RING, member, width, dtype=F32),
            vmem(2, member // 2, width, dtype=F32),
            vmem(2, member, width, dtype=F32),
            vmem(11, member, width, dtype=F32),
            vmem(5, member, width, dtype=F32),
            vmem(2, n_row, tiles, *one),
            vmem(2, RING, tiles, *one),
            vmem(2, RING, tiles, *one),
            vmem(2, 2, tiles // 2, *one),
            vmem(2, 2, tiles, *one),
            pltpu.SemaphoreType.DMA((7,)),
            pltpu.SemaphoreType.DMA((9,)),
            pltpu.SemaphoreType.DMA((65,)),
        ],
        compiler_params=pltpu.CompilerParams(
            vmem_limit_bytes=VMEM_BYTES, collective_id=0, has_side_effects=True
        ),
        name="layer",
    )(
        tile_count, features, weight, adj_tiles,
        tile_rows.reshape(1, slots), tile_cols.reshape(1, slots), cotangent,
    )
    out_features, weight_grad, feature_grad = pl.pallas_call(
        copy_kernel,
        out_shape=tuple(jax.ShapeDtypeStruct(r.shape, r.dtype) for r in results),
        in_specs=[anywhere] * 3,
        out_specs=(anywhere,) * 3,
        scratch_shapes=[pltpu.SemaphoreType.DMA((3,))],
        name="results",
    )(*results)
    return (out_features, weight_grad.reshape(width, width), feature_grad)


def solution(mesh):
    in_specs = (
        P(("row", "col"), None),
        P(),
        P(("row", "col"), None, None),
        P(("row", "col")),
        P(("row", "col")),
        P(("row", "col")),
        P(("row", "col"), None),
    )
    out_specs = (P(("row", "col"), None), P(), P(("row", "col"), None))
    return jax.shard_map(shards, mesh=mesh, in_specs=in_specs, out_specs=out_specs, check_vma=False)
```

```python
import jax
import jax.numpy as jnp
from jax import lax
from jax.experimental import pallas as pl
from jax.experimental.pallas import tpu as pltpu
from jax.sharding import PartitionSpec as P

MESH = pl.DeviceIdType.MESH
BF16, F32 = jnp.bfloat16, jnp.float32
VMEM_BYTES = 63 * 2**20
RING = 4
UNROLL = 8


class Links:
    def __init__(self, send_sem, recv_sem):
        self.send_sem, self.recv_sem = send_sem, recv_sem
        self.used, self.phases = 0, []

    def semaphore(self):
        self.used += 1
        return self.recv_sem.at[self.used - 1]

    def phase(self, ref):
        self.phases.append(ref)
        return len(self.phases) - 1

    def start(self, src, dst, device, arrived, phase):
        pltpu.make_async_remote_copy(
            src_ref=src,
            dst_ref=dst,
            send_sem=self.send_sem.at[phase],
            recv_sem=arrived,
            device_id=device,
            device_id_type=MESH,
        ).start()

    def wait(self, arrived, ref):
        pltpu.make_async_copy(ref, ref, arrived).wait()

    def drain(self):
        for at, ref in enumerate(self.phases):
            self.wait(self.send_sem.at[at], ref)


class Axis:
    def __init__(self, position, device_at):
        self.position = position
        self.up = device_at(lax.rem(position + 1, RING))
        self.down = device_at(lax.rem(position + 3, RING))
        odd = lax.rem(position, 2)
        self.pair = device_at(position + 1 - 2 * odd)
        self.other_pair = device_at(lax.rem(position + 3 + 2 * odd, RING))

    def at(self, offset):
        return lax.rem(self.position + offset, RING) if offset else self.position


class Place:
    def __init__(self):
        row, col = lax.axis_index("row"), lax.axis_index("col")
        self.row, self.col = row, col
        y, self.core = lax.div(row, 2), lax.rem(row, 2)
        x, z = lax.div(col, RING), lax.rem(col, RING)
        core = self.core
        self.y = Axis(y, lambda k: (k * 2 + core, col))
        self.x = Axis(x, lambda k: (row, k * RING + z))
        self.z = Axis(z, lambda k: (row, x * RING + k))
        self.sibling_row = row + 1 - 2 * core
        self.sibling = (self.sibling_row, col)

    def greet(self):
        barrier = pltpu.get_barrier_semaphore()
        others = [d for axis in (self.x, self.y, self.z) for d in (axis.up, axis.down)]
        others.append(self.sibling)
        for other in others:
            pl.semaphore_signal(barrier, inc=1, device_id=other, device_id_type=MESH)
        return lambda: pl.semaphore_wait(barrier, len(others))


def add_to(ref, value):
    ref[...] = (ref[...].astype(F32) + value.astype(F32)).astype(ref.dtype)


class Sum4:
    def __init__(self, links, axis, part, relays, blocks, passing, arrived, phase):
        self.links, self.axis, self.part = links, axis, part
        self.relay_up, self.relay_down = relays.at[0], relays.at[1]
        self.from_down, self.from_up = blocks.at[0], blocks.at[1]
        self.passing, self.arrived, self.phase = passing, arrived, phase
        half = relays.shape[1]
        self.low, self.high = pl.ds(0, half), pl.ds(half, half)

    def send(self, src, dst, device, arrived):
        self.links.start(src, dst, device, arrived, self.phase)

    def push_far(self):
        far = self.part(2)
        self.send(far.at[self.low], self.relay_up, self.axis.up, self.passing)
        self.send(far.at[self.high], self.relay_down, self.axis.down, self.passing)

    def push_up(self):
        near = self.part(1).at[self.high]
        self.send(near, self.from_down.at[self.high], self.axis.up, self.arrived)

    def push_down(self):
        near = self.part(3).at[self.low]
        self.send(near, self.from_up.at[self.low], self.axis.down, self.arrived)

    def push(self):
        self.push_far()
        self.push_up()
        self.push_down()

    def relay(self):
        add_to(self.relay_up, self.part(1)[self.low])
        self.send(self.relay_up, self.from_down.at[self.low], self.axis.up, self.arrived)
        add_to(self.relay_down, self.part(3)[self.high])
        self.send(self.relay_down, self.from_up.at[self.high], self.axis.down, self.arrived)

    def total(self):
        return (
            self.part(0)[...].astype(F32)
            + self.from_down[...].astype(F32)
            + self.from_up[...].astype(F32)
        )


class Share4:
    def __init__(self, links, axis, slot, half, first, near, far, phase):
        self.links, self.axis, self.slot = links, axis, slot
        self.first, self.near, self.far, self.phase = first, near, far, phase
        self.low, self.high = pl.ds(0, half), pl.ds(half, half)

    def send(self, k, rows, device, arrived):
        ref = self.slot(k).at[rows]
        self.links.start(ref, ref, device, arrived, self.phase)

    def push(self):
        self.send(0, self.low, self.axis.up, self.first)
        self.send(0, self.high, self.axis.down, self.first)
        self.send(0, self.high, self.axis.up, self.near)
        self.send(0, self.low, self.axis.down, self.near)

    def relay(self):
        self.send(3, self.low, self.axis.up, self.far)
        self.send(1, self.high, self.axis.down, self.far)


class SumAll:
    def __init__(self, links, here, term, result, relay, came, own, got):
        x = here.x
        self.links, self.own, self.got, self.relays, self.came = links, own, got, relay, came
        self.result = result
        phase = links.phase(own)
        passing, arrived, self.first, self.rest = (links.semaphore() for _ in range(4))
        self.ring = Sum4(links, x, lambda k: term.at[x.at(k)], relay, came, passing, arrived, phase)
        self.share = Share4(
            links, x, lambda k: result.at[x.at(k)], result.shape[1] // 2,
            self.first, self.rest, self.rest, phase,
        )
        self.slot = result.at[x.position]
        pairs = (here.z.pair, here.z.other_pair, here.y.pair, here.y.other_pair, here.sibling)
        self.steps = self.run(pairs)

    def run(self, pairs):
        links, ring, share = self.links, self.ring, self.share
        ring.push()
        yield
        links.wait(ring.passing, self.relays)
        ring.relay()
        yield
        links.wait(ring.arrived, self.came)
        total = ring.total()
        for at, pair in enumerate(pairs):
            self.own[at] = total
            arrived = links.semaphore()
            links.start(self.own.at[at], self.got.at[at], pair, arrived, ring.phase)
            yield
            links.wait(arrived, self.got.at[at])
            total = self.own[at] + self.got[at]
        self.slot[...] = total
        share.push()
        yield
        links.wait(self.first, self.result.at[0])
        share.relay()
        yield
        links.wait(self.rest, self.result.at[pl.ds(0, 2)])

    def next(self):
        next(self.steps, None)


def activation(value):
    root = 0.7978845608028654
    square = value * value
    t = jnp.tanh(root * (value + 0.044715 * (value * square)))
    half = 0.5 * (1.0 + t)
    slope = half + (0.5 * value) * (1.0 - t * t) * (root * (1.0 + 3.0 * 0.044715 * square))
    return value * half, slope


def spread(row):
    wide = jnp.broadcast_to(row, (row.shape[1], row.shape[1]))
    return wide, wide.T


def slot_order(key, source, count, empty):
    lanes = key.shape[1]
    lane = lax.broadcasted_iota(jnp.int32, (lanes, lanes), 1)
    sub = lax.broadcasted_iota(jnp.int32, (lanes, lanes), 0)
    at = lax.broadcasted_iota(jnp.int32, (1, lanes), 1)
    key = jnp.where(at < count, key, 2 * lanes)

    def over(mask, value):
        return jnp.sum(jnp.where(mask, value, 0), axis=0, keepdims=True)

    unique_row, unique_col = spread(key * lanes + at)
    _, rank = spread(over(unique_col < unique_row, 1))
    _, key_col = spread(key)
    _, source_col = spread(source)
    hit = rank == lane
    slot, source, sorted_key = over(hit, sub), over(hit, source_col), over(hit, key_col)
    same = over((rank == lane - 1) & (key_col == sorted_key), 1)
    last = jnp.where(over(key_col == lane, 1) > 0, over(key_col <= lane, 1) - 1, empty)
    return slot, source, same, last


def layer_kernel(
    count_ref, features_ref, weight_ref, adj_ref, rows_ref, cols_ref, cot_ref,
    out_ref, weight_grad_ref, feature_grad_ref,
    x_buf, weight_buf, adj, ids_buf, cot_buf, table_buf, table,
    group_0, group_1, running, parts, relay_buf, from_buf, part2_buf, relay2_buf, from2_buf,
    cot_t, hidden_buf, grad_buf, value_buf, grads_0, grads_1,
    term_buf, term_relay, term_from, term_own, term_got,
    sums, own_buf, twin_buf, relay3_buf, from3_buf, local_sem, send_sem, recv_sem,
):
    here = Place()
    group, grads = (group_0, group_1), (grads_0, grads_1)
    tiles, width, tile = parts.shape[2], parts.shape[3], parts.shape[4]
    slots = adj.shape[0]
    links = Links(send_sem, recv_sem)
    loads = [
        pltpu.make_async_copy(src, dst, local_sem.at[i])
        for i, (src, dst) in enumerate(
            (
                (features_ref, x_buf),
                (rows_ref, ids_buf.at[0]),
                (cols_ref, ids_buf.at[1]),
                (adj_ref, adj),
                (weight_ref, weight_buf),
                (cot_ref, cot_buf),
            )
        )
    ]
    for load in loads:
        load.start()
    met = here.greet()
    feature_halves = node_halves = (0, 1)

    def tile_rows(t):
        return pl.ds(t * tile, tile)

    def row_slot(h, k):
        return group[h].at[here.y.at(k) * 2 + here.core]

    def share_row(h):
        first, near, far = (links.semaphore() for _ in range(3))
        phase = links.phase(parts.at[h, pl.ds(0, 7)])
        return Share4(
            links, here.y, lambda k: row_slot(h, k), tiles // 2, first, near, far, phase
        )

    shares = [share_row(h) for h in feature_halves]
    twins = [links.semaphore() for _ in feature_halves]
    low, high = shares[0].low, shares[0].high

    def across(h, k, rows):
        ref = row_slot(h, k).at[rows]
        links.start(ref, ref, here.sibling, twins[h], shares[h].phase)

    def gather_load(h):
        for t in range(tiles):
            block = x_buf[tile_rows(t), pl.ds(h * width, width)]
            group[h][here.row, t] = block.astype(F32).T.astype(BF16)

    def gather_push(h):
        shares[h].push()
        across(h, 0, low)
        across(h, 0, high)

    def gather_relay(h):
        links.wait(shares[h].first, group[h].at[0])
        shares[h].relay()
        across(h, 3, low)
        across(h, 1, high)

    def gather_near(h):
        links.wait(shares[h].near, group[h].at[0])
        across(h, 3, high)
        across(h, 1, low)

    def gather_far(h):
        links.wait(shares[h].far, group[h].at[0])
        across(h, 2, low)
        across(h, 2, high)

    def gather_done(h):
        links.wait(twins[h], group[h].at[pl.ds(0, 4)])

    loads[0].wait()
    gather_load(0)
    met()
    gather_push(0)
    gather_load(1)

    loads[1].wait()
    loads[2].wait()
    table_buf[...] = jnp.zeros_like(table_buf)
    for i in (0, 1):
        table_buf[i : i + 1, 0:slots] = ids_buf[i]
    by_row, by_col = table_buf[0:1, :], table_buf[1:2, :]
    count = count_ref[0]
    order = slot_order(by_row, by_col, count, slots) + slot_order(by_col, by_row, count, slots)
    for i, line in enumerate(order):
        table_buf[i : i + 1, :] = line
    to_scalars = pltpu.make_async_copy(table_buf, table, local_sem.at[6])
    to_scalars.start()
    running[slots] = jnp.zeros(running.shape[1:], BF16)

    def tile_pass(source, backward):
        base = 4 if backward else 0
        contract = ((1,), (0,)) if backward else ((1,), (1,))

        def step(block, acc):
            products = []
            for k in range(UNROLL):
                at = block * UNROLL + k
                node = table[base + 1, at]
                products.append(
                    lax.dot_general(
                        source[lax.div(node, tiles), lax.rem(node, tiles)],
                        adj[table[base, at]],
                        (contract, ((), ())),
                        preferred_element_type=F32,
                    )
                )
            for k in range(UNROLL):
                at = block * UNROLL + k
                acc = acc * table[base + 2, at].astype(F32) + products[k]
                running[at] = acc.astype(BF16)
            return acc

        lax.fori_loop(0, slots // UNROLL, step, jnp.zeros((width, tile), F32))

    def pick(target, base, block):
        for t in range(tiles):
            target[block, t] = running[table[base + 3, block * tiles + t]]

    firsts, seconds = (here.z, here.x), (here.x, here.z)
    node_slices = [pl.ds(a * (tiles // 2), tiles // 2) for a in node_halves]

    def col_of(a, first, second):
        return second * RING + first if a == 0 else first * RING + second

    passing, arrived = (
        [[links.semaphore() for _ in range(RING)] for _ in feature_halves] for _ in range(2)
    )
    passing_2, arrived_2 = ([links.semaphore() for _ in feature_halves] for _ in range(2))
    phases = [links.phase(parts.at[h, pl.ds(0, 15)]) for h in feature_halves]

    def sum_first(h, a, delta):
        first, second = firsts[a], seconds[a]

        def part(k):
            return parts.at[h, col_of(a, first.at(k), second.at(delta)), node_slices[a]]

        return Sum4(
            links, first, part, relay_buf.at[h, delta, a], from_buf.at[h, delta, a],
            passing[h][delta], arrived[h][delta], phases[h],
        )

    def sum_second(h, a):
        return Sum4(
            links, seconds[a], lambda k: part2_buf.at[h, a, k], relay2_buf.at[h, a],
            from2_buf.at[h, a], passing_2[h], arrived_2[h], phases[h],
        )

    first_sums = [
        [[sum_first(h, a, d) for d in range(RING)] for a in node_halves] for h in feature_halves
    ]
    last_sums = [[sum_second(h, a) for a in node_halves] for h in feature_halves]

    def push_first(h, d):
        for a in node_halves:
            first_sums[h][a][d].push()

    def relay_first(h, d):
        links.wait(passing[h][d], relay_buf.at[h, d])
        for a in node_halves:
            first_sums[h][a][d].relay()

    def wait_first(h, d):
        links.wait(arrived[h][d], from_buf.at[h, d])

    def done_first(h, a, d):
        part2_buf[h, a, d] = first_sums[h][a][d].total().astype(BF16)

    def scatter_start(h):
        lax.fori_loop(0, RING * RING, lambda b, _: (pick(parts.at[h], 0, b), 0)[1], 0)
        for d in (2, 1, 3, 0):
            push_first(h, d)

    def scatter_relay(h):
        for d in (2, 1, 3, 0):
            relay_first(h, d)

    def scatter_far(h):
        wait_first(h, 2)
        for a in node_halves:
            done_first(h, a, 2)
            last_sums[h][a].push_far()

    def scatter_near(h):
        wait_first(h, 1)
        for a in node_halves:
            done_first(h, a, 1)
            last_sums[h][a].push_up()
        wait_first(h, 3)
        for a in node_halves:
            done_first(h, a, 3)
            last_sums[h][a].push_down()

    def scatter_end(h):
        links.wait(passing_2[h], relay2_buf.at[h])
        for a in node_halves:
            last_sums[h][a].relay()
        wait_first(h, 0)
        for a in node_halves:
            done_first(h, a, 0)

    gather_relay(0)
    gather_push(1)
    gather_near(0)
    gather_far(0)
    gather_relay(1)
    gather_done(0)
    to_scalars.wait()
    loads[3].wait()
    tile_pass(group[0], False)
    scatter_start(0)
    gather_near(1)
    gather_far(1)
    gather_done(1)
    tile_pass(group[1], False)
    scatter_start(1)
    scatter_relay(0)
    loads[4].wait()
    loads[5].wait()
    for t in range(tiles):
        cot_t[t] = cot_buf[tile_rows(t), :].astype(F32).T
    scatter_relay(1)
    scatter_far(0)
    scatter_far(1)
    scatter_near(0)
    scatter_near(1)
    scatter_end(0)
    scatter_end(1)

    weight = weight_buf[...]

    def dense(a):
        whole = [last_sums[h][a].total().astype(BF16) for h in feature_halves]
        for i in range(tiles // 2):
            t = a * (tiles // 2) + i
            hidden = jnp.concatenate([whole[0][i], whole[1][i]], axis=0)
            pre_act = lax.dot_general(
                weight, hidden, (((0,), (0,)), ((), ())), preferred_element_type=F32
            )
            value, slope = activation(pre_act)
            pre_grad = (cot_t[t] * slope).astype(BF16)
            own = jnp.dot(weight, pre_grad, preferred_element_type=F32).astype(BF16)
            for h in feature_halves:
                grads[h][here.col, t] = own[h * width : (h + 1) * width]
            value_buf[t] = value
            hidden_buf[t] = hidden
            grad_buf[t] = pre_grad

    share_phases = [links.phase(parts.at[h, pl.ds(0, 15)]) for h in feature_halves]
    one_sems = [[links.semaphore() for _ in range(3)] for _ in feature_halves]
    two_sems = [[links.semaphore() for _ in range(RING)] for _ in feature_halves]
    rest_sems = [links.semaphore() for _ in feature_halves]

    def share_first(h, a):
        first, second = seconds[a], firsts[a]
        return Share4(
            links,
            first,
            lambda k: grads[h].at[col_of(1 - a, first.at(k), second.position), node_slices[a]],
            tiles // 4,
            *one_sems[h],
            share_phases[h],
        )

    def share_second(h, a, delta):
        first, second = seconds[a], firsts[a]
        return Share4(
            links,
            second,
            lambda k: grads[h].at[col_of(1 - a, first.at(delta), second.at(k)), node_slices[a]],
            tiles // 4,
            two_sems[h][delta],
            rest_sems[h],
            rest_sems[h],
            share_phases[h],
        )

    ones = [[share_first(h, a) for a in node_halves] for h in feature_halves]
    twos = [
        [[share_second(h, a, d) for a in node_halves] for d in range(RING)] for h in feature_halves
    ]

    def one_push(h):
        for share in ones[h]:
            share.push()

    def one_wait(h, which):
        links.wait(one_sems[h][which], grads[h].at[0])

    def one_relay(h):
        one_wait(h, 0)
        for share in ones[h]:
            share.relay()

    def two_push(h, *offsets):
        for d in offsets:
            for share in twos[h][d]:
                share.push()

    def two_relay(h, *offsets):
        for d in offsets:
            links.wait(two_sems[h][d], grads[h].at[0])
            for share in twos[h][d]:
                share.relay()

    def shared(h):
        links.wait(rest_sems[h], grads[h].at[pl.ds(0, 8)])

    back_phases = [links.phase(parts.at[h, pl.ds(0, 7)]) for h in feature_halves]
    passing_3, arrived_3 = ([links.semaphore() for _ in feature_halves] for _ in range(2))
    swapped = [[links.semaphore() for _ in range(RING)] for _ in feature_halves]
    totals = [
        Sum4(
            links, here.y, lambda k, h=h: own_buf.at[h, k], relay3_buf.at[h], from3_buf.at[h],
            passing_3[h], arrived_3[h], back_phases[h],
        )
        for h in feature_halves
    ]
    near_order = (2, 1, 3, 0)

    def block(h, k, core):
        return sums.at[h, here.y.at(k) * 2 + core]

    def back_swap(h):
        lax.fori_loop(0, RING * 2, lambda b, _: (pick(sums.at[h], 4, b), 0)[1], 0)
        for k in near_order:
            links.start(
                block(h, k, 1 - here.core), twin_buf.at[h, k], here.sibling, swapped[h][k],
                back_phases[h],
            )

    def back_push(h):
        pushes = {2: totals[h].push_far, 1: totals[h].push_up, 3: totals[h].push_down}
        for k in near_order:
            links.wait(swapped[h][k], twin_buf.at[h, k])
            own = block(h, k, here.core)[...].astype(F32) + twin_buf[h, k].astype(F32)
            own_buf[h, k] = own.astype(BF16)
            if k in pushes:
                pushes[k]()

    def back_relay(h):
        links.wait(passing_3[h], relay3_buf.at[h])
        totals[h].relay()

    def back_end(h):
        links.wait(arrived_3[h], from3_buf.at[h])
        whole = totals[h].total()
        for t in range(tiles):
            feature_grad_ref[tile_rows(t), pl.ds(h * width, width)] = whole[t].T.astype(BF16)

    for h in feature_halves:
        links.wait(arrived_2[h], from2_buf.at[h])
    for a in node_halves:
        dense(a)
        ones[0][a].push()
        twos[0][0][a].push()
    for t in range(tiles):
        term = lax.dot_general(
            hidden_buf[t], grad_buf[t], (((1,), (1,)), ((), ())), preferred_element_type=F32
        ).reshape(term_buf.shape)
        if t == 0:
            term_buf[...] = term
        else:
            term_buf[...] += term
    weights = SumAll(
        links, here, term_buf, weight_grad_ref, term_relay, term_from, term_own, term_got
    )
    one_relay(0)
    one_wait(0, 1)
    two_push(0, 1, 3)
    weights.next()
    two_relay(0, 0)
    one_wait(0, 2)
    two_push(0, 2)
    two_relay(0, 1)
    weights.next()
    two_relay(0, 3)
    two_relay(0, 2)
    one_push(1)
    two_push(1, 0)
    weights.next()
    shared(0)
    tile_pass(grads[0], True)
    one_relay(1)
    one_wait(1, 1)
    two_push(1, 1, 3)
    weights.next()
    two_relay(1, 0)
    back_swap(0)
    one_wait(1, 2)
    two_push(1, 2)
    weights.next()
    back_push(0)
    two_relay(1, 1)
    two_relay(1, 3)
    weights.next()
    back_relay(0)
    two_relay(1, 2)
    weights.next()
    for t in range(tiles):
        out_ref[tile_rows(t), :] = value_buf[t].T.astype(BF16)
    weights.next()
    back_end(0)
    shared(1)
    tile_pass(grads[1], True)
    back_swap(1)
    weights.next()
    back_push(1)
    weights.next()
    back_relay(1)
    back_end(1)
    links.drain()


def copy_kernel(*refs):
    count = (len(refs) - 2) // 3
    sources, targets, held = (refs[i * count : (i + 1) * count] for i in range(3))
    came, left = refs[-2:]
    into = [pltpu.make_async_copy(sources[i], held[i], came.at[i]) for i in range(count)]
    out = [pltpu.make_async_copy(held[i], targets[i], left.at[i]) for i in range(count)]
    for copy in into:
        copy.start()
    for first, second in zip(into, out):
        first.wait()
        second.start()
    for copy in out:
        copy.wait()


def shards(features, weight, adj_tiles, tile_rows, tile_cols, tile_count, cotangent):
    nodes, width = features.shape
    slots, tile = adj_tiles.shape[:2]
    n_row, n_col = lax.axis_size("row"), lax.axis_size("col")
    tiles, half, member = nodes // tile, width // 2, width // RING
    one = (half, tile)

    def vmem(*shape, dtype=BF16):
        return pltpu.VMEM(shape, dtype)

    anywhere = pl.BlockSpec(memory_space=pl.ANY)
    in_vmem = pl.BlockSpec(memory_space=pltpu.VMEM)
    results = pl.pallas_call(
        layer_kernel,
        out_shape=(
            jax.ShapeDtypeStruct((nodes, width), BF16),
            jax.ShapeDtypeStruct((RING, member, width), F32),
            jax.ShapeDtypeStruct((nodes, width), BF16),
        ),
        in_specs=[pl.BlockSpec(memory_space=pltpu.SMEM)] + [anywhere] * 6,
        out_specs=(in_vmem,) * 3,
        scratch_shapes=[
            vmem(nodes, width),
            vmem(width, width),
            vmem(slots, tile, tile),
            vmem(2, 1, slots, dtype=jnp.int32),
            vmem(nodes, width),
            vmem(8, 128, dtype=jnp.int32),
            pltpu.SMEM((8, 128), jnp.int32),
            vmem(n_row, tiles, *one),
            vmem(n_row, tiles, *one),
            vmem(slots + 1, *one),
            vmem(2, n_col, tiles, *one),
            vmem(2, RING, 2, 2, tiles // 4, *one),
            vmem(2, RING, 2, 2, tiles // 2, *one),
            vmem(2, 2, RING, tiles // 2, *one),
            vmem(2, 2, 2, tiles // 4, *one),
            vmem(2, 2, 2, tiles // 2, *one),
            vmem(tiles, width, tile, dtype=F32),
            vmem(tiles, width, tile),
            vmem(tiles, width, tile),
            vmem(tiles, width, tile, dtype=F32),
            vmem(n_col, tiles, *one),
            vmem(n_col, tiles, *one),
            vmem(RING, member, width, dtype=F32),
            vmem(2, member // 2, width, dtype=F32),
            vmem(2, member, width, dtype=F32),
            vmem(11, member, width, dtype=F32),
            vmem(5, member, width, dtype=F32),
            vmem(2, n_row, tiles, *one),
            vmem(2, RING, tiles, *one),
            vmem(2, RING, tiles, *one),
            vmem(2, 2, tiles // 2, *one),
            vmem(2, 2, tiles, *one),
            pltpu.SemaphoreType.DMA((7,)),
            pltpu.SemaphoreType.DMA((9,)),
            pltpu.SemaphoreType.DMA((65,)),
        ],
        compiler_params=pltpu.CompilerParams(
            vmem_limit_bytes=VMEM_BYTES, collective_id=0, has_side_effects=True
        ),
        name="layer",
    )(
        tile_count, features, weight, adj_tiles,
        tile_rows.reshape(1, slots), tile_cols.reshape(1, slots), cotangent,
    )
    out_features, weight_grad, feature_grad = pl.pallas_call(
        copy_kernel,
        out_shape=tuple(jax.ShapeDtypeStruct(r.shape, r.dtype) for r in results),
        in_specs=[anywhere] * 3,
        out_specs=(anywhere,) * 3,
        scratch_shapes=[pltpu.VMEM(r.shape, r.dtype) for r in results]
        + [pltpu.SemaphoreType.DMA((3,))] * 2,
        compiler_params=pltpu.CompilerParams(vmem_limit_bytes=VMEM_BYTES),
        name="results",
    )(*results)
    return (out_features, weight_grad.reshape(width, width), feature_grad)


def solution(mesh):
    in_specs = (
        P(("row", "col"), None),
        P(),
        P(("row", "col"), None, None),
        P(("row", "col")),
        P(("row", "col")),
        P(("row", "col")),
        P(("row", "col"), None),
    )
    out_specs = (P(("row", "col"), None), P(), P(("row", "col"), None))
    return jax.shard_map(shards, mesh=mesh, in_specs=in_specs, out_specs=out_specs, check_vma=False)
```

```python
import jax
import jax.numpy as jnp
from jax import lax
from jax.experimental import pallas as pl
from jax.experimental.pallas import tpu as pltpu
from jax.sharding import PartitionSpec as P

MESH = pl.DeviceIdType.MESH
BF16, F32 = jnp.bfloat16, jnp.float32
VMEM_BYTES = 63 * 2**20
RING = 4
UNROLL = 8


class Links:
    def __init__(self, send_sem, recv_sem):
        self.send_sem, self.recv_sem = send_sem, recv_sem
        self.used, self.phases = 0, []

    def semaphore(self):
        self.used += 1
        return self.recv_sem.at[self.used - 1]

    def phase(self, ref):
        self.phases.append(ref)
        return len(self.phases) - 1

    def start(self, src, dst, device, arrived, phase):
        pltpu.make_async_remote_copy(
            src_ref=src,
            dst_ref=dst,
            send_sem=self.send_sem.at[phase],
            recv_sem=arrived,
            device_id=device,
            device_id_type=MESH,
        ).start()

    def wait(self, arrived, ref):
        pltpu.make_async_copy(ref, ref, arrived).wait()

    def drain(self):
        for at, ref in enumerate(self.phases):
            self.wait(self.send_sem.at[at], ref)


class Axis:
    def __init__(self, position, device_at):
        self.position = position
        self.up = device_at(lax.rem(position + 1, RING))
        self.down = device_at(lax.rem(position + 3, RING))
        odd = lax.rem(position, 2)
        self.pair = device_at(position + 1 - 2 * odd)
        self.other_pair = device_at(lax.rem(position + 3 + 2 * odd, RING))

    def at(self, offset):
        return lax.rem(self.position + offset, RING) if offset else self.position


class Place:
    def __init__(self):
        row, col = lax.axis_index("row"), lax.axis_index("col")
        self.row, self.col = row, col
        y, self.core = lax.div(row, 2), lax.rem(row, 2)
        x, z = lax.div(col, RING), lax.rem(col, RING)
        core = self.core
        self.y = Axis(y, lambda k: (k * 2 + core, col))
        self.x = Axis(x, lambda k: (row, k * RING + z))
        self.z = Axis(z, lambda k: (row, x * RING + k))
        self.sibling_row = row + 1 - 2 * core
        self.sibling = (self.sibling_row, col)

    def greet(self):
        barrier = pltpu.get_barrier_semaphore()
        others = [d for axis in (self.x, self.y, self.z) for d in (axis.up, axis.down)]
        others.append(self.sibling)
        for other in others:
            pl.semaphore_signal(barrier, inc=1, device_id=other, device_id_type=MESH)
        return lambda: pl.semaphore_wait(barrier, len(others))


def add_to(ref, value):
    ref[...] = (ref[...].astype(F32) + value.astype(F32)).astype(ref.dtype)


class Sum4:
    def __init__(self, links, axis, part, relays, blocks, passing, arrived, phase):
        self.links, self.axis, self.part = links, axis, part
        self.relay_up, self.relay_down = relays.at[0], relays.at[1]
        self.from_down, self.from_up = blocks.at[0], blocks.at[1]
        self.passing, self.arrived, self.phase = passing, arrived, phase
        half = relays.shape[1]
        self.low, self.high = pl.ds(0, half), pl.ds(half, half)

    def send(self, src, dst, device, arrived):
        self.links.start(src, dst, device, arrived, self.phase)

    def push_far(self):
        far = self.part(2)
        self.send(far.at[self.low], self.relay_up, self.axis.up, self.passing)
        self.send(far.at[self.high], self.relay_down, self.axis.down, self.passing)

    def push_up(self):
        near = self.part(1).at[self.high]
        self.send(near, self.from_down.at[self.high], self.axis.up, self.arrived)

    def push_down(self):
        near = self.part(3).at[self.low]
        self.send(near, self.from_up.at[self.low], self.axis.down, self.arrived)

    def push(self):
        self.push_far()
        self.push_up()
        self.push_down()

    def relay(self):
        add_to(self.relay_up, self.part(1)[self.low])
        self.send(self.relay_up, self.from_down.at[self.low], self.axis.up, self.arrived)
        add_to(self.relay_down, self.part(3)[self.high])
        self.send(self.relay_down, self.from_up.at[self.high], self.axis.down, self.arrived)

    def total(self):
        return (
            self.part(0)[...].astype(F32)
            + self.from_down[...].astype(F32)
            + self.from_up[...].astype(F32)
        )


class Share4:
    def __init__(self, links, axis, slot, half, first, near, far, phase):
        self.links, self.axis, self.slot = links, axis, slot
        self.first, self.near, self.far, self.phase = first, near, far, phase
        self.low, self.high = pl.ds(0, half), pl.ds(half, half)

    def send(self, k, rows, device, arrived):
        ref = self.slot(k).at[rows]
        self.links.start(ref, ref, device, arrived, self.phase)

    def push(self):
        self.send(0, self.low, self.axis.up, self.first)
        self.send(0, self.high, self.axis.down, self.first)
        self.send(0, self.high, self.axis.up, self.near)
        self.send(0, self.low, self.axis.down, self.near)

    def relay(self):
        self.send(3, self.low, self.axis.up, self.far)
        self.send(1, self.high, self.axis.down, self.far)


class SumAll:
    def __init__(self, links, here, term, result, relay, came, own, got):
        y = here.y
        self.links, self.own, self.got, self.relays, self.came = links, own, got, relay, came
        self.result = result
        phase = links.phase(own)
        passing, arrived, self.first, self.rest = (links.semaphore() for _ in range(4))
        self.ring = Sum4(links, y, lambda k: term.at[y.at(k)], relay, came, passing, arrived, phase)
        self.share = Share4(
            links, y, lambda k: result.at[y.at(k)], result.shape[1] // 2,
            self.first, self.rest, self.rest, phase,
        )
        self.slot = result.at[y.position]
        pairs = (here.sibling, here.x.pair, here.z.pair, here.x.other_pair, here.z.other_pair)
        self.steps = self.run(pairs)

    def run(self, pairs):
        links, ring, share = self.links, self.ring, self.share
        ring.push()
        yield
        links.wait(ring.passing, self.relays)
        ring.relay()
        yield
        links.wait(ring.arrived, self.came)
        total = ring.total()
        for at, pair in enumerate(pairs):
            self.own[at] = total
            arrived = links.semaphore()
            links.start(self.own.at[at], self.got.at[at], pair, arrived, ring.phase)
            yield
            links.wait(arrived, self.got.at[at])
            total = self.own[at] + self.got[at]
        self.slot[...] = total
        share.push()
        yield
        links.wait(self.first, self.result.at[0])
        share.relay()
        yield
        links.wait(self.rest, self.result.at[pl.ds(0, 2)])

    def next(self):
        next(self.steps, None)


def activation(value):
    root = 0.7978845608028654
    square = value * value
    t = jnp.tanh(root * (value + 0.044715 * (value * square)))
    half = 0.5 * (1.0 + t)
    slope = half + (0.5 * value) * (1.0 - t * t) * (root * (1.0 + 3.0 * 0.044715 * square))
    return value * half, slope


def spread(row):
    wide = jnp.broadcast_to(row, (row.shape[1], row.shape[1]))
    return wide, wide.T


def slot_order(key, source, count, empty):
    lanes = key.shape[1]
    lane = lax.broadcasted_iota(jnp.int32, (lanes, lanes), 1)
    sub = lax.broadcasted_iota(jnp.int32, (lanes, lanes), 0)
    at = lax.broadcasted_iota(jnp.int32, (1, lanes), 1)
    key = jnp.where(at < count, key, 2 * lanes)

    def over(mask, value):
        return jnp.sum(jnp.where(mask, value, 0), axis=0, keepdims=True)

    unique_row, unique_col = spread(key * lanes + at)
    _, rank = spread(over(unique_col < unique_row, 1))
    _, key_col = spread(key)
    _, source_col = spread(source)
    hit = rank == lane
    slot, source, sorted_key = over(hit, sub), over(hit, source_col), over(hit, key_col)
    same = over((rank == lane - 1) & (key_col == sorted_key), 1)
    last = jnp.where(over(key_col == lane, 1) > 0, over(key_col <= lane, 1) - 1, empty)
    return slot, source, same, last


def layer_kernel(
    count_ref, features_ref, weight_ref, adj_ref, rows_ref, cols_ref, cot_ref,
    out_ref, weight_grad_ref, feature_grad_ref,
    x_buf, weight_buf, adj, ids_buf, cot_buf, table_buf, table,
    group_0, group_1, running, parts, relay_buf, from_buf, part2_buf, relay2_buf, from2_buf,
    cot_t, hidden_buf, grad_buf, value_buf, grads_0, grads_1,
    term_buf, term_relay, term_from, term_own, term_got,
    sums, own_buf, twin_buf, relay3_buf, from3_buf,
    out_buf, weight_grad, feature_grad, count_buf, local_sem, send_sem, recv_sem,
):
    here = Place()
    group, grads = (group_0, group_1), (grads_0, grads_1)
    tiles, width, tile = parts.shape[2], parts.shape[3], parts.shape[4]
    slots = adj.shape[0]
    links = Links(send_sem, recv_sem)
    loads = [
        pltpu.make_async_copy(src, dst, local_sem.at[i])
        for i, (src, dst) in enumerate(
            (
                (features_ref, x_buf),
                (rows_ref, ids_buf.at[0]),
                (cols_ref, ids_buf.at[1]),
                (adj_ref, adj),
                (weight_ref, weight_buf),
                (cot_ref, cot_buf),
                (count_ref, count_buf),
            )
        )
    ]
    for load in loads:
        load.start()
    met = here.greet()
    feature_halves = node_halves = (0, 1)

    def tile_rows(t):
        return pl.ds(t * tile, tile)

    def row_slot(h, k):
        return group[h].at[here.y.at(k) * 2 + here.core]

    def share_row(h):
        first, near, far = (links.semaphore() for _ in range(3))
        phase = links.phase(parts.at[h, pl.ds(0, 7)])
        return Share4(
            links, here.y, lambda k: row_slot(h, k), tiles // 2, first, near, far, phase
        )

    shares = [share_row(h) for h in feature_halves]
    twins = [links.semaphore() for _ in feature_halves]
    low, high = shares[0].low, shares[0].high

    def across(h, k, rows):
        ref = row_slot(h, k).at[rows]
        links.start(ref, ref, here.sibling, twins[h], shares[h].phase)

    def gather_load(h):
        for t in range(tiles):
            block = x_buf[tile_rows(t), pl.ds(h * width, width)]
            group[h][here.row, t] = block.astype(F32).T.astype(BF16)

    def gather_push(h):
        shares[h].push()
        across(h, 0, low)
        across(h, 0, high)

    def gather_relay(h):
        links.wait(shares[h].first, group[h].at[0])
        shares[h].relay()
        across(h, 3, low)
        across(h, 1, high)

    def gather_near(h):
        links.wait(shares[h].near, group[h].at[0])
        across(h, 3, high)
        across(h, 1, low)

    def gather_far(h):
        links.wait(shares[h].far, group[h].at[0])
        across(h, 2, low)
        across(h, 2, high)

    def gather_done(h):
        links.wait(twins[h], group[h].at[pl.ds(0, 4)])

    loads[0].wait()
    gather_load(0)
    met()
    gather_push(0)
    gather_load(1)

    loads[1].wait()
    loads[2].wait()
    table_buf[...] = jnp.zeros_like(table_buf)
    for i in (0, 1):
        table_buf[i : i + 1, 0:slots] = ids_buf[i]
    by_row, by_col = table_buf[0:1, :], table_buf[1:2, :]
    loads[6].wait()
    count = count_buf[0]
    order = slot_order(by_row, by_col, count, slots) + slot_order(by_col, by_row, count, slots)
    for i, line in enumerate(order):
        table_buf[i : i + 1, :] = line
    to_scalars = pltpu.make_async_copy(table_buf, table, local_sem.at[7])
    to_scalars.start()
    running[slots] = jnp.zeros(running.shape[1:], BF16)

    def tile_pass(source, backward):
        base = 4 if backward else 0
        contract = ((1,), (0,)) if backward else ((1,), (1,))

        def step(block, acc):
            products = []
            for k in range(UNROLL):
                at = block * UNROLL + k
                node = table[base + 1, at]
                products.append(
                    lax.dot_general(
                        source[lax.div(node, tiles), lax.rem(node, tiles)],
                        adj[table[base, at]],
                        (contract, ((), ())),
                        preferred_element_type=F32,
                    )
                )
            for k in range(UNROLL):
                at = block * UNROLL + k
                acc = acc * table[base + 2, at].astype(F32) + products[k]
                running[at] = acc.astype(BF16)
            return acc

        lax.fori_loop(0, slots // UNROLL, step, jnp.zeros((width, tile), F32))

    def pick(target, base, block):
        picked = [running[table[base + 3, block * tiles + t]] for t in range(tiles)]
        for t in range(tiles):
            target[block, t] = picked[t]

    firsts, seconds = (here.z, here.x), (here.x, here.z)
    node_slices = [pl.ds(a * (tiles // 2), tiles // 2) for a in node_halves]

    def col_of(a, first, second):
        return second * RING + first if a == 0 else first * RING + second

    passing, arrived = (
        [[links.semaphore() for _ in range(RING)] for _ in feature_halves] for _ in range(2)
    )
    passing_2, arrived_2 = ([links.semaphore() for _ in feature_halves] for _ in range(2))
    phases = [links.phase(parts.at[h, pl.ds(0, 15)]) for h in feature_halves]

    def sum_first(h, a, delta):
        first, second = firsts[a], seconds[a]

        def part(k):
            return parts.at[h, col_of(a, first.at(k), second.at(delta)), node_slices[a]]

        return Sum4(
            links, first, part, relay_buf.at[h, delta, a], from_buf.at[h, delta, a],
            passing[h][delta], arrived[h][delta], phases[h],
        )

    def sum_second(h, a):
        return Sum4(
            links, seconds[a], lambda k: part2_buf.at[h, a, k], relay2_buf.at[h, a],
            from2_buf.at[h, a], passing_2[h], arrived_2[h], phases[h],
        )

    first_sums = [
        [[sum_first(h, a, d) for d in range(RING)] for a in node_halves] for h in feature_halves
    ]
    last_sums = [[sum_second(h, a) for a in node_halves] for h in feature_halves]

    def push_first(h, d):
        for a in node_halves:
            first_sums[h][a][d].push()

    def relay_first(h, d):
        links.wait(passing[h][d], relay_buf.at[h, d])
        for a in node_halves:
            first_sums[h][a][d].relay()

    def wait_first(h, d):
        links.wait(arrived[h][d], from_buf.at[h, d])

    def done_first(h, a, d):
        part2_buf[h, a, d] = first_sums[h][a][d].total().astype(BF16)

    def scatter_start(h):
        lax.fori_loop(0, RING * RING, lambda b, _: (pick(parts.at[h], 0, b), 0)[1], 0)
        for d in (2, 1, 3, 0):
            push_first(h, d)

    def scatter_relay(h):
        for d in (2, 1, 3, 0):
            relay_first(h, d)

    def scatter_far(h):
        wait_first(h, 2)
        for a in node_halves:
            done_first(h, a, 2)
            last_sums[h][a].push_far()

    def scatter_near(h):
        wait_first(h, 1)
        for a in node_halves:
            done_first(h, a, 1)
            last_sums[h][a].push_up()
        wait_first(h, 3)
        for a in node_halves:
            done_first(h, a, 3)
            last_sums[h][a].push_down()

    def scatter_end(h):
        links.wait(passing_2[h], relay2_buf.at[h])
        for a in node_halves:
            last_sums[h][a].relay()
        wait_first(h, 0)
        for a in node_halves:
            done_first(h, a, 0)

    gather_relay(0)
    gather_push(1)
    gather_near(0)
    gather_far(0)
    gather_relay(1)
    gather_done(0)
    to_scalars.wait()
    loads[3].wait()
    tile_pass(group[0], False)
    scatter_start(0)
    gather_near(1)
    gather_far(1)
    gather_done(1)
    tile_pass(group[1], False)
    scatter_start(1)
    scatter_relay(0)
    loads[4].wait()
    loads[5].wait()
    for t in range(tiles):
        cot_t[t] = cot_buf[tile_rows(t), :].astype(F32).T
    scatter_relay(1)
    scatter_far(0)
    scatter_far(1)
    scatter_near(0)
    scatter_near(1)
    scatter_end(0)
    scatter_end(1)

    weight = weight_buf[...]

    def dense(a):
        whole = [last_sums[h][a].total().astype(BF16) for h in feature_halves]
        for i in range(tiles // 2):
            t = a * (tiles // 2) + i
            hidden = jnp.concatenate([whole[0][i], whole[1][i]], axis=0)
            pre_act = lax.dot_general(
                weight, hidden, (((0,), (0,)), ((), ())), preferred_element_type=F32
            )
            value, slope = activation(pre_act)
            pre_grad = (cot_t[t] * slope).astype(BF16)
            own = jnp.dot(weight, pre_grad, preferred_element_type=F32).astype(BF16)
            for h in feature_halves:
                grads[h][here.col, t] = own[h * width : (h + 1) * width]
            value_buf[t] = value
            hidden_buf[t] = hidden
            grad_buf[t] = pre_grad

    share_phases = [links.phase(parts.at[h, pl.ds(0, 15)]) for h in feature_halves]
    one_sems = [[links.semaphore() for _ in range(3)] for _ in feature_halves]
    two_sems = [[links.semaphore() for _ in range(RING)] for _ in feature_halves]
    rest_sems = [links.semaphore() for _ in feature_halves]

    def share_first(h, a):
        first, second = seconds[a], firsts[a]
        return Share4(
            links,
            first,
            lambda k: grads[h].at[col_of(1 - a, first.at(k), second.position), node_slices[a]],
            tiles // 4,
            *one_sems[h],
            share_phases[h],
        )

    def share_second(h, a, delta):
        first, second = seconds[a], firsts[a]
        return Share4(
            links,
            second,
            lambda k: grads[h].at[col_of(1 - a, first.at(delta), second.at(k)), node_slices[a]],
            tiles // 4,
            two_sems[h][delta],
            rest_sems[h],
            rest_sems[h],
            share_phases[h],
        )

    ones = [[share_first(h, a) for a in node_halves] for h in feature_halves]
    twos = [
        [[share_second(h, a, d) for a in node_halves] for d in range(RING)] for h in feature_halves
    ]

    def one_push(h):
        for share in ones[h]:
            share.push()

    def one_wait(h, which):
        links.wait(one_sems[h][which], grads[h].at[0])

    def one_relay(h):
        one_wait(h, 0)
        for share in ones[h]:
            share.relay()

    def two_push(h, *offsets):
        for d in offsets:
            for share in twos[h][d]:
                share.push()

    def two_relay(h, *offsets):
        for d in offsets:
            links.wait(two_sems[h][d], grads[h].at[0])
            for share in twos[h][d]:
                share.relay()

    def shared(h):
        links.wait(rest_sems[h], grads[h].at[pl.ds(0, 8)])

    back_phases = [links.phase(parts.at[h, pl.ds(0, 7)]) for h in feature_halves]
    passing_3, arrived_3 = ([links.semaphore() for _ in feature_halves] for _ in range(2))
    swapped = [[links.semaphore() for _ in range(RING)] for _ in feature_halves]
    totals = [
        Sum4(
            links, here.y, lambda k, h=h: own_buf.at[h, k], relay3_buf.at[h], from3_buf.at[h],
            passing_3[h], arrived_3[h], back_phases[h],
        )
        for h in feature_halves
    ]
    near_order = (2, 1, 3, 0)

    def block(h, k, core):
        return sums.at[h, here.y.at(k) * 2 + core]

    def back_swap(h):
        for k in near_order:
            pick(sums.at[h], 4, here.y.at(k) * 2 + 1 - here.core)
            links.start(
                block(h, k, 1 - here.core), twin_buf.at[h, k], here.sibling, swapped[h][k],
                back_phases[h],
            )
        for k in near_order:
            pick(sums.at[h], 4, here.y.at(k) * 2 + here.core)

    def back_push(h):
        pushes = {2: totals[h].push_far, 1: totals[h].push_up, 3: totals[h].push_down}
        for k in near_order:
            links.wait(swapped[h][k], twin_buf.at[h, k])
            own = block(h, k, here.core)[...].astype(F32) + twin_buf[h, k].astype(F32)
            own_buf[h, k] = own.astype(BF16)
            if k in pushes:
                pushes[k]()

    def back_relay(h):
        links.wait(passing_3[h], relay3_buf.at[h])
        totals[h].relay()

    def back_end(h):
        links.wait(arrived_3[h], from3_buf.at[h])
        whole = totals[h].total()
        for t in range(tiles):
            feature_grad[tile_rows(t), pl.ds(h * width, width)] = whole[t].T.astype(BF16)

    for h in feature_halves:
        links.wait(arrived_2[h], from2_buf.at[h])
    for a in node_halves:
        dense(a)
        ones[0][a].push()
        twos[0][0][a].push()
    for t in range(tiles):
        term = lax.dot_general(
            hidden_buf[t], grad_buf[t], (((1,), (1,)), ((), ())), preferred_element_type=F32
        ).reshape(term_buf.shape)
        if t == 0:
            term_buf[...] = term
        else:
            term_buf[...] += term
    stores = [
        pltpu.make_async_copy(src, dst, local_sem.at[8 + i])
        for i, (src, dst) in enumerate(
            ((out_buf, out_ref), (weight_grad, weight_grad_ref), (feature_grad, feature_grad_ref))
        )
    ]
    weights = SumAll(
        links, here, term_buf, weight_grad, term_relay, term_from, term_own, term_got
    )
    weights.next()
    one_relay(0)
    one_wait(0, 1)
    two_push(0, 1, 3)
    weights.next()
    one_push(1)
    two_relay(0, 0)
    weights.next()
    one_wait(0, 2)
    two_push(0, 2)
    two_push(1, 0)
    weights.next()
    two_relay(0, 1, 3)
    one_relay(1)
    weights.next()
    two_relay(0, 2)
    one_wait(1, 1)
    two_push(1, 1, 3)
    two_relay(1, 0)
    one_wait(1, 2)
    two_push(1, 2)
    weights.next()
    shared(0)
    tile_pass(grads[0], True)
    back_swap(0)
    two_relay(1, 1, 3)
    weights.next()
    back_push(0)
    two_relay(1, 2)
    shared(1)
    tile_pass(grads[1], True)
    back_swap(1)
    back_relay(0)
    weights.next()
    back_push(1)
    weights.next()
    for t in range(tiles):
        out_buf[tile_rows(t), :] = value_buf[t].T.astype(BF16)
    stores[0].start()
    back_end(0)
    weights.next()
    back_relay(1)
    weights.next()
    stores[1].start()
    back_end(1)
    stores[2].start()
    links.drain()
    for store in stores:
        store.wait()


def copy_kernel(*refs):
    count = (len(refs) - 2) // 3
    sources, targets, held = (refs[i * count : (i + 1) * count] for i in range(3))
    came, left = refs[-2:]
    into = [pltpu.make_async_copy(sources[i], held[i], came.at[i]) for i in range(count)]
    out = [pltpu.make_async_copy(held[i], targets[i], left.at[i]) for i in range(count)]
    for copy in into:
        copy.start()
    for first, second in zip(into, out):
        first.wait()
        second.start()
    for copy in out:
        copy.wait()


def shards(features, weight, adj_tiles, tile_rows, tile_cols, tile_count, cotangent):
    nodes, width = features.shape
    slots, tile = adj_tiles.shape[:2]
    n_row, n_col = lax.axis_size("row"), lax.axis_size("col")
    tiles, half, member = nodes // tile, width // 2, width // RING
    one = (half, tile)

    def vmem(*shape, dtype=BF16):
        return pltpu.VMEM(shape, dtype)

    anywhere = pl.BlockSpec(memory_space=pl.ANY)
    results = pl.pallas_call(
        layer_kernel,
        out_shape=(
            jax.ShapeDtypeStruct((nodes, width), BF16),
            jax.ShapeDtypeStruct((RING, member, width), F32),
            jax.ShapeDtypeStruct((nodes, width), BF16),
        ),
        in_specs=[anywhere] * 7,
        out_specs=(anywhere,) * 3,
        scratch_shapes=[
            vmem(nodes, width),
            vmem(width, width),
            vmem(slots, tile, tile),
            vmem(2, 1, slots, dtype=jnp.int32),
            vmem(nodes, width),
            vmem(8, 128, dtype=jnp.int32),
            pltpu.SMEM((8, 128), jnp.int32),
            vmem(n_row, tiles, *one),
            vmem(n_row, tiles, *one),
            vmem(slots + 1, *one),
            vmem(2, n_col, tiles, *one),
            vmem(2, RING, 2, 2, tiles // 4, *one),
            vmem(2, RING, 2, 2, tiles // 2, *one),
            vmem(2, 2, RING, tiles // 2, *one),
            vmem(2, 2, 2, tiles // 4, *one),
            vmem(2, 2, 2, tiles // 2, *one),
            vmem(tiles, width, tile, dtype=F32),
            vmem(tiles, width, tile),
            vmem(tiles, width, tile),
            vmem(tiles, width, tile, dtype=F32),
            vmem(n_col, tiles, *one),
            vmem(n_col, tiles, *one),
            vmem(RING, member, width, dtype=F32),
            vmem(2, member // 2, width, dtype=F32),
            vmem(2, member, width, dtype=F32),
            vmem(11, member, width, dtype=F32),
            vmem(5, member, width, dtype=F32),
            vmem(2, n_row, tiles, *one),
            vmem(2, RING, tiles, *one),
            vmem(2, RING, tiles, *one),
            vmem(2, 2, tiles // 2, *one),
            vmem(2, 2, tiles, *one),
            vmem(nodes, width),
            vmem(RING, member, width, dtype=F32),
            vmem(nodes, width),
            pltpu.SMEM((1,), jnp.int32),
            pltpu.SemaphoreType.DMA((11,)),
            pltpu.SemaphoreType.DMA((9,)),
            pltpu.SemaphoreType.DMA((65,)),
        ],
        compiler_params=pltpu.CompilerParams(
            vmem_limit_bytes=VMEM_BYTES, collective_id=0, has_side_effects=True
        ),
        name="layer",
    )(
        tile_count, features, weight, adj_tiles,
        tile_rows.reshape(1, slots), tile_cols.reshape(1, slots), cotangent,
    )
    out_features, weight_grad, feature_grad = pl.pallas_call(
        copy_kernel,
        out_shape=tuple(jax.ShapeDtypeStruct(r.shape, r.dtype) for r in results),
        in_specs=[anywhere] * 3,
        out_specs=(anywhere,) * 3,
        scratch_shapes=[pltpu.VMEM(r.shape, r.dtype) for r in results]
        + [pltpu.SemaphoreType.DMA((3,))] * 2,
        compiler_params=pltpu.CompilerParams(vmem_limit_bytes=VMEM_BYTES),
        name="results",
    )(*results)
    return (out_features, weight_grad.reshape(width, width), feature_grad)


def solution(mesh):
    in_specs = (
        P(("row", "col"), None),
        P(),
        P(("row", "col"), None, None),
        P(("row", "col")),
        P(("row", "col")),
        P(("row", "col")),
        P(("row", "col"), None),
    )
    out_specs = (P(("row", "col"), None), P(), P(("row", "col"), None))
    return jax.shard_map(shards, mesh=mesh, in_specs=in_specs, out_specs=out_specs, check_vma=False)
```

```python
import jax
import jax.numpy as jnp
from jax import lax
from jax.experimental import pallas as pl
from jax.experimental.pallas import tpu as pltpu
from jax.sharding import PartitionSpec as P

MESH = pl.DeviceIdType.MESH
BF16, F32 = jnp.bfloat16, jnp.float32
VMEM_BYTES = 63 * 2**20
RING = 4
UNROLL = 48
BACK_WIDTHS = (64, 64)


class Links:
    def __init__(self, send_sem, recv_sem):
        self.send_sem, self.recv_sem = send_sem, recv_sem
        self.used, self.phases = 0, []

    def semaphore(self):
        self.used += 1
        return self.recv_sem.at[self.used - 1]

    def phase(self, ref):
        self.phases.append(ref)
        return len(self.phases) - 1

    def start(self, src, dst, device, arrived, phase):
        pltpu.make_async_remote_copy(
            src_ref=src,
            dst_ref=dst,
            send_sem=self.send_sem.at[phase],
            recv_sem=arrived,
            device_id=device,
            device_id_type=MESH,
        ).start()

    def wait(self, arrived, ref):
        pltpu.make_async_copy(ref, ref, arrived).wait()

    def drain(self):
        for at, ref in enumerate(self.phases):
            self.wait(self.send_sem.at[at], ref)


class Axis:
    def __init__(self, position, device_at):
        self.position = position
        self.up = device_at(lax.rem(position + 1, RING))
        self.down = device_at(lax.rem(position + 3, RING))
        odd = lax.rem(position, 2)
        self.pair = device_at(position + 1 - 2 * odd)
        self.other_pair = device_at(lax.rem(position + 3 + 2 * odd, RING))

    def at(self, offset):
        return lax.rem(self.position + offset, RING) if offset else self.position


class Place:
    def __init__(self):
        row, col = lax.axis_index("row"), lax.axis_index("col")
        self.row, self.col = row, col
        y, self.core = lax.div(row, 2), lax.rem(row, 2)
        x, z = lax.div(col, RING), lax.rem(col, RING)
        core = self.core
        self.y = Axis(y, lambda k: (k * 2 + core, col))
        self.x = Axis(x, lambda k: (row, k * RING + z))
        self.z = Axis(z, lambda k: (row, x * RING + k))
        self.sibling_row = row + 1 - 2 * core
        self.sibling = (self.sibling_row, col)

    def greet(self):
        barrier = pltpu.get_barrier_semaphore()
        others = [d for axis in (self.x, self.y, self.z) for d in (axis.up, axis.down)]
        others.append(self.sibling)
        for other in others:
            pl.semaphore_signal(barrier, inc=1, device_id=other, device_id_type=MESH)
        return lambda: pl.semaphore_wait(barrier, len(others))


def add_to(ref, value):
    ref[...] = (ref[...].astype(F32) + value.astype(F32)).astype(ref.dtype)


class Sum4:
    def __init__(self, links, axis, part, relays, blocks, passing, arrived, phase):
        self.links, self.axis, self.part = links, axis, part
        self.relay_up, self.relay_down = relays.at[0], relays.at[1]
        self.from_down, self.from_up = blocks.at[0], blocks.at[1]
        self.passing, self.arrived, self.phase = passing, arrived, phase
        half = relays.shape[1]
        self.low, self.high = pl.ds(0, half), pl.ds(half, half)

    def send(self, src, dst, device, arrived):
        self.links.start(src, dst, device, arrived, self.phase)

    def push_far(self):
        far = self.part(2)
        self.send(far.at[self.low], self.relay_up, self.axis.up, self.passing)
        self.send(far.at[self.high], self.relay_down, self.axis.down, self.passing)

    def push_up(self):
        near = self.part(1).at[self.high]
        self.send(near, self.from_down.at[self.high], self.axis.up, self.arrived)

    def push_down(self):
        near = self.part(3).at[self.low]
        self.send(near, self.from_up.at[self.low], self.axis.down, self.arrived)

    def push(self):
        self.push_far()
        self.push_up()
        self.push_down()

    def relay(self):
        add_to(self.relay_up, self.part(1)[self.low])
        self.send(self.relay_up, self.from_down.at[self.low], self.axis.up, self.arrived)
        add_to(self.relay_down, self.part(3)[self.high])
        self.send(self.relay_down, self.from_up.at[self.high], self.axis.down, self.arrived)

    def total(self):
        return (
            self.part(0)[...].astype(F32)
            + self.from_down[...].astype(F32)
            + self.from_up[...].astype(F32)
        )


class Share4:
    def __init__(self, links, axis, slot, half, first, near, far, phase):
        self.links, self.axis, self.slot = links, axis, slot
        self.first, self.near, self.far, self.phase = first, near, far, phase
        self.low, self.high = pl.ds(0, half), pl.ds(half, half)

    def send(self, k, rows, device, arrived):
        ref = self.slot(k).at[rows]
        self.links.start(ref, ref, device, arrived, self.phase)

    def push(self):
        self.send(0, self.low, self.axis.up, self.first)
        self.send(0, self.high, self.axis.down, self.first)
        self.send(0, self.high, self.axis.up, self.near)
        self.send(0, self.low, self.axis.down, self.near)

    def relay(self):
        self.send(3, self.low, self.axis.up, self.far)
        self.send(1, self.high, self.axis.down, self.far)


class SumAll:
    def __init__(self, links, here, term, result, relay, came, own, got):
        y = here.y
        self.links, self.own, self.got, self.relays, self.came = links, own, got, relay, came
        self.result = result
        phase = links.phase(own)
        passing, arrived, self.first, self.rest = (links.semaphore() for _ in range(4))
        self.ring = Sum4(links, y, lambda k: term.at[y.at(k)], relay, came, passing, arrived, phase)
        self.share = Share4(
            links, y, lambda k: result.at[y.at(k)], result.shape[1] // 2,
            self.first, self.rest, self.rest, phase,
        )
        self.slot = result.at[y.position]
        pairs = (here.sibling, here.x.pair, here.z.pair, here.x.other_pair, here.z.other_pair)
        self.steps = self.run(pairs)

    def run(self, pairs):
        links, ring, share = self.links, self.ring, self.share
        ring.push()
        yield
        links.wait(ring.passing, self.relays)
        ring.relay()
        yield
        links.wait(ring.arrived, self.came)
        total = ring.total()
        for at, pair in enumerate(pairs):
            self.own[at] = total
            arrived = links.semaphore()
            links.start(self.own.at[at], self.got.at[at], pair, arrived, ring.phase)
            yield
            links.wait(arrived, self.got.at[at])
            total = self.own[at] + self.got[at]
        self.slot[...] = total
        share.push()
        yield
        links.wait(self.first, self.result.at[0])
        share.relay()
        yield
        links.wait(self.rest, self.result.at[pl.ds(0, 2)])

    def next(self):
        next(self.steps, None)


def activation(value):
    root = 0.7978845608028654
    square = value * value
    t = jnp.tanh(root * (value + 0.044715 * (value * square)))
    half = 0.5 * (1.0 + t)
    slope = half + (0.5 * value) * (1.0 - t * t) * (root * (1.0 + 3.0 * 0.044715 * square))
    return value * half, slope


def spread(row):
    wide = jnp.broadcast_to(row, (row.shape[1], row.shape[1]))
    return wide, wide.T


def slot_order(key, source, count, empty):
    lanes = key.shape[1]
    lane = lax.broadcasted_iota(jnp.int32, (lanes, lanes), 1)
    sub = lax.broadcasted_iota(jnp.int32, (lanes, lanes), 0)
    at = lax.broadcasted_iota(jnp.int32, (1, lanes), 1)
    key = jnp.where(at < count, key, 2 * lanes)

    def over(mask, value):
        return jnp.sum(jnp.where(mask, value, 0), axis=0, keepdims=True)

    unique_row, unique_col = spread(key * lanes + at)
    _, rank = spread(over(unique_col < unique_row, 1))
    _, key_col = spread(key)
    _, source_col = spread(source)
    hit = rank == lane
    slot, source, sorted_key = over(hit, sub), over(hit, source_col), over(hit, key_col)
    same = over((rank == lane - 1) & (key_col == sorted_key), 1)
    last = jnp.where(over(key_col == lane, 1) > 0, over(key_col <= lane, 1) - 1, empty)
    return slot, source, same, last


def layer_kernel(
    count_ref, features_ref, weight_ref, adj_ref, rows_ref, cols_ref, cot_ref,
    out_ref, weight_grad_ref, feature_grad_ref,
    x_buf, weight_buf, adj, ids_buf, cot_buf, table_buf, table,
    group_0, group_1, running, running_0, running_1, parts, relay_buf, from_buf, part2_buf, relay2_buf, from2_buf,
    cot_t, hidden_buf, grad_buf, value_buf, grads_0, grads_1,
    term_buf, term_relay, term_from, term_own, term_got,
    sums_0, sums_1, own_0, own_1, twin_0, twin_1, relay3_0, relay3_1, from3_0, from3_1,
    out_buf, weight_grad, feature_grad, count_buf, local_sem, send_sem, recv_sem,
):
    here = Place()
    group, grads = (group_0, group_1), (grads_0, grads_1)
    running_back, sums, own_buf = (running_0, running_1), (sums_0, sums_1), (own_0, own_1)
    twin_buf, relay3_buf = (twin_0, twin_1), (relay3_0, relay3_1)
    from3_buf = (from3_0, from3_1)
    offsets = (0, BACK_WIDTHS[0])
    tiles, width, tile = parts.shape[2], parts.shape[3], parts.shape[4]
    slots = adj.shape[0]
    links = Links(send_sem, recv_sem)
    loads = [
        pltpu.make_async_copy(src, dst, local_sem.at[i])
        for i, (src, dst) in enumerate(
            (
                (features_ref, x_buf),
                (rows_ref, ids_buf.at[0]),
                (cols_ref, ids_buf.at[1]),
                (adj_ref, adj),
                (weight_ref, weight_buf),
                (cot_ref, cot_buf),
                (count_ref, count_buf),
            )
        )
    ]
    for load in loads:
        load.start()
    met = here.greet()
    feature_halves = node_halves = (0, 1)

    def tile_rows(t):
        return pl.ds(t * tile, tile)

    def row_slot(h, k):
        return group[h].at[here.y.at(k) * 2 + here.core]

    def share_row(h):
        first, near, far = (links.semaphore() for _ in range(3))
        phase = links.phase(parts.at[h, pl.ds(0, 7)])
        return Share4(
            links, here.y, lambda k: row_slot(h, k), tiles // 2, first, near, far, phase
        )

    shares = [share_row(h) for h in feature_halves]
    twins = [links.semaphore() for _ in feature_halves]
    low, high = shares[0].low, shares[0].high

    def across(h, k, rows):
        ref = row_slot(h, k).at[rows]
        links.start(ref, ref, here.sibling, twins[h], shares[h].phase)

    def gather_load(h):
        for t in range(tiles):
            block = x_buf[tile_rows(t), pl.ds(h * width, width)]
            group[h][here.row, t] = block.astype(F32).T.astype(BF16)

    def gather_push(h):
        shares[h].push()
        across(h, 0, low)
        across(h, 0, high)

    def gather_relay(h):
        links.wait(shares[h].first, group[h].at[0])
        shares[h].relay()
        across(h, 3, low)
        across(h, 1, high)

    def gather_near(h):
        links.wait(shares[h].near, group[h].at[0])
        across(h, 3, high)
        across(h, 1, low)

    def gather_far(h):
        links.wait(shares[h].far, group[h].at[0])
        across(h, 2, low)
        across(h, 2, high)

    def gather_done(h):
        links.wait(twins[h], group[h].at[pl.ds(0, 4)])

    loads[0].wait()
    gather_load(0)
    met()
    gather_push(0)
    gather_load(1)

    loads[1].wait()
    loads[2].wait()
    table_buf[...] = jnp.zeros_like(table_buf)
    for i in (0, 1):
        table_buf[i : i + 1, 0:slots] = ids_buf[i]
    by_row, by_col = table_buf[0:1, :], table_buf[1:2, :]
    loads[6].wait()
    count = count_buf[0]
    order = slot_order(by_row, by_col, count, slots) + slot_order(by_col, by_row, count, slots)
    for i, line in enumerate(order):
        table_buf[i : i + 1, :] = line
    to_scalars = pltpu.make_async_copy(table_buf, table, local_sem.at[7])
    to_scalars.start()
    for sums_to in (running, *running_back):
        sums_to[slots] = jnp.zeros(sums_to.shape[1:], BF16)

    def tile_pass(source, running, backward, between=lambda: None):
        base = 4 if backward else 0
        contract = ((1,), (0,)) if backward else ((1,), (1,))

        def step(block, acc):
            products = []
            for k in range(UNROLL):
                at = block * UNROLL + k
                node = table[base + 1, at]
                products.append(
                    lax.dot_general(
                        source[lax.div(node, tiles), lax.rem(node, tiles)],
                        adj[table[base, at]],
                        (contract, ((), ())),
                        preferred_element_type=F32,
                    )
                )
            for k in range(UNROLL):
                at = block * UNROLL + k
                acc = acc * table[base + 2, at].astype(F32) + products[k]
                running[at] = acc.astype(BF16)
            return acc

        steps = slots // UNROLL
        acc = lax.fori_loop(0, steps // 2, step, jnp.zeros(running.shape[1:], F32))
        between()
        lax.fori_loop(steps // 2, steps, step, acc)

    def pick(target, running, base, block):
        picked = [running[table[base + 3, block * tiles + t]] for t in range(tiles)]
        for t in range(tiles):
            target[block, t] = picked[t]

    firsts, seconds = (here.z, here.x), (here.x, here.z)
    node_slices = [pl.ds(a * (tiles // 2), tiles // 2) for a in node_halves]

    def col_of(a, first, second):
        return second * RING + first if a == 0 else first * RING + second

    passing, arrived = (
        [[links.semaphore() for _ in range(RING)] for _ in feature_halves] for _ in range(2)
    )
    passing_2, arrived_2 = ([links.semaphore() for _ in feature_halves] for _ in range(2))
    phases = [links.phase(parts.at[h, pl.ds(0, 15)]) for h in feature_halves]

    def sum_first(h, a, delta):
        first, second = firsts[a], seconds[a]

        def part(k):
            return parts.at[h, col_of(a, first.at(k), second.at(delta)), node_slices[a]]

        return Sum4(
            links, first, part, relay_buf.at[h, delta, a], from_buf.at[h, delta, a],
            passing[h][delta], arrived[h][delta], phases[h],
        )

    def sum_second(h, a):
        return Sum4(
            links, seconds[a], lambda k: part2_buf.at[h, a, k], relay2_buf.at[h, a],
            from2_buf.at[h, a], passing_2[h], arrived_2[h], phases[h],
        )

    first_sums = [
        [[sum_first(h, a, d) for d in range(RING)] for a in node_halves] for h in feature_halves
    ]
    last_sums = [[sum_second(h, a) for a in node_halves] for h in feature_halves]

    def push_first(h, d):
        for a in node_halves:
            first_sums[h][a][d].push()

    def relay_first(h, d):
        links.wait(passing[h][d], relay_buf.at[h, d])
        for a in node_halves:
            first_sums[h][a][d].relay()

    def wait_first(h, d):
        links.wait(arrived[h][d], from_buf.at[h, d])

    def done_first(h, a, d):
        part2_buf[h, a, d] = first_sums[h][a][d].total().astype(BF16)

    def scatter_start(h):
        lax.fori_loop(0, RING * RING, lambda b, _: (pick(parts.at[h], running, 0, b), 0)[1], 0)
        for d in (2, 1, 3, 0):
            push_first(h, d)

    def scatter_relay(h):
        for d in (2, 1, 3, 0):
            relay_first(h, d)

    def scatter_far(h):
        wait_first(h, 2)
        for a in node_halves:
            done_first(h, a, 2)
            last_sums[h][a].push_far()

    def scatter_near(h):
        wait_first(h, 1)
        for a in node_halves:
            done_first(h, a, 1)
            last_sums[h][a].push_up()
        wait_first(h, 3)
        for a in node_halves:
            done_first(h, a, 3)
            last_sums[h][a].push_down()

    def scatter_end(h):
        links.wait(passing_2[h], relay2_buf.at[h])
        for a in node_halves:
            last_sums[h][a].relay()
        wait_first(h, 0)
        for a in node_halves:
            done_first(h, a, 0)

    gather_relay(0)
    gather_push(1)
    gather_near(0)
    gather_far(0)
    gather_relay(1)
    gather_done(0)
    to_scalars.wait()
    loads[3].wait()

    def gather_rest():
        gather_near(1)
        gather_far(1)

    tile_pass(group[0], running, False, gather_rest)
    scatter_start(0)
    gather_done(1)
    tile_pass(group[1], running, False)
    scatter_start(1)
    scatter_relay(0)
    loads[4].wait()
    loads[5].wait()
    for t in range(tiles):
        cot_t[t] = cot_buf[tile_rows(t), :].astype(F32).T
    scatter_relay(1)
    scatter_far(0)
    scatter_far(1)
    scatter_near(0)
    scatter_near(1)
    scatter_end(0)
    scatter_end(1)

    weight = weight_buf[...]

    def dense(a):
        whole = [last_sums[h][a].total().astype(BF16) for h in feature_halves]
        for i in range(tiles // 2):
            t = a * (tiles // 2) + i
            hidden = jnp.concatenate([whole[0][i], whole[1][i]], axis=0)
            pre_act = lax.dot_general(
                weight, hidden, (((0,), (0,)), ((), ())), preferred_element_type=F32
            )
            value, slope = activation(pre_act)
            pre_grad = (cot_t[t] * slope).astype(BF16)
            own = jnp.dot(weight, pre_grad, preferred_element_type=F32).astype(BF16)
            for h in feature_halves:
                grads[h][here.col, t] = own[offsets[h] : offsets[h] + BACK_WIDTHS[h]]
            value_buf[t] = value
            hidden_buf[t] = hidden
            grad_buf[t] = pre_grad

    share_phases = [links.phase(grads[h].at[pl.ds(0, 15)]) for h in feature_halves]
    one_sems = [[links.semaphore() for _ in range(3)] for _ in feature_halves]
    two_sems = [[links.semaphore() for _ in range(RING)] for _ in feature_halves]
    rest_sems = [links.semaphore() for _ in feature_halves]

    def share_first(h, a):
        first, second = seconds[a], firsts[a]
        return Share4(
            links,
            first,
            lambda k: grads[h].at[col_of(1 - a, first.at(k), second.position), node_slices[a]],
            tiles // 4,
            *one_sems[h],
            share_phases[h],
        )

    def share_second(h, a, delta):
        first, second = seconds[a], firsts[a]
        return Share4(
            links,
            second,
            lambda k: grads[h].at[col_of(1 - a, first.at(delta), second.at(k)), node_slices[a]],
            tiles // 4,
            two_sems[h][delta],
            rest_sems[h],
            rest_sems[h],
            share_phases[h],
        )

    ones = [[share_first(h, a) for a in node_halves] for h in feature_halves]
    twos = [
        [[share_second(h, a, d) for a in node_halves] for d in range(RING)] for h in feature_halves
    ]

    def one_push(h):
        for share in ones[h]:
            share.push()

    def one_wait(h, which):
        links.wait(one_sems[h][which], grads[h].at[0])

    def one_relay(h):
        one_wait(h, 0)
        for share in ones[h]:
            share.relay()

    def two_push(h, *offsets):
        for d in offsets:
            for share in twos[h][d]:
                share.push()

    def two_relay(h, *offsets):
        for d in offsets:
            links.wait(two_sems[h][d], grads[h].at[0])
            for share in twos[h][d]:
                share.relay()

    def shared(h):
        links.wait(rest_sems[h], grads[h].at[pl.ds(0, 8)])

    back_phases = [links.phase(grads[h].at[pl.ds(0, 7)]) for h in feature_halves]
    passing_3, arrived_3 = ([links.semaphore() for _ in feature_halves] for _ in range(2))
    swapped = [[links.semaphore() for _ in range(RING)] for _ in feature_halves]
    totals = [
        Sum4(
            links, here.y, lambda k, h=h: own_buf[h].at[k], relay3_buf[h], from3_buf[h],
            passing_3[h], arrived_3[h], back_phases[h],
        )
        for h in feature_halves
    ]
    near_order = (2, 1, 3, 0)

    def block(h, k, core):
        return sums[h].at[here.y.at(k) * 2 + core]

    def back_swap(h):
        for k in near_order:
            pick(sums[h], running_back[h], 4, here.y.at(k) * 2 + 1 - here.core)
            links.start(
                block(h, k, 1 - here.core), twin_buf[h].at[k], here.sibling, swapped[h][k],
                back_phases[h],
            )
        for k in near_order:
            pick(sums[h], running_back[h], 4, here.y.at(k) * 2 + here.core)

    def back_push(h):
        pushes = {2: totals[h].push_far, 1: totals[h].push_up, 3: totals[h].push_down}
        for k in near_order:
            links.wait(swapped[h][k], twin_buf[h].at[k])
            own = block(h, k, here.core)[...].astype(F32) + twin_buf[h][k].astype(F32)
            own_buf[h][k] = own.astype(BF16)
            if k in pushes:
                pushes[k]()

    def back_relay(h):
        links.wait(passing_3[h], relay3_buf[h])
        totals[h].relay()

    def back_end(h):
        links.wait(arrived_3[h], from3_buf[h])
        whole = totals[h].total()
        for t in range(tiles):
            feature_grad[tile_rows(t), pl.ds(offsets[h], BACK_WIDTHS[h])] = whole[t].T.astype(BF16)

    for h in feature_halves:
        links.wait(arrived_2[h], from2_buf.at[h])
    for a in node_halves:
        dense(a)
        ones[0][a].push()
        twos[0][0][a].push()
    for t in range(tiles):
        term = lax.dot_general(
            hidden_buf[t], grad_buf[t], (((1,), (1,)), ((), ())), preferred_element_type=F32
        ).reshape(term_buf.shape)
        if t == 0:
            term_buf[...] = term
        else:
            term_buf[...] += term
    stores = [
        pltpu.make_async_copy(src, dst, local_sem.at[8 + i])
        for i, (src, dst) in enumerate(
            ((out_buf, out_ref), (weight_grad, weight_grad_ref), (feature_grad, feature_grad_ref))
        )
    ]
    weights = SumAll(
        links, here, term_buf, weight_grad, term_relay, term_from, term_own, term_got
    )
    weights.next()
    one_relay(0)
    one_wait(0, 1)
    two_push(0, 1, 3)
    weights.next()
    one_push(1)
    two_relay(0, 0)
    one_wait(0, 2)
    two_push(0, 2)
    weights.next()
    two_push(1, 0)
    two_relay(0, 1, 3)
    one_relay(1)
    weights.next()
    two_relay(0, 2)
    one_wait(1, 1)
    two_push(1, 1, 3)
    two_relay(1, 0)
    one_wait(1, 2)
    two_push(1, 2)
    shared(0)
    tile_pass(grads[0], running_0, True)
    weights.next()
    two_relay(1, 1, 3)
    back_swap(0)
    two_relay(1, 2)
    back_push(0)
    weights.next()
    shared(1)
    tile_pass(grads[1], running_1, True)
    weights.next()
    back_swap(1)
    back_relay(0)
    back_push(1)
    weights.next()
    for t in range(tiles):
        out_buf[tile_rows(t), :] = value_buf[t].T.astype(BF16)
    stores[0].start()
    weights.next()
    back_relay(1)
    back_end(0)
    weights.next()
    stores[1].start()
    back_end(1)
    stores[2].start()
    links.drain()
    for store in stores:
        store.wait()


def copy_kernel(*refs):
    count = (len(refs) - 2) // 3
    sources, targets, held = (refs[i * count : (i + 1) * count] for i in range(3))
    came, left = refs[-2:]
    into = [pltpu.make_async_copy(sources[i], held[i], came.at[i]) for i in range(count)]
    out = [pltpu.make_async_copy(held[i], targets[i], left.at[i]) for i in range(count)]
    for copy in into:
        copy.start()
    for first, second in zip(into, out):
        first.wait()
        second.start()
    for copy in out:
        copy.wait()


def shards(features, weight, adj_tiles, tile_rows, tile_cols, tile_count, cotangent):
    nodes, width = features.shape
    slots, tile = adj_tiles.shape[:2]
    n_row, n_col = lax.axis_size("row"), lax.axis_size("col")
    tiles, half, member = nodes // tile, width // 2, width // RING
    one = (half, tile)
    backs = [(back, tile) for back in BACK_WIDTHS]

    def vmem(*shape, dtype=BF16):
        return pltpu.VMEM(shape, dtype)

    anywhere = pl.BlockSpec(memory_space=pl.ANY)
    results = pl.pallas_call(
        layer_kernel,
        out_shape=(
            jax.ShapeDtypeStruct((nodes, width), BF16),
            jax.ShapeDtypeStruct((RING, member, width), F32),
            jax.ShapeDtypeStruct((nodes, width), BF16),
        ),
        in_specs=[anywhere] * 7,
        out_specs=(anywhere,) * 3,
        scratch_shapes=[
            vmem(nodes, width),
            vmem(width, width),
            vmem(slots, tile, tile),
            vmem(2, 1, slots, dtype=jnp.int32),
            vmem(nodes, width),
            vmem(8, 128, dtype=jnp.int32),
            pltpu.SMEM((8, 128), jnp.int32),
            vmem(n_row, tiles, *one),
            vmem(n_row, tiles, *one),
            vmem(slots + 1, *one),
            *(vmem(slots + 1, *back) for back in backs),
            vmem(2, n_col, tiles, *one),
            vmem(2, RING, 2, 2, tiles // 4, *one),
            vmem(2, RING, 2, 2, tiles // 2, *one),
            vmem(2, 2, RING, tiles // 2, *one),
            vmem(2, 2, 2, tiles // 4, *one),
            vmem(2, 2, 2, tiles // 2, *one),
            vmem(tiles, width, tile, dtype=F32),
            vmem(tiles, width, tile),
            vmem(tiles, width, tile),
            vmem(tiles, width, tile, dtype=F32),
            *(vmem(n_col, tiles, *back) for back in backs),
            vmem(RING, member, width, dtype=F32),
            vmem(2, member // 2, width, dtype=F32),
            vmem(2, member, width, dtype=F32),
            vmem(11, member, width, dtype=F32),
            vmem(5, member, width, dtype=F32),
            *(vmem(n_row, tiles, *back) for back in backs),
            *(vmem(RING, tiles, *back) for back in backs),
            *(vmem(RING, tiles, *back) for back in backs),
            *(vmem(2, tiles // 2, *back) for back in backs),
            *(vmem(2, tiles, *back) for back in backs),
            vmem(nodes, width),
            vmem(RING, member, width, dtype=F32),
            vmem(nodes, width),
            pltpu.SMEM((1,), jnp.int32),
            pltpu.SemaphoreType.DMA((11,)),
            pltpu.SemaphoreType.DMA((9,)),
            pltpu.SemaphoreType.DMA((65,)),
        ],
        compiler_params=pltpu.CompilerParams(
            vmem_limit_bytes=VMEM_BYTES, collective_id=0, has_side_effects=True
        ),
        name="layer",
    )(
        tile_count, features, weight, adj_tiles,
        tile_rows.reshape(1, slots), tile_cols.reshape(1, slots), cotangent,
    )
    out_features, weight_grad, feature_grad = pl.pallas_call(
        copy_kernel,
        out_shape=tuple(jax.ShapeDtypeStruct(r.shape, r.dtype) for r in results),
        in_specs=[anywhere] * 3,
        out_specs=(anywhere,) * 3,
        scratch_shapes=[pltpu.VMEM(r.shape, r.dtype) for r in results]
        + [pltpu.SemaphoreType.DMA((3,))] * 2,
        compiler_params=pltpu.CompilerParams(vmem_limit_bytes=VMEM_BYTES),
        name="results",
    )(*results)
    return (out_features, weight_grad.reshape(width, width), feature_grad)


def solution(mesh):
    in_specs = (
        P(("row", "col"), None),
        P(),
        P(("row", "col"), None, None),
        P(("row", "col")),
        P(("row", "col")),
        P(("row", "col")),
        P(("row", "col"), None),
    )
    out_specs = (P(("row", "col"), None), P(), P(("row", "col"), None))
    return jax.shard_map(shards, mesh=mesh, in_specs=in_specs, out_specs=out_specs, check_vma=False)
```

```python
import jax
import jax.numpy as jnp
from jax import lax
from jax.experimental import pallas as pl
from jax.experimental.pallas import tpu as pltpu
from jax.sharding import PartitionSpec as P

MESH = pl.DeviceIdType.MESH
BF16, F32 = jnp.bfloat16, jnp.float32
VMEM_BYTES = 63 * 2**20
RING = 4
UNROLL = 48
BACK_WIDTHS = (64, 64)


class Links:
    def __init__(self, send_sem, recv_sem):
        self.send_sem, self.recv_sem = send_sem, recv_sem
        self.used, self.phases = 0, []

    def semaphore(self):
        self.used += 1
        return self.recv_sem.at[self.used - 1]

    def phase(self, ref):
        self.phases.append(ref)
        return len(self.phases) - 1

    def start(self, src, dst, device, arrived, phase):
        pltpu.make_async_remote_copy(
            src_ref=src,
            dst_ref=dst,
            send_sem=self.send_sem.at[phase],
            recv_sem=arrived,
            device_id=device,
            device_id_type=MESH,
        ).start()

    def wait(self, arrived, ref):
        pltpu.make_async_copy(ref, ref, arrived).wait()

    def drain(self):
        for at, ref in enumerate(self.phases):
            self.wait(self.send_sem.at[at], ref)


class Axis:
    def __init__(self, position, device_at):
        self.position = position
        self.up = device_at(lax.rem(position + 1, RING))
        self.down = device_at(lax.rem(position + 3, RING))
        odd = lax.rem(position, 2)
        self.pair = device_at(position + 1 - 2 * odd)
        self.other_pair = device_at(lax.rem(position + 3 + 2 * odd, RING))

    def at(self, offset):
        return lax.rem(self.position + offset, RING) if offset else self.position


class Place:
    def __init__(self):
        row, col = lax.axis_index("row"), lax.axis_index("col")
        self.row, self.col = row, col
        y, self.core = lax.div(row, 2), lax.rem(row, 2)
        x, z = lax.div(col, RING), lax.rem(col, RING)
        core = self.core
        self.y = Axis(y, lambda k: (k * 2 + core, col))
        self.x = Axis(x, lambda k: (row, k * RING + z))
        self.z = Axis(z, lambda k: (row, x * RING + k))
        self.sibling_row = row + 1 - 2 * core
        self.sibling = (self.sibling_row, col)

    def greet(self):
        barrier = pltpu.get_barrier_semaphore()
        others = [d for axis in (self.x, self.y, self.z) for d in (axis.up, axis.down)]
        others.append(self.sibling)
        for other in others:
            pl.semaphore_signal(barrier, inc=1, device_id=other, device_id_type=MESH)
        return lambda: pl.semaphore_wait(barrier, len(others))


def add_to(ref, value):
    ref[...] = (ref[...].astype(F32) + value.astype(F32)).astype(ref.dtype)


class Sum4:
    def __init__(self, links, axis, part, relays, blocks, passing, arrived, phase):
        self.links, self.axis, self.part = links, axis, part
        self.relay_up, self.relay_down = relays.at[0], relays.at[1]
        self.from_down, self.from_up = blocks.at[0], blocks.at[1]
        self.passing, self.arrived, self.phase = passing, arrived, phase
        half = relays.shape[1]
        self.low, self.high = pl.ds(0, half), pl.ds(half, half)

    def send(self, src, dst, device, arrived):
        self.links.start(src, dst, device, arrived, self.phase)

    def push_far(self):
        far = self.part(2)
        self.send(far.at[self.low], self.relay_up, self.axis.up, self.passing)
        self.send(far.at[self.high], self.relay_down, self.axis.down, self.passing)

    def push_up(self):
        near = self.part(1).at[self.high]
        self.send(near, self.from_down.at[self.high], self.axis.up, self.arrived)

    def push_down(self):
        near = self.part(3).at[self.low]
        self.send(near, self.from_up.at[self.low], self.axis.down, self.arrived)

    def push(self):
        self.push_far()
        self.push_up()
        self.push_down()

    def relay(self):
        add_to(self.relay_up, self.part(1)[self.low])
        self.send(self.relay_up, self.from_down.at[self.low], self.axis.up, self.arrived)
        add_to(self.relay_down, self.part(3)[self.high])
        self.send(self.relay_down, self.from_up.at[self.high], self.axis.down, self.arrived)

    def total(self):
        return (
            self.part(0)[...].astype(F32)
            + self.from_down[...].astype(F32)
            + self.from_up[...].astype(F32)
        )


class Share4:
    def __init__(self, links, axis, slot, half, first, near, far, phase):
        self.links, self.axis, self.slot = links, axis, slot
        self.first, self.near, self.far, self.phase = first, near, far, phase
        self.low, self.high = pl.ds(0, half), pl.ds(half, half)

    def send(self, k, rows, device, arrived):
        ref = self.slot(k).at[rows]
        self.links.start(ref, ref, device, arrived, self.phase)

    def push(self):
        self.send(0, self.low, self.axis.up, self.first)
        self.send(0, self.high, self.axis.down, self.first)
        self.send(0, self.high, self.axis.up, self.near)
        self.send(0, self.low, self.axis.down, self.near)

    def relay(self):
        self.send(3, self.low, self.axis.up, self.far)
        self.send(1, self.high, self.axis.down, self.far)


class SumAll:
    def __init__(self, links, here, term, result, relay, came, own, got):
        y = here.y
        self.links, self.own, self.got, self.relays, self.came = links, own, got, relay, came
        self.result = result
        phase = links.phase(own)
        passing, arrived, self.first, self.rest = (links.semaphore() for _ in range(4))
        self.ring = Sum4(links, y, lambda k: term.at[y.at(k)], relay, came, passing, arrived, phase)
        self.share = Share4(
            links, y, lambda k: result.at[y.at(k)], result.shape[1] // 2,
            self.first, self.rest, self.rest, phase,
        )
        self.slot = result.at[y.position]
        pairs = (here.sibling, here.x.pair, here.z.pair, here.x.other_pair, here.z.other_pair)
        self.steps = self.run(pairs)

    def run(self, pairs):
        links, ring, share = self.links, self.ring, self.share
        ring.push()
        yield
        links.wait(ring.passing, self.relays)
        ring.relay()
        yield
        links.wait(ring.arrived, self.came)
        total = ring.total()
        for at, pair in enumerate(pairs):
            self.own[at] = total
            arrived = links.semaphore()
            links.start(self.own.at[at], self.got.at[at], pair, arrived, ring.phase)
            yield
            links.wait(arrived, self.got.at[at])
            total = self.own[at] + self.got[at]
        self.slot[...] = total
        share.push()
        yield
        links.wait(self.first, self.result.at[0])
        share.relay()
        yield
        links.wait(self.rest, self.result.at[pl.ds(0, 2)])

    def next(self):
        next(self.steps, None)


def activation(value):
    root = 0.7978845608028654
    square = value * value
    t = jnp.tanh(root * (value + 0.044715 * (value * square)))
    half = 0.5 * (1.0 + t)
    slope = half + (0.5 * value) * (1.0 - t * t) * (root * (1.0 + 3.0 * 0.044715 * square))
    return value * half, slope


def spread(row):
    wide = jnp.broadcast_to(row, (row.shape[1], row.shape[1]))
    return wide, wide.T


def slot_order(key, source, count, empty):
    lanes = key.shape[1]
    lane = lax.broadcasted_iota(jnp.int32, (lanes, lanes), 1)
    sub = lax.broadcasted_iota(jnp.int32, (lanes, lanes), 0)
    at = lax.broadcasted_iota(jnp.int32, (1, lanes), 1)
    key = jnp.where(at < count, key, 2 * lanes)

    def over(mask, value):
        return jnp.sum(jnp.where(mask, value, 0), axis=0, keepdims=True)

    unique_row, unique_col = spread(key * lanes + at)
    _, rank = spread(over(unique_col < unique_row, 1))
    _, key_col = spread(key)
    _, source_col = spread(source)
    hit = rank == lane
    slot, source, sorted_key = over(hit, sub), over(hit, source_col), over(hit, key_col)
    same = over((rank == lane - 1) & (key_col == sorted_key), 1)
    last = jnp.where(over(key_col == lane, 1) > 0, over(key_col <= lane, 1) - 1, empty)
    return slot, source, same, last


def layer_kernel(
    count_ref, features_ref, weight_ref, adj_ref, rows_ref, cols_ref, cot_ref,
    out_ref, weight_grad_ref, feature_grad_ref,
    x_buf, weight_buf, adj, ids_buf, cot_buf, table_buf, table,
    group_0, group_1, running, running_0, running_1, parts, relay_buf, from_buf, part2_buf, relay2_buf, from2_buf,
    cot_t, hidden_buf, grad_buf, value_buf, grads_0, grads_1,
    term_buf, term_relay, term_from, term_own, term_got,
    sums_0, sums_1, own_0, own_1, twin_0, twin_1, relay3_0, relay3_1, from3_0, from3_1,
    out_buf, weight_grad, feature_grad, count_buf, local_sem, send_sem, recv_sem,
):
    here = Place()
    group, grads = (group_0, group_1), (grads_0, grads_1)
    running_back, sums, own_buf = (running_0, running_1), (sums_0, sums_1), (own_0, own_1)
    twin_buf, relay3_buf = (twin_0, twin_1), (relay3_0, relay3_1)
    from3_buf = (from3_0, from3_1)
    offsets = (0, BACK_WIDTHS[0])
    tiles, width, tile = parts.shape[2], parts.shape[3], parts.shape[4]
    slots = adj.shape[0]
    links = Links(send_sem, recv_sem)
    loads = [
        pltpu.make_async_copy(src, dst, local_sem.at[i])
        for i, (src, dst) in enumerate(
            (
                (features_ref, x_buf),
                (rows_ref, ids_buf.at[0]),
                (cols_ref, ids_buf.at[1]),
                (adj_ref, adj),
                (weight_ref, weight_buf),
                (cot_ref, cot_buf),
                (count_ref, count_buf),
            )
        )
    ]
    for load in loads:
        load.start()
    met = here.greet()
    feature_halves = node_halves = (0, 1)

    def tile_rows(t):
        return pl.ds(t * tile, tile)

    def row_slot(h, k):
        return group[h].at[here.y.at(k) * 2 + here.core]

    def share_row(h):
        first, near, far = (links.semaphore() for _ in range(3))
        phase = links.phase(parts.at[h, pl.ds(0, 7)])
        return Share4(
            links, here.y, lambda k: row_slot(h, k), tiles // 2, first, near, far, phase
        )

    shares = [share_row(h) for h in feature_halves]
    twins = [links.semaphore() for _ in feature_halves]
    low, high = shares[0].low, shares[0].high

    def across(h, k, rows):
        ref = row_slot(h, k).at[rows]
        links.start(ref, ref, here.sibling, twins[h], shares[h].phase)

    def gather_load(h):
        for t in range(tiles):
            block = x_buf[tile_rows(t), pl.ds(h * width, width)]
            group[h][here.row, t] = block.astype(F32).T.astype(BF16)

    def gather_push(h):
        shares[h].push()
        across(h, 0, low)
        across(h, 0, high)

    def gather_relay(h):
        links.wait(shares[h].first, group[h].at[0])
        shares[h].relay()
        across(h, 3, low)
        across(h, 1, high)

    def gather_near(h):
        links.wait(shares[h].near, group[h].at[0])
        across(h, 3, high)
        across(h, 1, low)

    def gather_far(h):
        links.wait(shares[h].far, group[h].at[0])
        across(h, 2, low)
        across(h, 2, high)

    def gather_done(h):
        links.wait(twins[h], group[h].at[pl.ds(0, 4)])

    loads[0].wait()
    gather_load(0)
    met()
    gather_push(0)
    gather_load(1)

    loads[1].wait()
    loads[2].wait()
    table_buf[...] = jnp.zeros_like(table_buf)
    for i in (0, 1):
        table_buf[i : i + 1, 0:slots] = ids_buf[i]
    by_row, by_col = table_buf[0:1, :], table_buf[1:2, :]
    loads[6].wait()
    count = count_buf[0]
    order = slot_order(by_row, by_col, count, slots) + slot_order(by_col, by_row, count, slots)
    for i, line in enumerate(order):
        table_buf[i : i + 1, :] = line
    to_scalars = pltpu.make_async_copy(table_buf, table, local_sem.at[7])
    to_scalars.start()
    for sums_to in (running, *running_back):
        sums_to[slots] = jnp.zeros(sums_to.shape[1:], BF16)

    def tile_pass(source, running, backward, between=lambda: None):
        base = 4 if backward else 0
        contract = ((1,), (0,)) if backward else ((1,), (1,))

        def step(block, acc):
            products = []
            for k in range(UNROLL):
                at = block * UNROLL + k
                node = table[base + 1, at]
                products.append(
                    lax.dot_general(
                        source[lax.div(node, tiles), lax.rem(node, tiles)],
                        adj[table[base, at]],
                        (contract, ((), ())),
                        preferred_element_type=F32,
                    )
                )
            for k in range(UNROLL):
                at = block * UNROLL + k
                acc = acc * table[base + 2, at].astype(F32) + products[k]
                running[at] = acc.astype(BF16)
            return acc

        steps = slots // UNROLL
        acc = lax.fori_loop(0, steps // 2, step, jnp.zeros(running.shape[1:], F32))
        between()
        lax.fori_loop(steps // 2, steps, step, acc)

    def pick(target, running, base, block):
        picked = [running[table[base + 3, block * tiles + t]] for t in range(tiles)]
        for t in range(tiles):
            target[block, t] = picked[t]

    firsts, seconds = (here.z, here.x), (here.x, here.z)
    node_slices = [pl.ds(a * (tiles // 2), tiles // 2) for a in node_halves]

    def col_of(a, first, second):
        return second * RING + first if a == 0 else first * RING + second

    passing, arrived = (
        [[links.semaphore() for _ in range(RING)] for _ in feature_halves] for _ in range(2)
    )
    passing_2, arrived_2 = ([links.semaphore() for _ in feature_halves] for _ in range(2))
    phases = [links.phase(parts.at[h, pl.ds(0, 15)]) for h in feature_halves]

    def sum_first(h, a, delta):
        first, second = firsts[a], seconds[a]

        def part(k):
            return parts.at[h, col_of(a, first.at(k), second.at(delta)), node_slices[a]]

        return Sum4(
            links, first, part, relay_buf.at[h, delta, a], from_buf.at[h, delta, a],
            passing[h][delta], arrived[h][delta], phases[h],
        )

    def sum_second(h, a):
        return Sum4(
            links, seconds[a], lambda k: part2_buf.at[h, a, k], relay2_buf.at[h, a],
            from2_buf.at[h, a], passing_2[h], arrived_2[h], phases[h],
        )

    first_sums = [
        [[sum_first(h, a, d) for d in range(RING)] for a in node_halves] for h in feature_halves
    ]
    last_sums = [[sum_second(h, a) for a in node_halves] for h in feature_halves]

    def push_first(h, d):
        for a in node_halves:
            first_sums[h][a][d].push()

    def relay_first(h, d):
        links.wait(passing[h][d], relay_buf.at[h, d])
        for a in node_halves:
            first_sums[h][a][d].relay()

    def wait_first(h, d):
        links.wait(arrived[h][d], from_buf.at[h, d])

    def done_first(h, a, d):
        part2_buf[h, a, d] = first_sums[h][a][d].total().astype(BF16)

    def scatter_start(h):
        lax.fori_loop(0, RING * RING, lambda b, _: (pick(parts.at[h], running, 0, b), 0)[1], 0)
        for d in (2, 1, 3, 0):
            push_first(h, d)

    def scatter_relay(h):
        for d in (2, 1, 3, 0):
            relay_first(h, d)

    def scatter_far(h):
        wait_first(h, 2)
        for a in node_halves:
            done_first(h, a, 2)
            last_sums[h][a].push_far()

    def scatter_near(h):
        wait_first(h, 1)
        for a in node_halves:
            done_first(h, a, 1)
            last_sums[h][a].push_up()
        wait_first(h, 3)
        for a in node_halves:
            done_first(h, a, 3)
            last_sums[h][a].push_down()

    def scatter_end(h):
        links.wait(passing_2[h], relay2_buf.at[h])
        for a in node_halves:
            last_sums[h][a].relay()
        wait_first(h, 0)
        for a in node_halves:
            done_first(h, a, 0)

    gather_relay(0)
    gather_push(1)
    gather_near(0)
    gather_far(0)
    gather_relay(1)
    gather_done(0)
    to_scalars.wait()
    loads[3].wait()

    def gather_rest():
        gather_near(1)
        gather_far(1)

    tile_pass(group[0], running, False, gather_rest)
    scatter_start(0)
    gather_done(1)
    tile_pass(group[1], running, False)
    scatter_start(1)
    scatter_relay(0)
    loads[4].wait()
    loads[5].wait()
    for t in range(tiles):
        cot_t[t] = cot_buf[tile_rows(t), :].astype(F32).T
    scatter_relay(1)
    scatter_far(0)
    scatter_far(1)
    scatter_near(0)
    scatter_near(1)
    scatter_end(0)
    scatter_end(1)

    weight = weight_buf[...]

    def dense(a):
        whole = [last_sums[h][a].total().astype(BF16) for h in feature_halves]
        for i in range(tiles // 2):
            t = a * (tiles // 2) + i
            hidden = jnp.concatenate([whole[0][i], whole[1][i]], axis=0)
            pre_act = lax.dot_general(
                weight, hidden, (((0,), (0,)), ((), ())), preferred_element_type=F32
            )
            value, slope = activation(pre_act)
            pre_grad = (cot_t[t] * slope).astype(BF16)
            own = jnp.dot(weight, pre_grad, preferred_element_type=F32).astype(BF16)
            for h in feature_halves:
                grads[h][here.col, t] = own[offsets[h] : offsets[h] + BACK_WIDTHS[h]]
            value_buf[t] = value
            hidden_buf[t] = hidden
            grad_buf[t] = pre_grad

    share_phases = [links.phase(grads[h].at[pl.ds(0, 15)]) for h in feature_halves]
    one_sems = [[links.semaphore() for _ in range(3)] for _ in feature_halves]
    two_sems = [[links.semaphore() for _ in range(RING)] for _ in feature_halves]
    rest_sems = [links.semaphore() for _ in feature_halves]

    def share_first(h, a):
        first, second = seconds[a], firsts[a]
        return Share4(
            links,
            first,
            lambda k: grads[h].at[col_of(1 - a, first.at(k), second.position), node_slices[a]],
            tiles // 4,
            *one_sems[h],
            share_phases[h],
        )

    def share_second(h, a, delta):
        first, second = seconds[a], firsts[a]
        return Share4(
            links,
            second,
            lambda k: grads[h].at[col_of(1 - a, first.at(delta), second.at(k)), node_slices[a]],
            tiles // 4,
            two_sems[h][delta],
            rest_sems[h],
            rest_sems[h],
            share_phases[h],
        )

    ones = [[share_first(h, a) for a in node_halves] for h in feature_halves]
    twos = [
        [[share_second(h, a, d) for a in node_halves] for d in range(RING)] for h in feature_halves
    ]

    def one_push(h):
        for share in ones[h]:
            share.push()

    def one_wait(h, which):
        links.wait(one_sems[h][which], grads[h].at[0])

    def one_relay(h):
        one_wait(h, 0)
        for share in ones[h]:
            share.relay()

    def two_push(h, *offsets):
        for d in offsets:
            for share in twos[h][d]:
                share.push()

    def two_relay(h, *offsets):
        for d in offsets:
            links.wait(two_sems[h][d], grads[h].at[0])
            for share in twos[h][d]:
                share.relay()

    def shared(h):
        links.wait(rest_sems[h], grads[h].at[pl.ds(0, 8)])

    back_phases = [links.phase(grads[h].at[pl.ds(0, 7)]) for h in feature_halves]
    passing_3, arrived_3 = ([links.semaphore() for _ in feature_halves] for _ in range(2))
    swapped = [[links.semaphore() for _ in range(RING)] for _ in feature_halves]
    totals = [
        Sum4(
            links, here.y, lambda k, h=h: own_buf[h].at[k], relay3_buf[h], from3_buf[h],
            passing_3[h], arrived_3[h], back_phases[h],
        )
        for h in feature_halves
    ]
    near_order = (2, 1, 3, 0)

    def block(h, k, core):
        return sums[h].at[here.y.at(k) * 2 + core]

    def back_swap(h):
        for k in near_order:
            pick(sums[h], running_back[h], 4, here.y.at(k) * 2 + 1 - here.core)
            links.start(
                block(h, k, 1 - here.core), twin_buf[h].at[k], here.sibling, swapped[h][k],
                back_phases[h],
            )
        for k in near_order:
            pick(sums[h], running_back[h], 4, here.y.at(k) * 2 + here.core)

    def back_push(h):
        pushes = {2: totals[h].push_far, 1: totals[h].push_up, 3: totals[h].push_down}
        for k in near_order:
            links.wait(swapped[h][k], twin_buf[h].at[k])
            own = block(h, k, here.core)[...].astype(F32) + twin_buf[h][k].astype(F32)
            own_buf[h][k] = own.astype(BF16)
            if k in pushes:
                pushes[k]()

    def back_relay(h):
        links.wait(passing_3[h], relay3_buf[h])
        totals[h].relay()

    def back_end(h):
        links.wait(arrived_3[h], from3_buf[h])
        whole = totals[h].total()
        for t in range(tiles):
            feature_grad[tile_rows(t), pl.ds(offsets[h], BACK_WIDTHS[h])] = whole[t].T.astype(BF16)

    for h in feature_halves:
        links.wait(arrived_2[h], from2_buf.at[h])
    for a in node_halves:
        dense(a)
        ones[0][a].push()
        twos[0][0][a].push()
    for t in range(tiles):
        term = lax.dot_general(
            hidden_buf[t], grad_buf[t], (((1,), (1,)), ((), ())), preferred_element_type=F32
        ).reshape(term_buf.shape)
        if t == 0:
            term_buf[...] = term
        else:
            term_buf[...] += term
    stores = [
        pltpu.make_async_copy(src, dst, local_sem.at[8 + i])
        for i, (src, dst) in enumerate(
            ((out_buf, out_ref), (weight_grad, weight_grad_ref), (feature_grad, feature_grad_ref))
        )
    ]
    weights = SumAll(
        links, here, term_buf, weight_grad, term_relay, term_from, term_own, term_got
    )
    weights.next()
    one_relay(0)
    one_wait(0, 1)
    two_push(0, 1, 3)
    weights.next()
    one_push(1)
    two_relay(0, 0)
    one_wait(0, 2)
    two_push(0, 2)
    weights.next()
    two_push(1, 0)
    two_relay(0, 1, 3)
    one_relay(1)
    weights.next()
    two_relay(0, 2)
    one_wait(1, 1)
    two_push(1, 1, 3)
    two_relay(1, 0)
    one_wait(1, 2)
    two_push(1, 2)
    shared(0)
    tile_pass(grads[0], running_0, True)
    two_relay(1, 1, 3)
    back_swap(0)
    two_relay(1, 2)
    weights.next()
    back_push(0)
    weights.next()
    shared(1)
    tile_pass(grads[1], running_1, True)
    back_swap(1)
    back_relay(0)
    back_push(1)
    weights.next()
    weights.next()
    for t in range(tiles):
        out_buf[tile_rows(t), :] = value_buf[t].T.astype(BF16)
    stores[0].start()
    weights.next()
    back_relay(1)
    back_end(0)
    weights.next()
    stores[1].start()
    back_end(1)
    stores[2].start()
    links.drain()
    for store in stores:
        store.wait()


def copy_kernel(*refs):
    count = (len(refs) - 2) // 3
    sources, targets, held = (refs[i * count : (i + 1) * count] for i in range(3))
    came, left = refs[-2:]
    into = [pltpu.make_async_copy(sources[i], held[i], came.at[i]) for i in range(count)]
    out = [pltpu.make_async_copy(held[i], targets[i], left.at[i]) for i in range(count)]
    for copy in into:
        copy.start()
    for first, second in zip(into, out):
        first.wait()
        second.start()
    for copy in out:
        copy.wait()


def shards(features, weight, adj_tiles, tile_rows, tile_cols, tile_count, cotangent):
    nodes, width = features.shape
    slots, tile = adj_tiles.shape[:2]
    n_row, n_col = lax.axis_size("row"), lax.axis_size("col")
    tiles, half, member = nodes // tile, width // 2, width // RING
    one = (half, tile)
    backs = [(back, tile) for back in BACK_WIDTHS]

    def vmem(*shape, dtype=BF16):
        return pltpu.VMEM(shape, dtype)

    anywhere = pl.BlockSpec(memory_space=pl.ANY)
    results = pl.pallas_call(
        layer_kernel,
        out_shape=(
            jax.ShapeDtypeStruct((nodes, width), BF16),
            jax.ShapeDtypeStruct((RING, member, width), F32),
            jax.ShapeDtypeStruct((nodes, width), BF16),
        ),
        in_specs=[anywhere] * 7,
        out_specs=(anywhere,) * 3,
        scratch_shapes=[
            vmem(nodes, width),
            vmem(width, width),
            vmem(slots, tile, tile),
            vmem(2, 1, slots, dtype=jnp.int32),
            vmem(nodes, width),
            vmem(8, 128, dtype=jnp.int32),
            pltpu.SMEM((8, 128), jnp.int32),
            vmem(n_row, tiles, *one),
            vmem(n_row, tiles, *one),
            vmem(slots + 1, *one),
            *(vmem(slots + 1, *back) for back in backs),
            vmem(2, n_col, tiles, *one),
            vmem(2, RING, 2, 2, tiles // 4, *one),
            vmem(2, RING, 2, 2, tiles // 2, *one),
            vmem(2, 2, RING, tiles // 2, *one),
            vmem(2, 2, 2, tiles // 4, *one),
            vmem(2, 2, 2, tiles // 2, *one),
            vmem(tiles, width, tile, dtype=F32),
            vmem(tiles, width, tile),
            vmem(tiles, width, tile),
            vmem(tiles, width, tile, dtype=F32),
            *(vmem(n_col, tiles, *back) for back in backs),
            vmem(RING, member, width, dtype=F32),
            vmem(2, member // 2, width, dtype=F32),
            vmem(2, member, width, dtype=F32),
            vmem(11, member, width, dtype=F32),
            vmem(5, member, width, dtype=F32),
            *(vmem(n_row, tiles, *back) for back in backs),
            *(vmem(RING, tiles, *back) for back in backs),
            *(vmem(RING, tiles, *back) for back in backs),
            *(vmem(2, tiles // 2, *back) for back in backs),
            *(vmem(2, tiles, *back) for back in backs),
            vmem(nodes, width),
            vmem(RING, member, width, dtype=F32),
            vmem(nodes, width),
            pltpu.SMEM((1,), jnp.int32),
            pltpu.SemaphoreType.DMA((11,)),
            pltpu.SemaphoreType.DMA((9,)),
            pltpu.SemaphoreType.DMA((65,)),
        ],
        compiler_params=pltpu.CompilerParams(
            vmem_limit_bytes=VMEM_BYTES, collective_id=0, has_side_effects=True
        ),
        name="layer",
    )(
        tile_count, features, weight, adj_tiles,
        tile_rows.reshape(1, slots), tile_cols.reshape(1, slots), cotangent,
    )
    out_features, weight_grad, feature_grad = pl.pallas_call(
        copy_kernel,
        out_shape=tuple(jax.ShapeDtypeStruct(r.shape, r.dtype) for r in results),
        in_specs=[anywhere] * 3,
        out_specs=(anywhere,) * 3,
        scratch_shapes=[pltpu.VMEM(r.shape, r.dtype) for r in results]
        + [pltpu.SemaphoreType.DMA((3,))] * 2,
        compiler_params=pltpu.CompilerParams(vmem_limit_bytes=VMEM_BYTES),
        name="results",
    )(*results)
    return (out_features, weight_grad.reshape(width, width), feature_grad)


def solution(mesh):
    in_specs = (
        P(("row", "col"), None),
        P(),
        P(("row", "col"), None, None),
        P(("row", "col")),
        P(("row", "col")),
        P(("row", "col")),
        P(("row", "col"), None),
    )
    out_specs = (P(("row", "col"), None), P(), P(("row", "col"), None))
    return jax.shard_map(shards, mesh=mesh, in_specs=in_specs, out_specs=out_specs, check_vma=False)
```

```python
import jax
import jax.numpy as jnp
from jax import lax
from jax.experimental import pallas as pl
from jax.experimental.pallas import tpu as pltpu
from jax.sharding import PartitionSpec as P

MESH = pl.DeviceIdType.MESH
BF16, F32 = jnp.bfloat16, jnp.float32
VMEM_BYTES = 63 * 2**20
RING = 4
UNROLL = 48
BACK_WIDTHS = (64, 64)


class Links:
    def __init__(self, send_sem, recv_sem):
        self.send_sem, self.recv_sem = send_sem, recv_sem
        self.used, self.phases = 0, []

    def semaphore(self):
        self.used += 1
        return self.recv_sem.at[self.used - 1]

    def phase(self, ref):
        self.phases.append(ref)
        return len(self.phases) - 1

    def start(self, src, dst, device, arrived, phase):
        pltpu.make_async_remote_copy(
            src_ref=src,
            dst_ref=dst,
            send_sem=self.send_sem.at[phase],
            recv_sem=arrived,
            device_id=device,
            device_id_type=MESH,
        ).start()

    def wait(self, arrived, ref):
        pltpu.make_async_copy(ref, ref, arrived).wait()

    def drain(self):
        for at, ref in enumerate(self.phases):
            self.wait(self.send_sem.at[at], ref)


class Axis:
    def __init__(self, position, device_at):
        self.position = position
        self.up = device_at(lax.rem(position + 1, RING))
        self.down = device_at(lax.rem(position + 3, RING))
        odd = lax.rem(position, 2)
        self.pair = device_at(position + 1 - 2 * odd)
        self.other_pair = device_at(lax.rem(position + 3 + 2 * odd, RING))

    def at(self, offset):
        return lax.rem(self.position + offset, RING) if offset else self.position


class Place:
    def __init__(self):
        row, col = lax.axis_index("row"), lax.axis_index("col")
        self.row, self.col = row, col
        y, self.core = lax.div(row, 2), lax.rem(row, 2)
        x, z = lax.div(col, RING), lax.rem(col, RING)
        core = self.core
        self.y = Axis(y, lambda k: (k * 2 + core, col))
        self.x = Axis(x, lambda k: (row, k * RING + z))
        self.z = Axis(z, lambda k: (row, x * RING + k))
        self.sibling_row = row + 1 - 2 * core
        self.sibling = (self.sibling_row, col)

    def greet(self):
        barrier = pltpu.get_barrier_semaphore()
        others = [d for axis in (self.x, self.y, self.z) for d in (axis.up, axis.down)]
        others.append(self.sibling)
        for other in others:
            pl.semaphore_signal(barrier, inc=1, device_id=other, device_id_type=MESH)
        return lambda: pl.semaphore_wait(barrier, len(others))


def add_to(ref, value):
    ref[...] = (ref[...].astype(F32) + value.astype(F32)).astype(ref.dtype)


class Sum4:
    def __init__(self, links, axis, part, relays, blocks, passing, arrived, phase):
        self.links, self.axis, self.part = links, axis, part
        self.relay_up, self.relay_down = relays.at[0], relays.at[1]
        self.from_down, self.from_up = blocks.at[0], blocks.at[1]
        self.passing, self.arrived, self.phase = passing, arrived, phase
        half = relays.shape[1]
        self.low, self.high = pl.ds(0, half), pl.ds(half, half)

    def send(self, src, dst, device, arrived):
        self.links.start(src, dst, device, arrived, self.phase)

    def push_far(self):
        far = self.part(2)
        self.send(far.at[self.low], self.relay_up, self.axis.up, self.passing)
        self.send(far.at[self.high], self.relay_down, self.axis.down, self.passing)

    def push_up(self):
        near = self.part(1).at[self.high]
        self.send(near, self.from_down.at[self.high], self.axis.up, self.arrived)

    def push_down(self):
        near = self.part(3).at[self.low]
        self.send(near, self.from_up.at[self.low], self.axis.down, self.arrived)

    def push(self):
        self.push_far()
        self.push_up()
        self.push_down()

    def relay(self):
        add_to(self.relay_up, self.part(1)[self.low])
        self.send(self.relay_up, self.from_down.at[self.low], self.axis.up, self.arrived)
        add_to(self.relay_down, self.part(3)[self.high])
        self.send(self.relay_down, self.from_up.at[self.high], self.axis.down, self.arrived)

    def total(self):
        return (
            self.part(0)[...].astype(F32)
            + self.from_down[...].astype(F32)
            + self.from_up[...].astype(F32)
        )


class Share4:
    def __init__(self, links, axis, slot, half, first, near, far, phase):
        self.links, self.axis, self.slot = links, axis, slot
        self.first, self.near, self.far, self.phase = first, near, far, phase
        self.low, self.high = pl.ds(0, half), pl.ds(half, half)

    def send(self, k, rows, device, arrived):
        ref = self.slot(k).at[rows]
        self.links.start(ref, ref, device, arrived, self.phase)

    def push(self):
        self.send(0, self.low, self.axis.up, self.first)
        self.send(0, self.high, self.axis.down, self.first)
        self.send(0, self.high, self.axis.up, self.near)
        self.send(0, self.low, self.axis.down, self.near)

    def relay(self):
        self.send(3, self.low, self.axis.up, self.far)
        self.send(1, self.high, self.axis.down, self.far)


class SumAll:
    def __init__(self, links, here, term, result, relay, came, own, got):
        y = here.y
        self.links, self.own, self.got, self.relays, self.came = links, own, got, relay, came
        self.result = result
        phase = links.phase(own)
        passing, arrived, self.first, self.rest = (links.semaphore() for _ in range(4))
        self.ring = Sum4(links, y, lambda k: term.at[y.at(k)], relay, came, passing, arrived, phase)
        self.share = Share4(
            links, y, lambda k: result.at[y.at(k)], result.shape[1] // 2,
            self.first, self.rest, self.rest, phase,
        )
        self.slot = result.at[y.position]
        pairs = (here.sibling, here.x.pair, here.z.pair, here.x.other_pair, here.z.other_pair)
        self.steps = self.run(pairs)

    def run(self, pairs):
        links, ring, share = self.links, self.ring, self.share
        ring.push()
        yield
        links.wait(ring.passing, self.relays)
        ring.relay()
        yield
        links.wait(ring.arrived, self.came)
        total = ring.total()
        for at, pair in enumerate(pairs):
            self.own[at] = total
            arrived = links.semaphore()
            links.start(self.own.at[at], self.got.at[at], pair, arrived, ring.phase)
            yield
            links.wait(arrived, self.got.at[at])
            total = self.own[at] + self.got[at]
        self.slot[...] = total
        share.push()
        yield
        links.wait(self.first, self.result.at[0])
        share.relay()
        yield
        links.wait(self.rest, self.result.at[pl.ds(0, 2)])

    def next(self):
        next(self.steps, None)


def activation(value):
    root = 0.7978845608028654
    square = value * value
    t = jnp.tanh(root * (value + 0.044715 * (value * square)))
    half = 0.5 * (1.0 + t)
    slope = half + (0.5 * value) * (1.0 - t * t) * (root * (1.0 + 3.0 * 0.044715 * square))
    return value * half, slope


def spread(row):
    wide = jnp.broadcast_to(row, (row.shape[1], row.shape[1]))
    return wide, wide.T


def slot_order(key, source, count, empty):
    lanes = key.shape[1]
    lane = lax.broadcasted_iota(jnp.int32, (lanes, lanes), 1)
    sub = lax.broadcasted_iota(jnp.int32, (lanes, lanes), 0)
    at = lax.broadcasted_iota(jnp.int32, (1, lanes), 1)
    key = jnp.where(at < count, key, 2 * lanes)

    def over(mask, value):
        return jnp.sum(jnp.where(mask, value, 0), axis=0, keepdims=True)

    unique_row, unique_col = spread(key * lanes + at)
    _, rank = spread(over(unique_col < unique_row, 1))
    _, key_col = spread(key)
    _, source_col = spread(source)
    hit = rank == lane
    slot, source, sorted_key = over(hit, sub), over(hit, source_col), over(hit, key_col)
    same = over((rank == lane - 1) & (key_col == sorted_key), 1)
    last = jnp.where(over(key_col == lane, 1) > 0, over(key_col <= lane, 1) - 1, empty)
    return slot, source, same, last


def layer_kernel(
    count_ref, features_ref, weight_ref, adj_ref, rows_ref, cols_ref, cot_ref,
    out_ref, weight_grad_ref, feature_grad_ref,
    x_buf, weight_buf, adj, ids_buf, cot_buf, table_buf, table,
    group_0, group_1, running, running_0, running_1, parts, relay_buf, from_buf, part2_buf, relay2_buf, from2_buf,
    cot_t, hidden_buf, grad_buf, value_buf, grads_0, grads_1,
    term_buf, term_relay, term_from, term_own, term_got,
    sums_0, sums_1, own_0, own_1, twin_0, twin_1, relay3_0, relay3_1, from3_0, from3_1,
    out_buf, weight_grad, feature_grad, count_buf, local_sem, send_sem, recv_sem,
):
    here = Place()
    group, grads = (group_0, group_1), (grads_0, grads_1)
    running_back, sums, own_buf = (running_0, running_1), (sums_0, sums_1), (own_0, own_1)
    twin_buf, relay3_buf = (twin_0, twin_1), (relay3_0, relay3_1)
    from3_buf = (from3_0, from3_1)
    offsets = (0, BACK_WIDTHS[0])
    tiles, width, tile = parts.shape[2], parts.shape[3], parts.shape[4]
    slots = adj.shape[0]
    links = Links(send_sem, recv_sem)
    loads = [
        pltpu.make_async_copy(src, dst, local_sem.at[i])
        for i, (src, dst) in enumerate(
            (
                (features_ref, x_buf),
                (rows_ref, ids_buf.at[0]),
                (cols_ref, ids_buf.at[1]),
                (adj_ref, adj),
                (weight_ref, weight_buf),
                (cot_ref, cot_buf),
                (count_ref, count_buf),
            )
        )
    ]
    for load in loads:
        load.start()
    met = here.greet()
    feature_halves = node_halves = (0, 1)

    def tile_rows(t):
        return pl.ds(t * tile, tile)

    def row_slot(h, k):
        return group[h].at[here.y.at(k) * 2 + here.core]

    def share_row(h):
        first, near, far = (links.semaphore() for _ in range(3))
        phase = links.phase(parts.at[h, pl.ds(0, 7)])
        return Share4(
            links, here.y, lambda k: row_slot(h, k), tiles // 2, first, near, far, phase
        )

    shares = [share_row(h) for h in feature_halves]
    twins = [links.semaphore() for _ in feature_halves]
    low, high = shares[0].low, shares[0].high

    def across(h, k, rows):
        ref = row_slot(h, k).at[rows]
        links.start(ref, ref, here.sibling, twins[h], shares[h].phase)

    def gather_load(h):
        for t in range(tiles):
            block = x_buf[tile_rows(t), pl.ds(h * width, width)]
            group[h][here.row, t] = block.astype(F32).T.astype(BF16)

    def gather_push(h):
        shares[h].push()
        across(h, 0, low)
        across(h, 0, high)

    def gather_relay(h):
        links.wait(shares[h].first, group[h].at[0])
        shares[h].relay()
        across(h, 3, low)
        across(h, 1, high)

    def gather_near(h):
        links.wait(shares[h].near, group[h].at[0])
        across(h, 3, high)
        across(h, 1, low)

    def gather_far(h):
        links.wait(shares[h].far, group[h].at[0])
        across(h, 2, low)
        across(h, 2, high)

    def gather_done(h):
        links.wait(twins[h], group[h].at[pl.ds(0, 4)])

    loads[0].wait()
    gather_load(0)
    met()
    gather_push(0)
    gather_load(1)

    loads[1].wait()
    loads[2].wait()
    table_buf[...] = jnp.zeros_like(table_buf)
    for i in (0, 1):
        table_buf[i : i + 1, 0:slots] = ids_buf[i]
    by_row, by_col = table_buf[0:1, :], table_buf[1:2, :]
    loads[6].wait()
    count = count_buf[0]
    order = slot_order(by_row, by_col, count, slots) + slot_order(by_col, by_row, count, slots)
    for i, line in enumerate(order):
        table_buf[i : i + 1, :] = line
    to_scalars = pltpu.make_async_copy(table_buf, table, local_sem.at[7])
    to_scalars.start()
    for sums_to in (running, *running_back):
        sums_to[slots] = jnp.zeros(sums_to.shape[1:], BF16)

    def tile_pass(source, running, backward, between=lambda: None):
        base = 4 if backward else 0
        contract = ((1,), (0,)) if backward else ((1,), (1,))

        def step(block, acc):
            products = []
            for k in range(UNROLL):
                at = block * UNROLL + k
                node = table[base + 1, at]
                products.append(
                    lax.dot_general(
                        source[lax.div(node, tiles), lax.rem(node, tiles)],
                        adj[table[base, at]],
                        (contract, ((), ())),
                        preferred_element_type=F32,
                    )
                )
            for k in range(UNROLL):
                at = block * UNROLL + k
                acc = acc * table[base + 2, at].astype(F32) + products[k]
                running[at] = acc.astype(BF16)
            return acc

        steps = slots // UNROLL
        acc = lax.fori_loop(0, steps // 2, step, jnp.zeros(running.shape[1:], F32))
        between()
        lax.fori_loop(steps // 2, steps, step, acc)

    def pick(target, running, base, block):
        picked = [running[table[base + 3, block * tiles + t]] for t in range(tiles)]
        for t in range(tiles):
            target[block, t] = picked[t]

    firsts, seconds = (here.z, here.x), (here.x, here.z)
    node_slices = [pl.ds(a * (tiles // 2), tiles // 2) for a in node_halves]

    def col_of(a, first, second):
        return second * RING + first if a == 0 else first * RING + second

    passing, arrived = (
        [[links.semaphore() for _ in range(RING)] for _ in feature_halves] for _ in range(2)
    )
    passing_2, arrived_2 = ([links.semaphore() for _ in feature_halves] for _ in range(2))
    phases = [links.phase(parts.at[h, pl.ds(0, 15)]) for h in feature_halves]

    def sum_first(h, a, delta):
        first, second = firsts[a], seconds[a]

        def part(k):
            return parts.at[h, col_of(a, first.at(k), second.at(delta)), node_slices[a]]

        return Sum4(
            links, first, part, relay_buf.at[h, delta, a], from_buf.at[h, delta, a],
            passing[h][delta], arrived[h][delta], phases[h],
        )

    def sum_second(h, a):
        return Sum4(
            links, seconds[a], lambda k: part2_buf.at[h, a, k], relay2_buf.at[h, a],
            from2_buf.at[h, a], passing_2[h], arrived_2[h], phases[h],
        )

    first_sums = [
        [[sum_first(h, a, d) for d in range(RING)] for a in node_halves] for h in feature_halves
    ]
    last_sums = [[sum_second(h, a) for a in node_halves] for h in feature_halves]

    def push_first(h, d):
        for a in node_halves:
            first_sums[h][a][d].push()

    def relay_first(h, d):
        links.wait(passing[h][d], relay_buf.at[h, d])
        for a in node_halves:
            first_sums[h][a][d].relay()

    def wait_first(h, d):
        links.wait(arrived[h][d], from_buf.at[h, d])

    def done_first(h, a, d):
        part2_buf[h, a, d] = first_sums[h][a][d].total().astype(BF16)

    def scatter_start(h):
        lax.fori_loop(0, RING * RING, lambda b, _: (pick(parts.at[h], running, 0, b), 0)[1], 0)
        for d in (2, 1, 3, 0):
            push_first(h, d)

    def scatter_relay(h):
        for d in (2, 1, 3, 0):
            relay_first(h, d)

    def scatter_far(h):
        wait_first(h, 2)
        for a in node_halves:
            done_first(h, a, 2)
            last_sums[h][a].push_far()

    def scatter_near(h):
        wait_first(h, 1)
        for a in node_halves:
            done_first(h, a, 1)
            last_sums[h][a].push_up()
        wait_first(h, 3)
        for a in node_halves:
            done_first(h, a, 3)
            last_sums[h][a].push_down()

    def scatter_end(h):
        links.wait(passing_2[h], relay2_buf.at[h])
        for a in node_halves:
            last_sums[h][a].relay()
        wait_first(h, 0)
        for a in node_halves:
            done_first(h, a, 0)

    gather_relay(0)
    gather_push(1)
    gather_near(0)
    gather_far(0)
    gather_relay(1)
    gather_done(0)
    to_scalars.wait()
    loads[3].wait()

    def gather_rest():
        gather_near(1)
        gather_far(1)

    tile_pass(group[0], running, False, gather_rest)
    scatter_start(0)
    gather_done(1)
    tile_pass(group[1], running, False)
    scatter_start(1)
    scatter_relay(0)
    loads[4].wait()
    loads[5].wait()
    for t in range(tiles):
        cot_t[t] = cot_buf[tile_rows(t), :].astype(F32).T
    scatter_relay(1)
    scatter_far(0)
    scatter_far(1)
    scatter_near(0)
    scatter_near(1)
    scatter_end(0)
    scatter_end(1)

    weight = weight_buf[...]

    def dense(a):
        whole = [last_sums[h][a].total().astype(BF16) for h in feature_halves]
        for i in range(tiles // 2):
            t = a * (tiles // 2) + i
            hidden = jnp.concatenate([whole[0][i], whole[1][i]], axis=0)
            pre_act = lax.dot_general(
                weight, hidden, (((0,), (0,)), ((), ())), preferred_element_type=F32
            )
            value, slope = activation(pre_act)
            pre_grad = (cot_t[t] * slope).astype(BF16)
            own = jnp.dot(weight, pre_grad, preferred_element_type=F32).astype(BF16)
            for h in feature_halves:
                grads[h][here.col, t] = own[offsets[h] : offsets[h] + BACK_WIDTHS[h]]
            value_buf[t] = value
            hidden_buf[t] = hidden
            grad_buf[t] = pre_grad

    share_phases = [links.phase(grads[h].at[pl.ds(0, 15)]) for h in feature_halves]
    one_sems = [[links.semaphore() for _ in range(3)] for _ in feature_halves]
    two_sems = [[links.semaphore() for _ in range(RING)] for _ in feature_halves]
    rest_sems = [links.semaphore() for _ in feature_halves]

    def share_first(h, a):
        first, second = seconds[a], firsts[a]
        return Share4(
            links,
            first,
            lambda k: grads[h].at[col_of(1 - a, first.at(k), second.position), node_slices[a]],
            tiles // 4,
            *one_sems[h],
            share_phases[h],
        )

    def share_second(h, a, delta):
        first, second = seconds[a], firsts[a]
        return Share4(
            links,
            second,
            lambda k: grads[h].at[col_of(1 - a, first.at(delta), second.at(k)), node_slices[a]],
            tiles // 4,
            two_sems[h][delta],
            rest_sems[h],
            rest_sems[h],
            share_phases[h],
        )

    ones = [[share_first(h, a) for a in node_halves] for h in feature_halves]
    twos = [
        [[share_second(h, a, d) for a in node_halves] for d in range(RING)] for h in feature_halves
    ]

    def one_push(h):
        for share in ones[h]:
            share.push()

    def one_wait(h, which):
        links.wait(one_sems[h][which], grads[h].at[0])

    def one_relay(h):
        one_wait(h, 0)
        for share in ones[h]:
            share.relay()

    def two_push(h, *offsets):
        for d in offsets:
            for share in twos[h][d]:
                share.push()

    def two_relay(h, *offsets):
        for d in offsets:
            links.wait(two_sems[h][d], grads[h].at[0])
            for share in twos[h][d]:
                share.relay()

    def shared(h):
        links.wait(rest_sems[h], grads[h].at[pl.ds(0, 8)])

    back_phases = [links.phase(grads[h].at[pl.ds(0, 7)]) for h in feature_halves]
    passing_3, arrived_3 = ([links.semaphore() for _ in feature_halves] for _ in range(2))
    swapped = [[links.semaphore() for _ in range(RING)] for _ in feature_halves]
    totals = [
        Sum4(
            links, here.y, lambda k, h=h: own_buf[h].at[k], relay3_buf[h], from3_buf[h],
            passing_3[h], arrived_3[h], back_phases[h],
        )
        for h in feature_halves
    ]
    near_order = (2, 1, 3, 0)

    def block(h, k, core):
        return sums[h].at[here.y.at(k) * 2 + core]

    def back_swap(h):
        for k in near_order:
            pick(sums[h], running_back[h], 4, here.y.at(k) * 2 + 1 - here.core)
            links.start(
                block(h, k, 1 - here.core), twin_buf[h].at[k], here.sibling, swapped[h][k],
                back_phases[h],
            )
        for k in near_order:
            pick(sums[h], running_back[h], 4, here.y.at(k) * 2 + here.core)

    def back_push(h):
        pushes = {2: totals[h].push_far, 1: totals[h].push_up, 3: totals[h].push_down}
        for k in near_order:
            links.wait(swapped[h][k], twin_buf[h].at[k])
            own = block(h, k, here.core)[...].astype(F32) + twin_buf[h][k].astype(F32)
            own_buf[h][k] = own.astype(BF16)
            if k in pushes:
                pushes[k]()

    def back_relay(h):
        links.wait(passing_3[h], relay3_buf[h])
        totals[h].relay()

    def back_end(h):
        links.wait(arrived_3[h], from3_buf[h])
        whole = totals[h].total()
        for t in range(tiles):
            feature_grad[tile_rows(t), pl.ds(offsets[h], BACK_WIDTHS[h])] = whole[t].T.astype(BF16)

    for h in feature_halves:
        links.wait(arrived_2[h], from2_buf.at[h])
    for a in node_halves:
        dense(a)
        ones[0][a].push()
        twos[0][0][a].push()
    for t in range(tiles):
        term = lax.dot_general(
            hidden_buf[t], grad_buf[t], (((1,), (1,)), ((), ())), preferred_element_type=F32
        ).reshape(term_buf.shape)
        if t == 0:
            term_buf[...] = term
        else:
            term_buf[...] += term
    stores = [
        pltpu.make_async_copy(src, dst, local_sem.at[8 + i])
        for i, (src, dst) in enumerate(
            ((out_buf, out_ref), (weight_grad, weight_grad_ref), (feature_grad, feature_grad_ref))
        )
    ]
    weights = SumAll(
        links, here, term_buf, weight_grad, term_relay, term_from, term_own, term_got
    )
    weights.next()
    one_relay(0)
    one_wait(0, 1)
    two_push(0, 1, 3)
    weights.next()
    one_push(1)
    two_relay(0, 0)
    one_wait(0, 2)
    two_push(0, 2)
    weights.next()
    two_push(1, 0)
    two_relay(0, 1, 3)
    one_relay(1)
    weights.next()
    two_relay(0, 2)
    one_wait(1, 1)
    two_push(1, 1, 3)
    two_relay(1, 0)
    one_wait(1, 2)
    two_push(1, 2)
    shared(0)
    tile_pass(grads[0], running_0, True)
    weights.next()
    two_relay(1, 1, 3)
    back_swap(0)
    two_relay(1, 2)
    back_push(0)
    weights.next()
    for t in range(tiles):
        out_buf[tile_rows(t), :] = value_buf[t].T.astype(BF16)
    stores[0].start()
    shared(1)
    tile_pass(grads[1], running_1, True)
    weights.next()
    back_swap(1)
    back_relay(0)
    back_push(1)
    weights.next()
    weights.next()
    back_relay(1)
    back_end(0)
    weights.next()
    stores[1].start()
    back_end(1)
    stores[2].start()
    links.drain()
    for store in stores:
        store.wait()


def copy_kernel(*refs):
    count = (len(refs) - 2) // 3
    sources, targets, held = (refs[i * count : (i + 1) * count] for i in range(3))
    came, left = refs[-2:]
    into = [pltpu.make_async_copy(sources[i], held[i], came.at[i]) for i in range(count)]
    out = [pltpu.make_async_copy(held[i], targets[i], left.at[i]) for i in range(count)]
    for copy in into:
        copy.start()
    for first, second in zip(into, out):
        first.wait()
        second.start()
    for copy in out:
        copy.wait()


def shards(features, weight, adj_tiles, tile_rows, tile_cols, tile_count, cotangent):
    nodes, width = features.shape
    slots, tile = adj_tiles.shape[:2]
    n_row, n_col = lax.axis_size("row"), lax.axis_size("col")
    tiles, half, member = nodes // tile, width // 2, width // RING
    one = (half, tile)
    backs = [(back, tile) for back in BACK_WIDTHS]

    def vmem(*shape, dtype=BF16):
        return pltpu.VMEM(shape, dtype)

    anywhere = pl.BlockSpec(memory_space=pl.ANY)
    results = pl.pallas_call(
        layer_kernel,
        out_shape=(
            jax.ShapeDtypeStruct((nodes, width), BF16),
            jax.ShapeDtypeStruct((RING, member, width), F32),
            jax.ShapeDtypeStruct((nodes, width), BF16),
        ),
        in_specs=[anywhere] * 7,
        out_specs=(anywhere,) * 3,
        scratch_shapes=[
            vmem(nodes, width),
            vmem(width, width),
            vmem(slots, tile, tile),
            vmem(2, 1, slots, dtype=jnp.int32),
            vmem(nodes, width),
            vmem(8, 128, dtype=jnp.int32),
            pltpu.SMEM((8, 128), jnp.int32),
            vmem(n_row, tiles, *one),
            vmem(n_row, tiles, *one),
            vmem(slots + 1, *one),
            *(vmem(slots + 1, *back) for back in backs),
            vmem(2, n_col, tiles, *one),
            vmem(2, RING, 2, 2, tiles // 4, *one),
            vmem(2, RING, 2, 2, tiles // 2, *one),
            vmem(2, 2, RING, tiles // 2, *one),
            vmem(2, 2, 2, tiles // 4, *one),
            vmem(2, 2, 2, tiles // 2, *one),
            vmem(tiles, width, tile, dtype=F32),
            vmem(tiles, width, tile),
            vmem(tiles, width, tile),
            vmem(tiles, width, tile, dtype=F32),
            *(vmem(n_col, tiles, *back) for back in backs),
            vmem(RING, member, width, dtype=F32),
            vmem(2, member // 2, width, dtype=F32),
            vmem(2, member, width, dtype=F32),
            vmem(11, member, width, dtype=F32),
            vmem(5, member, width, dtype=F32),
            *(vmem(n_row, tiles, *back) for back in backs),
            *(vmem(RING, tiles, *back) for back in backs),
            *(vmem(RING, tiles, *back) for back in backs),
            *(vmem(2, tiles // 2, *back) for back in backs),
            *(vmem(2, tiles, *back) for back in backs),
            vmem(nodes, width),
            vmem(RING, member, width, dtype=F32),
            vmem(nodes, width),
            pltpu.SMEM((1,), jnp.int32),
            pltpu.SemaphoreType.DMA((11,)),
            pltpu.SemaphoreType.DMA((9,)),
            pltpu.SemaphoreType.DMA((65,)),
        ],
        compiler_params=pltpu.CompilerParams(
            vmem_limit_bytes=VMEM_BYTES, collective_id=0, has_side_effects=True
        ),
        name="layer",
    )(
        tile_count, features, weight, adj_tiles,
        tile_rows.reshape(1, slots), tile_cols.reshape(1, slots), cotangent,
    )
    out_features, weight_grad, feature_grad = pl.pallas_call(
        copy_kernel,
        out_shape=tuple(jax.ShapeDtypeStruct(r.shape, r.dtype) for r in results),
        in_specs=[anywhere] * 3,
        out_specs=(anywhere,) * 3,
        scratch_shapes=[pltpu.VMEM(r.shape, r.dtype) for r in results]
        + [pltpu.SemaphoreType.DMA((3,))] * 2,
        compiler_params=pltpu.CompilerParams(vmem_limit_bytes=VMEM_BYTES),
        name="results",
    )(*results)
    return (out_features, weight_grad.reshape(width, width), feature_grad)


def solution(mesh):
    in_specs = (
        P(("row", "col"), None),
        P(),
        P(("row", "col"), None, None),
        P(("row", "col")),
        P(("row", "col")),
        P(("row", "col")),
        P(("row", "col"), None),
    )
    out_specs = (P(("row", "col"), None), P(), P(("row", "col"), None))
    return jax.shard_map(shards, mesh=mesh, in_specs=in_specs, out_specs=out_specs, check_vma=False)
```
